32 devices in a mesh: dp: 32 (over z, y, x, core).
Axes of the slice: x: 2, y: 2, z: 4, core: 2. Of those that a mesh axis runs over, the one named last changes fastest.
Arguments:
- tokens: bfloat16 [32768, 768], P('dp'), may hold values from -6 to 6
- seg_lengths: int32 [32, 6], P('dp'), may hold values from 24 to 180, as said below
- owner: int32 [32, 5], replicated, may hold values from 0 to 31, as said below
- place: int32 [32, 5], replicated, may hold values from 0 to 4, as said below
- w_qkv: bfloat16 [768, 2304], replicated, may hold values from -0.21875 to 0.21875
- b_qv: float32 [1536], replicated, may hold values from -2 to 2
- w_out: bfloat16 [768, 768], replicated, may hold values from -0.875 to 0.875
- b_out: float32 [768], replicated, may hold values from -2 to 2
- ln1_gain: float32 [768], replicated, may hold values from 0.1 to 1.9
- ln1_bias: float32 [768], replicated, may hold values from -2 to 2
- w_up: bfloat16 [768, 3072], replicated, may hold values from -0.21875 to 0.21875
- b_up: float32 [3072], replicated, may hold values from -2 to 2
- w_down: bfloat16 [3072, 768], replicated, may hold values from -0.109375 to 0.109375
- b_down: float32 [768], replicated, may hold values from -2 to 2
- ln2_gain: float32 [768], replicated, may hold values from 0.1 to 1.9
- ln2_bias: float32 [768], replicated, may hold values from -2 to 2
- w_proj: bfloat16 [768, 128], replicated, may hold values from -0.21875 to 0.21875
Outputs:
- losses: float32 [32], P('dp')
- d_tokens: float32 [32768, 768], P('dp')
- g_w_qkv: float32 [768, 2304], replicated
- g_b_qv: float32 [1536], replicated
- g_w_out: float32 [768, 768], replicated
- g_b_out: float32 [768], replicated
- g_ln1_gain: float32 [768], replicated
- g_ln1_bias: float32 [768], replicated
- g_w_up: float32 [768, 3072], replicated
- g_b_up: float32 [3072], replicated
- g_w_down: float32 [3072, 768], replicated
- g_b_down: float32 [768], replicated
- g_ln2_gain: float32 [768], replicated
- g_ln2_bias: float32 [768], replicated
- g_w_proj: float32 [768, 128], replicated
The draws below stay inside these ranges and needn't reach their ends.
Inputs may be any that keep to these rules, and one draw needn't show every extreme that they name: `seg_lengths`: entry 0 of a row is its query's length, at least 24, and 32 in some row; entries 1 to 5 are passage lengths of at least 90, and every row has a passage of exactly 180. `owner`: every row's query scores exactly 5 passages, none of them in its own row. `place`: the 5 passages scored by one query have the roles 0 to 4, each once.
All inputs are finite; a program needn't handle non-finite values.
Results may differ from the reference program's by a relative error of at most 0.014.
Values may be sent and summed in bfloat16 or wider, within the bound.
No kernel may reach another device: no remote copies, remote signals or barrier semaphores. Data moves between devices by JAX's collectives and lax.ppermute only.
A program may use at most 384 MiB of HBM per device.

```python
import math
import jax
import jax.numpy as jnp
from jax import lax

D = 768
HEADS = 12
FF = 3072
OUT = 128
ROW_LEN = 1024
QLEN = 32
PLEN = 180
NPAS = 5
TOKENS = 32768
N_DP = 32


def shared_tables(key):
    half_offset = N_DP // 2
    candidates = jnp.array([k for k in range(2, N_DP) if k != half_offset], dtype=jnp.int32)
    others = jax.random.permutation(jax.random.fold_in(key, 11), candidates)[:NPAS - 2]
    fixed_shifts = jnp.array([1, half_offset], dtype=jnp.int32)
    shifts = jnp.concatenate([fixed_shifts, others])
    shifts = jax.random.permutation(jax.random.fold_in(key, 13), shifts)
    row_ids = jnp.arange(N_DP, dtype=jnp.int32)[:, None]
    owners = (row_ids + shifts[None, :]) % N_DP
    key_list = jax.random.split(jax.random.fold_in(key, 12), N_DP)
    orders = jax.vmap(lambda single: jax.random.permutation(single, NPAS))(key_list)
    columns = jnp.broadcast_to(jnp.arange(NPAS, dtype=jnp.int32)[None, :], owners.shape)
    places = orders[owners, columns]
    return (owners.astype(jnp.int32), places.astype(jnp.int32))


def draw_owner(key, part):
    tables = shared_tables(key)
    return tables[0]


def draw_place(key, part):
    tables = shared_tables(key)
    return tables[1]


def draw_seg_lengths(key, part):
    key = jax.random.fold_in(key, 5)
    keys = jax.random.split(key, 5)
    query = jax.random.randint(keys[0], (N_DP, 1), 3 * QLEN // 4, QLEN + 1)
    full_query = jax.random.randint(keys[1], (), 0, N_DP)
    query = jnp.where(jnp.arange(N_DP)[:, None] == full_query, QLEN, query)
    first = jax.random.randint(keys[2], (N_DP, NPAS), PLEN // 2, PLEN + 1)
    second = jax.random.randint(keys[3], (N_DP, NPAS), PLEN // 2, PLEN + 1)
    passage = jnp.maximum(first, second)
    full_passage = jax.random.randint(keys[4], (N_DP, 1), 0, NPAS)
    passage = jnp.where(jnp.arange(NPAS)[None, :] == full_passage, PLEN, passage)
    return jnp.concatenate([query, passage], axis=1).astype(jnp.int32)


def level_of(own_key, dims, cuts, least, top_value):
    level = 1.0
    for dim, blocks in cuts:
        steps = jax.random.uniform(jax.random.fold_in(jax.random.fold_in(own_key, 6), dim), (blocks,), jnp.float32, least / len(cuts), top_value / len(cuts))
        level = level * jnp.repeat(jnp.exp(steps), dims[dim] // blocks).reshape((-1,) + (1,) * (len(dims) - 1 - dim))
    return level


def bell_draw(key, extent, scale, bound, shards=(), kind=jnp.bfloat16):
    level = level_of(key, extent, shards, -0.22, 0.18) if shards else 1.0
    entries = jax.random.normal(key, extent, jnp.float32) * scale * level
    return jnp.minimum(jnp.maximum(entries, -bound), bound).astype(kind)


def setup_inputs(seed: int = 0) -> dict:
    key_of = jax.random.split(jax.random.key(seed), 18)
    return {
        "tokens": bell_draw(key_of[0], (TOKENS, D), 1.0, 6.0, ((0, 32),)),
        "seg_lengths": draw_seg_lengths(jax.random.fold_in(key_of[17], 71), 0),
        "owner": draw_owner(jax.random.fold_in(key_of[17], 71), 0),
        "place": draw_place(jax.random.fold_in(key_of[17], 71), 0),
        "w_qkv": bell_draw(key_of[4], (D, 3 * D), D ** -0.5, 0.21875),
        "b_qv": bell_draw(key_of[5], (2 * D,), 0.3, 2.0, (), jnp.float32),
        "w_out": bell_draw(key_of[6], (D, D), (D // 16) ** -0.5, 0.875),
        "b_out": bell_draw(key_of[7], (D,), 0.3, 2.0, (), jnp.float32),
        "ln1_gain": jnp.clip(1.0 + 0.18 * jax.random.normal(key_of[8], (D,), jnp.float32), 0.1, 1.9),
        "ln1_bias": bell_draw(key_of[9], (D,), 0.3, 2.0, (), jnp.float32),
        "w_up": bell_draw(key_of[10], (D, FF), D ** -0.5, 0.21875),
        "b_up": bell_draw(key_of[11], (FF,), 0.3, 2.0, (), jnp.float32),
        "w_down": bell_draw(key_of[12], (FF, D), FF ** -0.5, 0.109375),
        "b_down": bell_draw(key_of[13], (D,), 0.3, 2.0, (), jnp.float32),
        "ln2_gain": jnp.clip(1.0 + 0.18 * jax.random.normal(key_of[14], (D,), jnp.float32), 0.1, 1.9),
        "ln2_bias": bell_draw(key_of[15], (D,), 0.3, 2.0, (), jnp.float32),
        "w_proj": bell_draw(key_of[16], (D, OUT), D ** -0.5, 0.21875),
    }


precise = lax.Precision.HIGHEST
logit_divisor = 0.1
huge_penalty_constant = -1e+30
ln_epsilon = 1e-12
norm_epsilon = 1e-06

@jax.custom_vjp
def low(v):
    return lax.optimization_barrier(v.astype(jnp.bfloat16)).astype(jnp.float32)

@jax.custom_vjp
def low_back(v):
    return v

def low_keep(v):
    return (low(v), None)

def low_pass(kept, grad):
    return (grad,)

def back_keep(v):
    return (v, None)

def back_low(kept, grad):
    return (low(grad),)
low.defvjp(low_keep, low_pass)
low_back.defvjp(back_keep, back_low)

def both_round(value):
    return low(low_back(value))

def layer_norm(resid, gain, shift):
    center = resid - lax.optimization_barrier(jnp.mean(resid, axis=-1, keepdims=True))
    spread = lax.optimization_barrier(jnp.mean(center * center, axis=-1, keepdims=True))
    return center * lax.rsqrt(spread + ln_epsilon) * gain + shift

def encode_row(params, inputs, lengths):
    w_qkv, b_qv, w_out, b_out, gain_one, bias_one, w_up, b_up, w_down, b_down, gain_two, bias_two, w_proj = params
    count = inputs.shape[0]
    width = inputs.shape[1]
    head_size = width // HEADS
    ends = jnp.cumsum(lengths)
    position = jnp.arange(count, dtype=jnp.int32)
    segment = lax.optimization_barrier(jnp.sum((position[:, None] >= ends[None, :]).astype(jnp.int32), axis=1))
    bias_all = jnp.concatenate([b_qv[:width], jnp.zeros((width,), jnp.float32), b_qv[width:]])
    packed = both_round(jnp.dot(inputs, w_qkv, precision=precise) + bias_all)
    queries = packed[:, :width].reshape(count, HEADS, head_size)
    keys_all = packed[:, width:2 * width].reshape(count, HEADS, head_size)
    values = packed[:, 2 * width:].reshape(count, HEADS, head_size)
    scores = jnp.einsum('qhd,khd->hqk', queries, keys_all, precision=precise) * head_size ** (-0.5)
    scores = low_back(scores)
    same = segment[:, None] == segment[None, :]
    scores = jnp.where(same[None], scores, huge_penalty_constant)
    probs = low(jax.nn.softmax(scores, axis=-1))
    attended = jnp.einsum('hqk,khd->qhd', probs, values, precision=precise).reshape(count, width)
    attended = both_round(attended)
    projected = low_back(jnp.dot(attended, w_out, precision=precise) + b_out)
    hidden = layer_norm(inputs + projected, gain_one, bias_one)
    inner = low_back(jnp.dot(low(hidden), w_up, precision=precise) + b_up)
    activ = low(jax.nn.gelu(inner, approximate=False))
    branch = low_back(jnp.dot(activ, w_down, precision=precise) + b_down)
    normed = layer_norm(hidden + branch, gain_two, bias_two)
    embedded = low_back(jnp.dot(low(normed), w_proj, precision=precise))
    unit = embedded * lax.rsqrt(lax.optimization_barrier(jnp.sum(embedded * embedded, axis=-1, keepdims=True)) + norm_epsilon)
    return both_round(unit)

def reference(tokens, seg_lengths, owner, place, w_qkv, b_qv, w_out, b_out, ln1_gain, ln1_bias, w_up, b_up, w_down, b_down, ln2_gain, ln2_bias, w_proj):
    params = (w_qkv.astype(jnp.float32), b_qv.astype(jnp.float32), w_out.astype(jnp.float32), b_out.astype(jnp.float32), ln1_gain.astype(jnp.float32), ln1_bias.astype(jnp.float32), w_up.astype(jnp.float32), b_up.astype(jnp.float32), w_down.astype(jnp.float32), b_down.astype(jnp.float32), ln2_gain.astype(jnp.float32), ln2_bias.astype(jnp.float32), w_proj.astype(jnp.float32))
    inputs = tokens.astype(jnp.float32).reshape(N_DP, ROW_LEN, D)
    stack_size = math.gcd(N_DP, 4)

    def total(row_inputs, weights):
        stacked = row_inputs.reshape(N_DP // stack_size, stack_size, ROW_LEN, D)
        lens_stack = seg_lengths.reshape(N_DP // stack_size, stack_size, NPAS + 1)

        def one_step(carry, piece):
            block_in, block_len = piece
            out_rows = jax.vmap(lambda rows_in, rows_len: encode_row(weights, rows_in, rows_len))(block_in, block_len)
            return (carry, out_rows)
        _, vectors = lax.scan(jax.checkpoint(one_step), jnp.zeros((), jnp.float32), (stacked, lens_stack))
        vectors = vectors.reshape(N_DP, ROW_LEN, OUT)
        ends = jnp.cumsum(seg_lengths, axis=1)
        starts = ends - seg_lengths
        query_slots = jnp.arange(QLEN, dtype=jnp.int32)
        query_valid = query_slots[None, :] < seg_lengths[:, 0:1]
        query_vectors = jnp.where(query_valid[..., None], vectors[:, :QLEN], 0.0)
        passage_slots = jnp.arange(PLEN, dtype=jnp.int32)
        index = jnp.minimum(starts[:, 1:, None] + passage_slots[None, None, :], ROW_LEN - 1).astype(jnp.int32)
        document_exists_flag = passage_slots[None, None, :] < seg_lengths[:, 1:, None]
        picked = jax.vmap(lambda table, where_from: table[where_from])(vectors, index)
        passage_vectors = jnp.where(document_exists_flag[..., None], picked, 0.0)
        query_for = query_vectors[owner]
        length_for = seg_lengths[:, 0][owner]
        matching_logits = jnp.einsum('npid,npjd->npij', query_for, passage_vectors, precision=precise)
        divided_logits = jnp.where(document_exists_flag[:, :, None, :], matching_logits / logit_divisor, huge_penalty_constant)
        normalized_likelihoods = logit_divisor * jax.nn.logsumexp(divided_logits, axis=-1)
        query_mask = query_slots[None, None, :] < length_for[..., None]
        score = lax.optimization_barrier(jnp.sum(jnp.where(query_mask, normalized_likelihoods, 0.0), axis=-1))
        table = jnp.zeros((N_DP, NPAS), score.dtype).at[owner, place].set(score)
        return jax.nn.logsumexp(table, axis=-1) - table[:, 0]
    losses, pullback = jax.vjp(total, inputs, params)
    d_inputs, grads = pullback(jnp.ones_like(losses))
    return (losses, d_inputs.reshape(N_DP * ROW_LEN, D), grads[0], grads[1], grads[2], grads[3], grads[4], grads[5], grads[6], grads[7], grads[8], grads[9], grads[10], grads[11], grads[12])
```

```python
import functools

import jax
import jax.numpy as jnp
from jax import lax
from jax.experimental import pallas as pl
from jax.experimental.pallas import tpu as pltpu
from jax.sharding import PartitionSpec as P

HEADS = 12
QLEN = 32
PLEN = 180
QB = 128
WIDTHS = (256, 384, 512, 768, 1024)
PIECES = 16
PORTIONS = 3
NEG = -1e30
LN_EPS = 1e-12
NORM_EPS = 1e-6
f32, bf16, i32 = jnp.float32, jnp.bfloat16, jnp.int32


def nn(a, b):
    return lax.dot_general(a, b, (((1,), (0,)), ((), ())), preferred_element_type=f32)


def nt(a, b):
    return lax.dot_general(a, b, (((1,), (1,)), ((), ())), preferred_element_type=f32)


def tn(a, b):
    return lax.dot_general(a, b, (((0,), (0,)), ((), ())), preferred_element_type=f32)


def params(mib=48):
    return pltpu.CompilerParams(vmem_limit_bytes=mib << 20)


def cost(flops, nbytes):
    return pl.CostEstimate(flops=int(flops), bytes_accessed=int(nbytes), transcendentals=0)


SMEM = pl.BlockSpec(memory_space=pltpu.SMEM)
VMEM = pl.BlockSpec(memory_space=pltpu.VMEM)


def whole(shape):
    return pl.BlockSpec(shape, lambda *g: (0,) * len(shape))


def struct(shape, dtype):
    return jax.ShapeDtypeStruct(shape, dtype)


def segment_ends(lens):
    ends = [lens[0, 0]]
    for s in range(1, lens.shape[1]):
        ends.append(ends[-1] + lens[0, s])
    return ends


def segment_of(ends, position):
    seg = jnp.zeros(position.shape, i32)
    for e in ends:
        seg = seg + (position >= e).astype(i32)
    return seg


def key_window(ends, rows, first):
    lo = jnp.zeros((), i32)
    hi = jnp.asarray(rows, i32)
    for e in ends:
        lo = jnp.where(e <= first, e, lo)
    for e in reversed(ends):
        hi = jnp.where(e >= first + QB, e, hi)
    lo = lax.div(lo, QB) * QB
    need = hi - lo
    cls = jnp.zeros((), i32)
    wide = jnp.asarray(WIDTHS[0], i32)
    for c, w in enumerate(WIDTHS[:-1]):
        if WIDTHS[c + 1] <= rows:
            cls = jnp.where(need > w, c + 1, cls)
            wide = jnp.where(need > w, WIDTHS[c + 1], wide)
    return pl.multiple_of(jnp.minimum(lo, rows - wide), QB), cls


def fill_segments(ends, segq, segk):
    segk[...] = segment_of(ends, lax.broadcasted_iota(i32, segk.shape, 0))
    at = lax.broadcasted_iota(i32, segq.shape, 0) * QB + lax.broadcasted_iota(i32, segq.shape, 1)
    segq[...] = segment_of(ends, at)


def two_heads(x, scale=None):
    lane = lax.broadcasted_iota(i32, x.shape, 1)
    zero = jnp.zeros_like(x)
    if scale is not None:
        x = x * scale
    return jnp.concatenate([jnp.where(lane < 64, x, zero), jnp.where(lane < 64, zero, x)], axis=0)


def pick_heads(t):
    return jnp.concatenate([t[:64, :QB], t[64:, QB:]], axis=0)


def attn_fwd_kernel(lens, tok, wqkv, bqv, packed, out, lse, vt, segq, segk):
    rows, width = tok.shape
    ends = segment_ends(lens)
    fill_segments(ends, segq, segk)
    pairs = width // 128
    for j in range(3 * width // 256):
        at = slice(j * 256, (j + 1) * 256)
        x = nn(tok[...], wqkv[:, at])
        which = j * 256 // width
        if which != 1:
            b0 = j * 256 - (width if which else 0)
            x = x + bqv[b0 : b0 + 256].reshape(1, 256)
        packed[:, at] = x.astype(bf16)
    q = packed.at[:, 0:width]
    k = packed.at[:, width : 2 * width]
    v = packed.at[:, 2 * width : 3 * width]
    for g in range(pairs):
        vt[g] = v[:, g * 128 : (g + 1) * 128].T

    def step(i, carry):
        base = pl.multiple_of(i * QB, QB)
        k0, cls = key_window(ends, rows, base)
        sq = segq[pl.ds(i, 1), :]

        def body(w):
            same = segk[pl.ds(k0, w), :] == sq
            sts = []
            for g in range(pairs):
                sl = slice(g * 128, (g + 1) * 128)
                q2 = two_heads(q[pl.ds(base, QB), sl], jnp.asarray(0.125, bf16))
                sts.append(nt(k[pl.ds(k0, w), sl], q2))
            for g in range(pairs):
                sl = slice(g * 128, (g + 1) * 128)
                st = sts[g]
                ps, ms, ls = [], [], []
                for h in range(2):
                    s = jnp.where(same, st[:, h * QB : (h + 1) * QB], NEG)
                    m = jnp.max(s, axis=0, keepdims=True)
                    p = jnp.exp(s - m)
                    ls.append(jnp.sum(p, axis=0, keepdims=True))
                    ms.append(m)
                    ps.append(p.astype(bf16))
                total = jnp.concatenate(ls, 1)
                top = jnp.concatenate(ms, 1)
                ot = nn(vt[g, :, pl.ds(k0, w)], jnp.concatenate(ps, 1)) * (1.0 / total)
                out[pl.ds(base, QB), sl] = pick_heads(ot).T.astype(bf16)
                lse[g, pl.ds(i, 1), :] = top + jnp.log(total)

        for c, w in enumerate(WIDTHS):
            if w <= rows:
                pl.when(cls == c)(functools.partial(body, w))
        return carry

    lax.fori_loop(0, rows // QB, step, 0)


def attn_bwd_kernel(
    part, lens, packed, do, o, lse, dq, dk, dv, sums, kt, dka, dva, segq, segk
):
    rows = packed.shape[0]
    width = packed.shape[1] // 3
    span = dq.shape[1]
    ends = segment_ends(lens)
    fill_segments(ends, segq, segk)
    pairs = span // 128
    q, k, v = [packed.at[:, i * width + part * span : i * width + (part + 1) * span] for i in range(3)]
    do = do.at[:, part * span : (part + 1) * span]
    o = o.at[:, part * span : (part + 1) * span]
    for g in range(pairs):
        kt[g] = k[:, g * 128 : (g + 1) * 128].T
    dka[...] = jnp.zeros_like(dka)
    dva[...] = jnp.zeros_like(dva)
    head = (
        lax.broadcasted_iota(i32, (8, 128), 0) == lax.broadcasted_iota(i32, (8, 128), 1) // 64
    ).astype(f32)

    def step(i, carry):
        base = pl.multiple_of(i * QB, QB)
        k0, cls = key_window(ends, rows, base)
        sq = segq[pl.ds(i, 1), :]

        def body(w):
            at = pl.ds(k0, w)
            same = segk[at, :] == sq
            for g in range(pairs):
                gs = slice(g * 128, (g + 1) * 128)
                q2 = two_heads(q[pl.ds(base, QB), gs], jnp.asarray(0.125, bf16))
                do_ = do[pl.ds(base, QB), gs]
                do2 = two_heads(do_)
                d8 = lax.dot_general(
                    head,
                    do_.astype(f32) * o[pl.ds(base, QB), gs].astype(f32),
                    (((1,), (1,)), ((), ())),
                    precision=lax.Precision.HIGHEST,
                    preferred_element_type=f32,
                )
                lrow = lse[part * pairs + g, pl.ds(i, 1), :]
                st = nt(k[at, gs], q2)
                dpt = nt(v[at, gs], do2)
                ps, ds = [], []
                for h in range(2):
                    sl = slice(h * QB, (h + 1) * QB)
                    p = jnp.exp(jnp.where(same, st[:, sl] - lrow[:, sl], NEG))
                    ps.append(p.astype(bf16))
                    ds.append((p * (dpt[:, sl] - d8[h : h + 1, :])).astype(bf16))
                p = jnp.concatenate(ps, 1)
                d = jnp.concatenate(ds, 1)
                dka[at, gs] += nn(d, q2)
                dva[at, gs] += nn(p, do2)
                dqt = nn(kt[g, :, pl.ds(k0, w)], d)
                dq[pl.ds(base, QB), gs] = (pick_heads(dqt).T * 0.125).astype(bf16)

        for c, w in enumerate(WIDTHS):
            if w <= rows:
                pl.when(cls == c)(functools.partial(body, w))
        return carry

    lax.fori_loop(0, rows // QB, step, 0)
    dk[...] = dka[...].astype(bf16)
    dvl = dva[...].astype(bf16)
    dv[...] = dvl
    sums[0:1, :] = jnp.sum(dq[...].astype(f32), axis=0, keepdims=True)
    sums[1:2, :] = jnp.sum(dvl.astype(f32), axis=0, keepdims=True)


def segment_scratch(rows):
    return [pltpu.VMEM((rows // QB, QB), i32), pltpu.VMEM((rows, 128), i32)]


def attention(lens, tok, wqkv, bqv):
    rows, width = tok.shape
    pairs = width // 128
    return pl.pallas_call(
        attn_fwd_kernel,
        in_specs=[SMEM, VMEM, VMEM, VMEM],
        out_specs=[VMEM] * 3,
        out_shape=[
            struct((rows, 3 * width), bf16),
            struct((rows, width), bf16),
            struct((pairs, rows // QB, 2 * QB), f32),
        ],
        scratch_shapes=[pltpu.VMEM((pairs, 128, rows), bf16)] + segment_scratch(rows),
        compiler_params=params(32),
        cost_estimate=cost(16e9, 8 * rows * width),
        name="attention_forward",
    )(lens, tok, wqkv, bqv)


def attention_back(part, lens, packed, do, o, lse):
    rows, width = packed.shape[0], packed.shape[1] // 3
    span = width // PORTIONS
    pairs = span // 128
    shp = struct((rows, span), bf16)
    return pl.pallas_call(
        functools.partial(attn_bwd_kernel, part),
        in_specs=[SMEM] + [VMEM] * 4,
        out_specs=[VMEM] * 4,
        out_shape=[shp, shp, shp, struct((8, span), f32)],
        scratch_shapes=[
            pltpu.VMEM((pairs, 128, rows), bf16),
            pltpu.VMEM((rows, span), f32),
            pltpu.VMEM((rows, span), f32),
        ]
        + segment_scratch(rows),
        compiler_params=params(24),
        cost_estimate=cost(10e9, 16 * rows * span),
        name="attention_backward",
    )(lens, packed, do, o, lse)


def normalize(resid):
    center = resid - jnp.mean(resid, axis=-1, keepdims=True)
    inv = lax.rsqrt(jnp.mean(center * center, axis=-1, keepdims=True) + LN_EPS)
    return center * inv, inv


def norm_back(grad, gain, normal, inv):
    dn = grad * gain
    return inv * (
        dn
        - jnp.mean(dn, axis=-1, keepdims=True)
        - normal * jnp.mean(dn * normal, axis=-1, keepdims=True)
    )


def row(v):
    return v[...].reshape(1, -1)


def mid_fwd_kernel(
    lens, att, tok, wo, bo, g1, b1, wu, bu, wd, bd, g2, b2, wp,
    ht, act, slp, n1, i1, n2, i2, nl, emb, ul, msg,
    hid, low, acc, bus,
):
    rows = att.shape[0]
    ff = wu.shape[1]
    chunk = 512
    tile = 256
    tiles = [slice(r, r + tile) for r in range(0, rows, tile)]
    bus[...] = row(bu)
    for r in tiles:
        resid = tok[r, :].astype(f32) + (nn(att[r, :], wo[...]) + row(bo))
        normal, inv = normalize(resid)
        hidden = normal * row(g1) + row(b1)
        hid[r, :] = hidden
        hl = hidden.astype(bf16)
        low[r, :] = hl
        ht[:, r] = hl.T
        n1[r, :] = normal.astype(bf16)
        i1[r, :] = inv
        acc[r, :] = hidden + row(bd)

    def step(c, carry):
        at = pl.ds(pl.multiple_of(c * chunk, chunk), chunk)
        for r in tiles:
            inner = nn(low[r, :], wu[:, at]) + bus[:, at]
            cdf = 0.5 + 0.5 * lax.erf(inner * 0.7071067811865476)
            a = (inner * cdf).astype(bf16)
            act[r, at] = a
            slp[r, at] = (
                cdf + inner * (jnp.exp(inner * inner * -0.5) * 0.3989422804014327)
            ).astype(bf16)
            acc[r, :] += nn(a, wd[at, :])
        return carry

    lax.fori_loop(0, ff // chunk, step, 0)
    for r in tiles:
        normal, inv = normalize(acc[r, :])
        normed = (normal * row(g2) + row(b2)).astype(bf16)
        n2[r, :] = normal.astype(bf16)
        i2[r, :] = inv
        nl[r, :] = normed
        e = nn(normed, wp[...])
        emb[r, :] = e
        ul[r, :] = (e * lax.rsqrt(jnp.sum(e * e, axis=-1, keepdims=True) + NORM_EPS)).astype(bf16)
    count = lens[0, 0]
    slot = lax.broadcasted_iota(i32, (QLEN, ul.shape[1]), 0)
    msg[0, 0:QLEN, :] = jnp.where(slot < count, ul[0:QLEN, :].astype(f32), 0.0).astype(bf16)
    msg[0, QLEN : QLEN + 16, :] = jnp.full((16, ul.shape[1]), count, i32).astype(f32).astype(bf16)


def mid_fwd(lens, att, tok, wo, bo, g1, b1, wu, bu, wd, bd, g2, b2, wp):
    rows, width = att.shape
    ff, out = wu.shape[1], wp.shape[1]
    ins = [lens, att, tok, wo, bo, g1, b1, wu, bu, wd, bd, g2, b2, wp]
    outs = [
        struct((width, rows), bf16),
        struct((rows, ff), bf16),
        struct((rows, ff), bf16),
        struct((rows, width), bf16),
        struct((rows, 1), f32),
        struct((rows, width), bf16),
        struct((rows, 1), f32),
        struct((rows, width), bf16),
        struct((rows, out), f32),
        struct((rows, out), bf16),
        struct((1, QLEN + 16, out), bf16),
    ]
    return pl.pallas_call(
        mid_fwd_kernel,
        in_specs=[SMEM] + [VMEM] * (len(ins) - 1),
        out_specs=[VMEM] * len(outs),
        out_shape=outs,
        scratch_shapes=[
            pltpu.VMEM((rows, width), f32),
            pltpu.VMEM((rows, width), bf16),
            pltpu.VMEM((rows, width), f32),
            pltpu.VMEM((1, ff), f32),
        ],
        compiler_params=params(56),
        cost_estimate=cost(20e9, 40e6),
        name="middle_forward",
    )(*ins)


def relative(device, n):
    bits = n.bit_length() - 1
    at = jnp.zeros((), i32)
    for b in range(bits):
        at = at | (((device >> b) & 1) << (bits - 1 - b))
    return at


def loss_kernel(me, lens, owner, gathered, ul, msg, dpb):
    n, nump = owner.shape
    rows = ul.shape[0]
    total = nump * QLEN
    seg = segment_of(segment_ends(lens), lax.broadcasted_iota(i32, (1, rows), 1))
    rel = [relative(owner[me[0], p] ^ me[0], n) for p in range(nump)]
    qs = [gathered[rel[p], 0:QLEN, :] for p in range(nump)]
    q = jnp.concatenate(qs, axis=0)
    slot = lax.broadcasted_iota(i32, (QLEN, 1), 0).astype(f32)
    valid = jnp.concatenate(
        [
            (slot < gathered[rel[p], QLEN : QLEN + 16, :][0:1, 0:1].astype(f32)).astype(f32)
            for p in range(nump)
        ],
        axis=0,
    )
    group = lax.broadcasted_iota(i32, (total, rows), 0) // QLEN + 1
    x = jnp.where(group == seg, nt(q, ul[...]) * 10.0, NEG)
    top = jnp.max(x, axis=1, keepdims=True)
    e = jnp.exp(x - top)
    sm = jnp.sum(e, axis=1, keepdims=True)
    soft = valid * (0.1 * (top + jnp.log(sm)))
    lane = lax.broadcasted_iota(i32, (1, 128), 1)
    score = jnp.zeros((1, 128), f32)
    for p in range(nump):
        score = score + jnp.where(
            lane == p, jnp.sum(soft[p * QLEN : (p + 1) * QLEN], axis=0, keepdims=True), 0.0
        )
    w = e * (valid / sm)
    wh = w.astype(bf16)
    wl = (w - wh.astype(f32)).astype(bf16)
    msg[0, 0:total, :] = (nn(wh, ul[...]) + nn(wl, ul[...])).astype(bf16)
    hi = score.astype(bf16)
    rest = score - hi.astype(f32)
    mid = rest.astype(bf16)
    lo = (rest - mid.astype(f32)).astype(bf16)
    row = lax.broadcasted_iota(i32, (16, 128), 0)
    tail = jnp.where(row == 0, hi.astype(f32), 0.0)
    tail = tail + jnp.where(row == 1, mid.astype(f32), 0.0)
    tail = tail + jnp.where(row == 2, lo.astype(f32), 0.0)
    msg[0, total : total + 16, :] = tail.astype(bf16)
    dpb[...] = tn(wh, q) + tn(wl, q)


def loss_forward(me, lens, owner, gathered, ul):
    rows, out = ul.shape
    total = owner.shape[1] * QLEN
    smem = pl.BlockSpec(memory_space=pltpu.SMEM)
    vmem = pl.BlockSpec(memory_space=pltpu.VMEM)
    return pl.pallas_call(
        loss_kernel,
        in_specs=[smem] * 3 + [vmem] * 2,
        out_specs=[vmem] * 2,
        out_shape=[struct((1, total + 16, out), bf16), struct((rows, out), f32)],
        compiler_params=params(16),
        cost_estimate=cost(1e9, 2e6),
        name="loss_forward",
    )(me, lens, owner, gathered, ul)


def loss_back_kernel(
    me, lens, owner, place, messages, dpb, emb, nl, n2, i2, g2, wp,
    loss, dr2, dbr, gwp, sums, du, gwpt, inverse,
):
    n, nump = owner.shape
    groups = nump + 1
    rows, width = nl.shape
    total = nump * QLEN
    mine = me[0]

    def note(i, carry):
        for p in range(nump):
            inverse[owner[i, p] * nump + place[i, p]] = i * nump + p
        return carry

    lax.fori_loop(0, n, note, 0)
    group = [mine] + [owner[mine, p] for p in range(nump)]
    plc = [place[mine, p] for p in range(nump)]
    src, col = {}, {}
    for g in range(groups):
        for r in range(nump):
            entry = inverse[group[g] * nump + r]
            src[g, r] = relative(lax.div(entry, nump) ^ mine, n)
            col[g, r] = lax.rem(entry, nump)
    lane = lax.broadcasted_iota(i32, (8, 128), 1)
    sub = lax.broadcasted_iota(i32, (8, 128), 0)
    vals = []
    for r in range(nump):
        a = jnp.zeros((8, 128), f32)
        for g in range(groups):
            t = messages[src[g, r], total : total + 16, :].astype(f32)
            t = t[0:1, :] + t[1:2, :] + t[2:3, :]
            a = jnp.where((sub == g) & (lane == col[g, r]), t, a)
        vals.append(jnp.sum(a, axis=1, keepdims=True))
    top = vals[0]
    for v in vals[1:]:
        top = jnp.maximum(top, v)
    es = [jnp.exp(v - top) for v in vals]
    sm = es[0]
    for e in es[1:]:
        sm = sm + e
    loss[...] = jnp.broadcast_to((top + jnp.log(sm) - vals[0])[0:1], (8, 128))
    dt = [e / sm - (1.0 if r == 0 else 0.0) for r, e in enumerate(es)]
    sub1 = lax.broadcasted_iota(i32, (8, 1), 0)
    place = jnp.zeros((8, 1), i32)
    for p in range(nump):
        place = jnp.where(sub1 == p + 1, plc[p], place)
    dscore = jnp.zeros((8, 1), f32)
    for r in range(nump):
        dscore = jnp.where(place == r, dt[r], dscore)
    dmq = jnp.zeros((QLEN, 128), f32)
    for r in range(nump):
        at = pl.multiple_of(col[0, r] * QLEN, QLEN)
        dmq = dmq + dt[r][0:1] * messages[src[0, r], pl.ds(at, QLEN), :].astype(f32)
    sk = segment_of(segment_ends(lens), lax.broadcasted_iota(i32, (rows, 128), 0))
    scale = jnp.zeros(sk.shape, f32)
    for p in range(nump):
        scale = jnp.where(sk == p + 1, dscore[p + 1 : p + 2], scale)
    du[...] = scale * dpb[...]
    du[0:QLEN, :] = jnp.where(sk[0:QLEN] == 0, dmq, du[0:QLEN, :])

    gwpt[...] = jnp.zeros_like(gwpt)
    sums[...] = jnp.zeros_like(sums)
    tile = 256
    for r0 in range(0, rows, tile):
        r = slice(r0, r0 + tile)
        e = emb[r, :]
        inv = lax.rsqrt(jnp.sum(e * e, axis=-1, keepdims=True) + NORM_EPS)
        unit = e * inv
        d = du[r, :].astype(bf16).astype(f32)
        de = (inv * (d - unit * jnp.sum(unit * d, axis=-1, keepdims=True))).astype(bf16)
        gwpt[...] += tn(de, nl[r, :])
        dn = nt(de, wp[...])
        normal = n2[r, :].astype(f32)
        sums[0:1, :] += jnp.sum(dn * normal, axis=0, keepdims=True)
        sums[1:2, :] += jnp.sum(dn, axis=0, keepdims=True)
        dr = norm_back(dn, row(g2), normal, i2[r, :])
        dr2[r, :] = dr
        db = dr.astype(bf16)
        dbr[r, :] = db
        sums[2:3, :] += jnp.sum(db.astype(f32), axis=0, keepdims=True)
    gwp[...] = gwpt[...].T


def loss_back(me, lens, owner, place, messages, dpb, emb, nl, n2, i2, g2, wp):
    rows, width = nl.shape
    out = wp.shape[1]
    smem = pl.BlockSpec(memory_space=pltpu.SMEM)
    vmem = pl.BlockSpec(memory_space=pltpu.VMEM)
    return pl.pallas_call(
        loss_back_kernel,
        in_specs=[smem] * 4 + [vmem] * 8,
        out_specs=[vmem] * 5,
        out_shape=[
            struct((8, 128), f32),
            struct((rows, width), f32),
            struct((rows, width), bf16),
            struct((width, out), f32),
            struct((8, width), f32),
        ],
        scratch_shapes=[
            pltpu.VMEM((rows, out), f32),
            pltpu.VMEM((out, width), f32),
            pltpu.SMEM((owner.size,), i32),
        ],
        compiler_params=params(32),
        cost_estimate=cost(6e9, 10e6),
        name="loss_backward",
    )(me, lens, owner, place, messages, dpb, emb, nl, n2, i2, g2, wp)


def flip_of(device, dims):
    m = jnp.zeros((), i32)
    for i, d in enumerate(dims[:4]):
        m = m | jnp.where((device & d) != 0, 8 >> i, 0)
    return m


def sides(me, dims, keep, send):
    m = flip_of(me[0], dims)
    half = PIECES // 2
    top, low = lax.div(m, half), lax.rem(m, half)
    return [(keep, top, low), (send, 1 - top, low)]


def down_grad_kernel(dims, me, act, dbr, keep, send):
    pr = keep.shape[1]
    half = PIECES // 2
    for dst, side, low in sides(me, dims, keep, send):
        for t in range(0, half, 2):
            at = pl.multiple_of((side * half + t) * pr, 128)
            g = tn(act[:, pl.ds(at, 2 * pr)], dbr[...])
            dst[t ^ low] = g[:pr]
            dst[(t + 1) ^ low] = g[pr:]


def down_grad(dims, me, act, dbr):
    rows, width = dbr.shape
    buf = struct((PIECES // 2, act.shape[1] // PIECES, width), f32)
    return pl.pallas_call(
        functools.partial(down_grad_kernel, dims),
        in_specs=[SMEM, VMEM, VMEM],
        out_specs=[VMEM] * 2,
        out_shape=[buf, buf],
        compiler_params=params(32),
        cost_estimate=cost(5e9, 17e6),
        name="down_gradient",
    )(me, act, dbr)


def up_grad_kernel(dims, me, dbr, slp, wd, ht, keep, send, din, dsum):
    ff = slp.shape[1]
    pr = keep.shape[1]
    half = PIECES // 2
    chunk = 512

    def step(c, carry):
        at = pl.ds(pl.multiple_of(c * chunk, chunk), chunk)
        d_inner = (nt(dbr[...], wd[at, :]) * slp[:, at].astype(f32)).astype(bf16)
        din[:, at] = d_inner
        dsum[:, at] = jnp.sum(d_inner.astype(f32), axis=0, keepdims=True)
        for dst, side, low in sides(me, dims, keep, send):
            r = pl.ds(pl.multiple_of(side * (half * pr), half * pr), half * pr)
            g = nn(ht[r, :], d_inner)
            for t in range(half):
                dst[t ^ low, :, at] = g[t * pr : (t + 1) * pr]
        return carry

    lax.fori_loop(0, ff // chunk, step, 0)


def up_grad(dims, me, dbr, slp, wd, ht):
    rows, width = dbr.shape
    ff = slp.shape[1]
    buf = struct((PIECES // 2, width // PIECES, ff), f32)
    return pl.pallas_call(
        functools.partial(up_grad_kernel, dims),
        in_specs=[SMEM] + [VMEM] * 4,
        out_specs=[VMEM] * 4,
        out_shape=[buf, buf, struct((rows, ff), bf16), struct((1, ff), f32)],
        compiler_params=params(48),
        cost_estimate=cost(10e9, 30e6),
        name="up_gradient",
    )(me, dbr, slp, wd, ht)


def mid_back_kernel(me, din, wu, dr2, n1, i1, g1, wo, dr1, dpr, dat, sums):
    rows, width = dr2.shape
    sums[...] = jnp.zeros_like(sums)
    tile = 256
    for r0 in range(0, rows, tile):
        r = slice(r0, r0 + tile)
        d = dr2[r, :] + nt(din[r, :], wu[...])
        normal = n1[r, :].astype(f32)
        sums[0:1, :] += jnp.sum(d * normal, axis=0, keepdims=True)
        sums[1:2, :] += jnp.sum(d, axis=0, keepdims=True)
        dr = norm_back(d, row(g1), normal, i1[r, :])
        dr1[r, :] = dr
        low = dr.astype(bf16)
        dpr[r, :] = low
        sums[2:3, :] += jnp.sum(low.astype(f32), axis=0, keepdims=True)
        dat[r, :] = nt(low, wo[...]).astype(bf16)


def mid_back(me, din, wu, dr2, n1, i1, g1, wo):
    rows, width = dr2.shape
    return pl.pallas_call(
        mid_back_kernel,
        in_specs=[SMEM] + [VMEM] * 7,
        out_specs=[VMEM] * 4,
        out_shape=[
            struct((rows, width), f32),
            struct((rows, width), bf16),
            struct((rows, width), bf16),
            struct((8, width), f32),
        ],
        compiler_params=params(40),
        cost_estimate=cost(9e9, 15e6),
        name="middle_backward",
    )(me, din, wu, dr2, n1, i1, g1, wo)


def qkv_grad_kernel(p, dims, me, tok, d0, d1, d2, att, dpr, *rest):
    keep, send = rest[-2:]
    extra = rest[0] if len(rest) == 3 else None
    half = PIECES // 2
    pr = keep.shape[1]
    for dst, side, low in sides(me, dims, keep, send):
        at = pl.ds(pl.multiple_of(side * (half * pr), half * pr), half * pr)
        col = 0
        dpr_own = dpr.at[:, p * 256 : (p + 1) * 256]
        for left, d in ((tok, d0), (tok, d1), (tok, d2), (att, dpr_own)):
            g = tn(left[:, at], d[...])
            for t in range(half):
                dst[t ^ low, :, col : col + 256] = g[t * pr : (t + 1) * pr]
            col += 256
        if extra is not None:
            for t in range(half):
                first = pl.multiple_of((side * half + t) * pr, 16)
                dst[t ^ low, :, col : col + 128] = extra[pl.ds(first, pr), :]


def qkv_grad(p, dims, me, tok, ds, att, dpr, extra):
    rows, width = att.shape
    ins = [me, tok, *ds, att, dpr] + ([] if extra is None else [extra])
    buf = struct((PIECES // 2, width // PIECES, width + 256 + (0 if extra is None else 128)), f32)
    return pl.pallas_call(
        functools.partial(qkv_grad_kernel, p, dims),
        in_specs=[SMEM] + [VMEM] * (len(ins) - 1),
        out_specs=[VMEM] * 2,
        out_shape=[buf, buf],
        compiler_params=params(24),
        cost_estimate=cost(4e9, 8e6),
        name="qkv_gradient",
    )(*ins)


def input_grad_kernel(count, me, *refs):
    ds = refs[:count]
    w, dr1, out = refs[count:]
    tile = 256
    for r0 in range(0, out.shape[0], tile):
        r = slice(r0, r0 + tile)
        acc = dr1[r, :]
        for j, d in enumerate(ds):
            acc = acc + nt(d[r, :], w[:, j * 256 : (j + 1) * 256])
        out[r, :] = acc


def input_grad(me, ds, w, dr1):
    return pl.pallas_call(
        functools.partial(input_grad_kernel, len(ds)),
        in_specs=[SMEM] + [VMEM] * (len(ds) + 2),
        out_specs=VMEM,
        out_shape=struct(dr1.shape, f32),
        compiler_params=params(32),
        cost_estimate=cost(5e9, 15e6),
        name="input_gradient",
    )(me, *ds, w, dr1)


def collect_kernel(s0, s1, s2, dsum, sm1, sm2, out):
    width = out.shape[1]
    for j, s in enumerate((s0, s1, s2)):
        out[0:2, j * 256 : (j + 1) * 256] = s[0:2, :]
    out[2:3, :] = sm1[2:3, :]
    out[3:5, :] = sm1[0:2, :]
    end = 5
    for j in range(dsum.shape[1] // width):
        out[end : end + 1, :] = dsum[:, j * width : (j + 1) * width]
        end += 1
    out[end : end + 1, :] = sm2[2:3, :]
    out[end + 1 : end + 3, :] = sm2[0:2, :]
    out[end + 3 :, :] = jnp.zeros((out.shape[0] - end - 3, width), f32)


def collect(s, dsum, sm1, sm2):
    ins = [*s, dsum, sm1, sm2]
    return pl.pallas_call(
        collect_kernel,
        in_specs=[VMEM] * len(ins),
        out_specs=VMEM,
        out_shape=struct((16, sm1.shape[1]), f32),
        compiler_params=params(16),
        cost_estimate=cost(1e4, 1e5),
        name="collect_vectors",
    )(*ins)


def swap(x, mask, n):
    return lax.ppermute(x, "dp", [(i, i ^ mask) for i in range(n)])


def after(x, *others):
    return lax.optimization_barrier((x,) + others)[0]


def join(x, y):
    which = lax.broadcasted_iota(i32, (2,) + x.shape, 0)
    both = jnp.where(which == 0, x[None], y[None])
    return both.reshape((2 * x.shape[0],) + x.shape[1:])


class Chain:
    def __init__(self, keep, send, dims, n):
        self.keep, self.ready, self.dims, self.n = keep, send, dims, n
        self.at = 0
        self.out = None
        self.recv = None

    def start(self):
        k, dims = self.at, self.dims
        d = dims[k] if k < len(dims) else dims[3 - (k - len(dims))]
        self.recv = swap(self.ready, d, self.n)

    def land(self, *others):
        k, dims = self.at, self.dims
        self.at += 1
        recv = after(self.recv, *others) if others else self.recv
        if k < 4:
            recv = recv.astype(f32)
            half = self.keep.shape[0] // 2
            if k < 3:
                self.ready = (self.keep[half:] + recv[half:]).astype(bf16)
                self.keep = self.keep[:half] + recv[:half]
            else:
                self.ready = (self.keep + recv).astype(bf16)
        elif k < len(dims):
            self.ready = (self.ready.astype(f32) + recv.astype(f32)).astype(bf16)
        elif k == len(dims) + 3:
            self.out = (self.ready, recv)
        else:
            self.ready = join(self.ready, recv)

    def step(self):
        self.start()
        self.land()

    def finish(self):
        while self.out is None:
            self.step()
        return self.out


def sum_all(x, n):
    for b in range(n.bit_length() - 1):
        x = x + swap(x, 1 << b, n)
    return x


def gather_all(x, n):
    for b in reversed(range(n.bit_length() - 1)):
        x = join(x, swap(x, 1 << b, n))
    return x


BATCH = 4


def spread_kernel(dims, cuts, count, me, x, y, *refs):
    outs = refs[-count:]
    low = flip_of(me[0], dims) & (BATCH - 1)
    pr = x.shape[1]

    def put(src):
        for t in range(BATCH):
            col = 0
            for out, cols in zip(outs, cuts):
                out[t * pr : (t + 1) * pr, :] = src[t ^ low, :, col : col + cols].astype(f32)
                col += cols

    j = pl.program_id(0)
    here = PIECES // 2 // BATCH
    pl.when(j < here)(lambda: put(x))
    pl.when(j >= here)(lambda: put(y))


def spread(dims, me, x, y, places, previous, name):
    ins = [me, x, y]
    pr = x.shape[1]
    half = PIECES // 2 // BATCH
    block = (BATCH,) + x.shape[1:]
    specs = [
        pl.BlockSpec(block, lambda j, f: (jnp.minimum(j, half - 1), 0, 0)),
        pl.BlockSpec(block, lambda j, f: (jnp.maximum(j - half, 0), 0, 0)),
    ]
    aliases = {}
    if previous is not None:
        for i, g in enumerate(previous):
            aliases[3 + i] = i
            ins.append(g)
            specs.append(pl.BlockSpec(memory_space=pl.ANY))

    def place(col):
        return lambda j, f: (j ^ lax.div(flip_of(f[0], dims), BATCH), col)

    return pl.pallas_call(
        functools.partial(spread_kernel, dims, [c for c, _, _ in places], len(places)),
        grid_spec=pltpu.PrefetchScalarGridSpec(
            num_scalar_prefetch=1,
            grid=(PIECES // BATCH,),
            in_specs=specs,
            out_specs=[pl.BlockSpec((BATCH * pr, c), place(col)) for c, col, _ in places],
        ),
        out_shape=[struct((PIECES * pr, w), f32) for _, _, w in places],
        input_output_aliases=aliases,
        compiler_params=params(24),
        cost_estimate=cost(1e6, 6 * x.size * 2),
        name=name,
    )(*ins)


def axis_orders(n):
    rest = [1 << i for i in range(1, n.bit_length() - 1)]
    if n == 32:
        x, y, z, far = rest
        return [(1, x, z, y, far), (1, y, x, z, far), (1, z, y, x, far)]
    return [tuple([1] + rest[i:] + rest[:i]) for i in range(PORTIONS)]


def body(
    tokens, seg_lengths, owner, place, w_qkv, b_qv, w_out, b_out, ln1_gain, ln1_bias,
    w_up, b_up, w_down, b_down, ln2_gain, ln2_bias, w_proj,
):
    rows, width = tokens.shape
    ff = w_up.shape[1]
    n = lax.axis_size("dp")
    me = lax.axis_index("dp").astype(i32).reshape(1)
    orders = axis_orders(n)

    packed, attended, lse = attention(seg_lengths, tokens, w_qkv, b_qv)
    ht, act, slp, n1, i1, n2, i2, nl, emb, ul, query = mid_fwd(
        seg_lengths, attended, tokens, w_out, b_out, ln1_gain, ln1_bias, w_up, b_up,
        w_down, b_down, ln2_gain, ln2_bias, w_proj,
    )

    msg, dpb = loss_forward(me, seg_lengths, owner, gather_all(query, n), ul)
    loss, dr2, dbr, gwp, sums2 = loss_back(
        me, seg_lengths, owner, place, gather_all(msg, n), dpb, emb, nl, n2, i2, ln2_gain, w_proj
    )

    down = Chain(*down_grad(orders[0], me, act, dbr), orders[0], n)
    down.start()
    keep, send, din, dsum = up_grad(orders[1], after(me, down.ready), dbr, slp, w_down, ht)
    up = Chain(keep, send, orders[1], n)
    down.land(dsum)
    down.start()
    up.start()
    dr1, dpr, dat, sums1 = mid_back(
        after(me, down.ready, up.ready), din, w_up, dr2, n1, i1, ln1_gain, w_out
    )
    up.land(sums1)
    up.start()
    parts = [
        attention_back(0, after(seg_lengths, up.ready), packed, dat, attended, lse)
    ]
    down.land(parts[0][3])
    down.start()
    parts.append(
        attention_back(1, after(seg_lengths, down.ready), packed, dat, attended, lse)
    )
    down.land(parts[1][3])
    up.land(parts[1][3])
    down.start()
    up.start()
    parts.append(
        attention_back(2, after(seg_lengths, down.ready, up.ready), packed, dat, attended, lse)
    )
    down.land(parts[2][3])
    up.land(parts[2][3])
    down.start()
    up.start()
    held = after(me, down.ready, up.ready)
    vector = collect([x[3] for x in parts], dsum, sums1, sums2)
    more = []
    for p in reversed(range(PORTIONS)):
        keep, send = qkv_grad(
            p, orders[p], held, tokens, [x[p] for x in parts], attended, dpr, gwp if p == 2 else None
        )
        more.append((p, Chain(keep, send, orders[p], n)))
    d_tokens = input_grad(
        after(me, *[c.ready for _, c in more]), [x[p] for p in range(3) for x in parts], w_qkv, dr1
    )
    down.land()
    up.land()

    g_w_down = spread(orders[0], me, *down.finish(), [(width, 0, width)], None, "down_place")[0]
    g_w_up = spread(orders[1], me, *up.finish(), [(ff, 0, ff)], None, "up_place")[0]
    vector = sum_all(vector, n)
    grads = None
    for p, c in more:
        places = [(width, p, 3 * width), (256, p, width)]
        if p == 2:
            places.append((128, 0, 128))
        out = spread(orders[p], me, *c.finish(), places, grads, "qkv_place")
        grads = out[:2]
        if p == 2:
            g_w_proj = out[2]
    g_w_qkv, g_w_out = grads
    at = 5 + ff // width
    return (
        loss[0, 0:1], d_tokens, g_w_qkv, vector[0:2].reshape(-1), g_w_out, vector[2], vector[3],
        vector[4], g_w_up, vector[5:at].reshape(-1), g_w_down, vector[at], vector[at + 1],
        vector[at + 2], g_w_proj,
    )


def solution(mesh):
    whole_rows = P("dp", None)
    return jax.shard_map(
        body,
        mesh=mesh,
        in_specs=(whole_rows, whole_rows) + (P(),) * 15,
        out_specs=(P("dp"), whole_rows) + (P(),) * 13,
        check_vma=False,
    )
```

```python
import functools

import jax
import jax.numpy as jnp
from jax import lax
from jax.experimental import pallas as pl
from jax.experimental.pallas import tpu as pltpu
from jax.sharding import PartitionSpec as P

HEADS = 12
QLEN = 32
PLEN = 180
QB = 128
WIDTHS = (256, 384, 512, 768, 1024)
PIECES = 16
PORTIONS = 3
NEG = -1e30
LN_EPS = 1e-12
NORM_EPS = 1e-6
f32, bf16, i32 = jnp.float32, jnp.bfloat16, jnp.int32


def nn(a, b):
    return lax.dot_general(a, b, (((1,), (0,)), ((), ())), preferred_element_type=f32)


def nt(a, b):
    return lax.dot_general(a, b, (((1,), (1,)), ((), ())), preferred_element_type=f32)


def tn(a, b):
    return lax.dot_general(a, b, (((0,), (0,)), ((), ())), preferred_element_type=f32)


def params(mib=48):
    return pltpu.CompilerParams(vmem_limit_bytes=mib << 20)


def cost(flops, nbytes):
    return pl.CostEstimate(flops=int(flops), bytes_accessed=int(nbytes), transcendentals=0)


SMEM = pl.BlockSpec(memory_space=pltpu.SMEM)
VMEM = pl.BlockSpec(memory_space=pltpu.VMEM)


def whole(shape):
    return pl.BlockSpec(shape, lambda *g: (0,) * len(shape))


def held(shape):
    return pl.BlockSpec(shape, lambda *g: (0,) * len(shape), pipeline_mode=pl.Buffered(1))


def struct(shape, dtype):
    return jax.ShapeDtypeStruct(shape, dtype)


def row(v):
    return v[...].reshape(1, -1)


def normalize(resid):
    center = resid - jnp.mean(resid, axis=-1, keepdims=True)
    inv = lax.rsqrt(jnp.mean(center * center, axis=-1, keepdims=True) + LN_EPS)
    return center * inv, inv


def segment_ends(lens):
    ends = [lens[0, 0]]
    for s in range(1, lens.shape[1]):
        ends.append(ends[-1] + lens[0, s])
    return ends


def segment_of(ends, position):
    seg = jnp.zeros(position.shape, i32)
    for e in ends:
        seg = seg + (position >= e).astype(i32)
    return seg


def key_window(ends, rows, first):
    lo = jnp.zeros((), i32)
    hi = jnp.asarray(rows, i32)
    for e in ends:
        lo = jnp.where(e <= first, e, lo)
    for e in reversed(ends):
        hi = jnp.where(e >= first + QB, e, hi)
    lo = lax.div(lo, QB) * QB
    need = hi - lo
    cls = jnp.zeros((), i32)
    wide = jnp.asarray(WIDTHS[0], i32)
    for c, w in enumerate(WIDTHS[:-1]):
        if WIDTHS[c + 1] <= rows:
            cls = jnp.where(need > w, c + 1, cls)
            wide = jnp.where(need > w, WIDTHS[c + 1], wide)
    return pl.multiple_of(jnp.minimum(lo, rows - wide), QB), cls


def fill_segments(ends, segq, segk):
    segk[...] = segment_of(ends, lax.broadcasted_iota(i32, segk.shape, 0))
    at = lax.broadcasted_iota(i32, segq.shape, 0) * QB + lax.broadcasted_iota(i32, segq.shape, 1)
    segq[...] = segment_of(ends, at)


def two_heads(x, scale=None):
    lane = lax.broadcasted_iota(i32, x.shape, 1)
    zero = jnp.zeros_like(x)
    if scale is not None:
        x = x * scale
    return jnp.concatenate([jnp.where(lane < 64, x, zero), jnp.where(lane < 64, zero, x)], axis=0)


def pick_heads(t):
    return jnp.concatenate([t[:64, :QB], t[64:, QB:]], axis=0)


def attn_fwd_kernel(
    lens, tok, wqkv, bqv, wo, bo, g1, b1,
    packed, out, lse, hid, low, ht, n1, i1, vt, segq, segk,
):
    rows, width = tok.shape
    ends = segment_ends(lens)
    fill_segments(ends, segq, segk)
    pairs = width // 128
    for j in range(3 * width // 256):
        at = slice(j * 256, (j + 1) * 256)
        x = nn(tok[...], wqkv[:, at])
        which = j * 256 // width
        if which != 1:
            b0 = j * 256 - (width if which else 0)
            x = x + bqv[b0 : b0 + 256].reshape(1, 256)
        packed[:, at] = x.astype(bf16)
    q = packed.at[:, 0:width]
    k = packed.at[:, width : 2 * width]
    v = packed.at[:, 2 * width : 3 * width]
    for g in range(pairs):
        vt[g] = v[:, g * 128 : (g + 1) * 128].T

    def step(i, carry):
        base = pl.multiple_of(i * QB, QB)
        k0, cls = key_window(ends, rows, base)
        sq = segq[pl.ds(i, 1), :]

        def body(w):
            same = segk[pl.ds(k0, w), :] == sq
            sts = []
            for g in range(pairs):
                sl = slice(g * 128, (g + 1) * 128)
                q2 = two_heads(q[pl.ds(base, QB), sl], jnp.asarray(0.125, bf16))
                sts.append(nt(k[pl.ds(k0, w), sl], q2))
            for g in range(pairs):
                sl = slice(g * 128, (g + 1) * 128)
                st = sts[g]
                ps, ms, ls = [], [], []
                for h in range(2):
                    s = jnp.where(same, st[:, h * QB : (h + 1) * QB], NEG)
                    m = jnp.max(s, axis=0, keepdims=True)
                    p = jnp.exp(s - m)
                    ls.append(jnp.sum(p, axis=0, keepdims=True))
                    ms.append(m)
                    ps.append(p.astype(bf16))
                total = jnp.concatenate(ls, 1)
                top = jnp.concatenate(ms, 1)
                ot = nn(vt[g, :, pl.ds(k0, w)], jnp.concatenate(ps, 1)) * (1.0 / total)
                out[pl.ds(base, QB), sl] = pick_heads(ot).T.astype(bf16)
                lse[g, pl.ds(i, 1), :] = top + jnp.log(total)

        for c, w in enumerate(WIDTHS):
            if w <= rows:
                pl.when(cls == c)(functools.partial(body, w))
        return carry

    lax.fori_loop(0, rows // QB, step, 0)
    tile = 256
    for r0 in range(0, rows, tile):
        r = slice(r0, r0 + tile)
        resid = tok[r, :].astype(f32) + (nn(out[r, :], wo[...]) + row(bo))
        normal, inv = normalize(resid)
        hidden = normal * row(g1) + row(b1)
        hid[r, :] = hidden
        hl = hidden.astype(bf16)
        low[r, :] = hl
        ht[:, r] = hl.T
        n1[r, :] = normal.astype(bf16)
        i1[r, :] = inv


def attn_bwd_kernel(
    part, lens, packed, do, o, lse, dq, dk, dv, sums, kt, dka, dva, segq, segk
):
    rows = packed.shape[0]
    width = packed.shape[1] // 3
    span = dq.shape[1]
    ends = segment_ends(lens)
    fill_segments(ends, segq, segk)
    pairs = span // 128
    q, k, v = [packed.at[:, i * width + part * span : i * width + (part + 1) * span] for i in range(3)]
    do = do.at[:, part * span : (part + 1) * span]
    o = o.at[:, part * span : (part + 1) * span]
    for g in range(pairs):
        kt[g] = k[:, g * 128 : (g + 1) * 128].T
    dka[...] = jnp.zeros_like(dka)
    dva[...] = jnp.zeros_like(dva)
    head = (
        lax.broadcasted_iota(i32, (8, 128), 0) == lax.broadcasted_iota(i32, (8, 128), 1) // 64
    ).astype(f32)

    def step(i, carry):
        base = pl.multiple_of(i * QB, QB)
        k0, cls = key_window(ends, rows, base)
        sq = segq[pl.ds(i, 1), :]

        def body(w):
            at = pl.ds(k0, w)
            same = segk[at, :] == sq
            for g in range(pairs):
                gs = slice(g * 128, (g + 1) * 128)
                q2 = two_heads(q[pl.ds(base, QB), gs], jnp.asarray(0.125, bf16))
                do_ = do[pl.ds(base, QB), gs]
                do2 = two_heads(do_)
                d8 = lax.dot_general(
                    head,
                    do_.astype(f32) * o[pl.ds(base, QB), gs].astype(f32),
                    (((1,), (1,)), ((), ())),
                    precision=lax.Precision.HIGHEST,
                    preferred_element_type=f32,
                )
                lrow = lse[part * pairs + g, pl.ds(i, 1), :]
                st = nt(k[at, gs], q2)
                dpt = nt(v[at, gs], do2)
                ps, ds = [], []
                for h in range(2):
                    sl = slice(h * QB, (h + 1) * QB)
                    p = jnp.exp(jnp.where(same, st[:, sl] - lrow[:, sl], NEG))
                    ps.append(p.astype(bf16))
                    ds.append((p * (dpt[:, sl] - d8[h : h + 1, :])).astype(bf16))
                p = jnp.concatenate(ps, 1)
                d = jnp.concatenate(ds, 1)
                dka[at, gs] += nn(d, q2)
                dva[at, gs] += nn(p, do2)
                dqt = nn(kt[g, :, pl.ds(k0, w)], d)
                dq[pl.ds(base, QB), gs] = (pick_heads(dqt).T * 0.125).astype(bf16)

        for c, w in enumerate(WIDTHS):
            if w <= rows:
                pl.when(cls == c)(functools.partial(body, w))
        return carry

    lax.fori_loop(0, rows // QB, step, 0)
    dk[...] = dka[...].astype(bf16)
    dvl = dva[...].astype(bf16)
    dv[...] = dvl
    sums[0:1, :] = jnp.sum(dq[...].astype(f32), axis=0, keepdims=True)
    sums[1:2, :] = jnp.sum(dvl.astype(f32), axis=0, keepdims=True)


def segment_scratch(rows):
    return [pltpu.VMEM((rows // QB, QB), i32), pltpu.VMEM((rows, 128), i32)]


def attention(lens, tok, wqkv, bqv, wo, bo, g1, b1):
    rows, width = tok.shape
    pairs = width // 128
    return pl.pallas_call(
        attn_fwd_kernel,
        in_specs=[SMEM] + [VMEM] * 7,
        out_specs=[VMEM] * 8,
        out_shape=[
            struct((rows, 3 * width), bf16),
            struct((rows, width), bf16),
            struct((pairs, rows // QB, 2 * QB), f32),
            struct((rows, width), f32),
            struct((rows, width), bf16),
            struct((width, rows), bf16),
            struct((rows, width), bf16),
            struct((rows, 1), f32),
        ],
        scratch_shapes=[pltpu.VMEM((pairs, 128, rows), bf16)] + segment_scratch(rows),
        compiler_params=params(32),
        cost_estimate=cost(18e9, 8 * rows * width),
        name="attention_forward",
    )(lens, tok, wqkv, bqv, wo, bo, g1, b1)


def attention_back(part, lens, packed, do, o, lse):
    rows, width = packed.shape[0], packed.shape[1] // 3
    span = width // PORTIONS
    pairs = span // 128
    shp = struct((rows, span), bf16)
    return pl.pallas_call(
        functools.partial(attn_bwd_kernel, part),
        in_specs=[SMEM] + [VMEM] * 4,
        out_specs=[VMEM] * 4,
        out_shape=[shp, shp, shp, struct((8, span), f32)],
        scratch_shapes=[
            pltpu.VMEM((pairs, 128, rows), bf16),
            pltpu.VMEM((rows, span), f32),
            pltpu.VMEM((rows, span), f32),
        ]
        + segment_scratch(rows),
        compiler_params=params(24),
        cost_estimate=cost(10e9, 16 * rows * span),
        name="attention_backward",
    )(lens, packed, do, o, lse)


def norm_back(grad, gain, normal, inv):
    dn = grad * gain
    return inv * (
        dn
        - jnp.mean(dn, axis=-1, keepdims=True)
        - normal * jnp.mean(dn * normal, axis=-1, keepdims=True)
    )


FF_CHUNK = 1024


def ffn_fwd_kernel(
    lens, hid, low, wu, bu, wd, bd, g2, b2, wp, act, slp, n2, i2, nl, emb, ul, msg, acc
):
    c = pl.program_id(0)
    rows = low.shape[0]
    span = hid.shape[1]
    tile = 256
    tiles = [slice(r, r + tile) for r in range(0, rows, tile)]

    @pl.when(c == 0)
    def _():
        for r in tiles:
            acc[r, :] = jnp.broadcast_to(row(bd), acc[r, :].shape)

    for r in tiles:
        inner = nn(low[r, :], wu[...]) + row(bu)
        cdf = 0.5 + 0.5 * lax.erf(inner * 0.7071067811865476)
        a = (inner * cdf).astype(bf16)
        act[r, :] = a
        slp[r, :] = (cdf + inner * (jnp.exp(inner * inner * -0.5) * 0.3989422804014327)).astype(bf16)
        acc[r, :] += nn(a, wd[...])
    at = pl.ds(pl.multiple_of(c * span, span), span)
    acc[:, at] += hid[...]

    @pl.when(c == pl.num_programs(0) - 1)
    def _():
        for r in tiles:
            normal, inv = normalize(acc[r, :])
            normed = (normal * row(g2) + row(b2)).astype(bf16)
            n2[r, :] = normal.astype(bf16)
            i2[r, :] = inv
            nl[r, :] = normed
            e = nn(normed, wp[...])
            emb[r, :] = e
            ul[r, :] = (
                e * lax.rsqrt(jnp.sum(e * e, axis=-1, keepdims=True) + NORM_EPS)
            ).astype(bf16)
        count = lens[0, 0]
        slot = lax.broadcasted_iota(i32, (QLEN, ul.shape[1]), 0)
        msg[0, 0:QLEN, :] = jnp.where(slot < count, ul[0:QLEN, :].astype(f32), 0.0).astype(bf16)
        msg[0, QLEN : QLEN + 16, :] = (
            jnp.full((16, ul.shape[1]), count, i32).astype(f32).astype(bf16)
        )


def ffn_fwd(lens, hid, low, wu, bu, wd, bd, g2, b2, wp):
    rows, width = hid.shape
    ff, out = wu.shape[1], wp.shape[1]
    steps = ff // FF_CHUNK
    ins = [lens, hid, low, wu, bu, wd, bd, g2, b2, wp]
    specs = [held(x.shape) for x in ins]
    specs[0] = SMEM
    specs[1] = pl.BlockSpec((rows, width // steps), lambda c: (0, c))
    specs[3] = pl.BlockSpec((width, FF_CHUNK), lambda c: (0, c))
    specs[4] = pl.BlockSpec((FF_CHUNK,), lambda c: (c,))
    specs[5] = pl.BlockSpec((FF_CHUNK, width), lambda c: (c, 0))
    outs = [
        struct((rows, ff), bf16),
        struct((rows, ff), bf16),
        struct((rows, width), bf16),
        struct((rows, 1), f32),
        struct((rows, width), bf16),
        struct((rows, out), f32),
        struct((rows, out), bf16),
        struct((1, QLEN + 16, out), bf16),
    ]
    ospecs = [whole(x.shape) for x in outs]
    ospecs[0] = ospecs[1] = pl.BlockSpec((rows, FF_CHUNK), lambda c: (0, c))
    return pl.pallas_call(
        ffn_fwd_kernel,
        grid=(steps,),
        in_specs=specs,
        out_specs=ospecs,
        out_shape=outs,
        scratch_shapes=[pltpu.VMEM((rows, width), f32)],
        compiler_params=params(36),
        cost_estimate=cost(18e9, 40e6),
        name="ffn_forward",
    )(*ins)


def relative(device, n):
    bits = n.bit_length() - 1
    at = jnp.zeros((), i32)
    for b in range(bits):
        at = at | (((device >> b) & 1) << (bits - 1 - b))
    return at


def loss_kernel(me, lens, owner, gathered, ul, msg, dpb):
    n, nump = owner.shape
    rows = ul.shape[0]
    total = nump * QLEN
    seg = segment_of(segment_ends(lens), lax.broadcasted_iota(i32, (1, rows), 1))
    rel = [relative(owner[me[0], p] ^ me[0], n) for p in range(nump)]
    qs = [gathered[rel[p], 0:QLEN, :] for p in range(nump)]
    q = jnp.concatenate(qs, axis=0)
    slot = lax.broadcasted_iota(i32, (QLEN, 1), 0).astype(f32)
    valid = jnp.concatenate(
        [
            (slot < gathered[rel[p], QLEN : QLEN + 16, :][0:1, 0:1].astype(f32)).astype(f32)
            for p in range(nump)
        ],
        axis=0,
    )
    group = lax.broadcasted_iota(i32, (total, rows), 0) // QLEN + 1
    x = jnp.where(group == seg, nt(q, ul[...]) * 10.0, NEG)
    top = jnp.max(x, axis=1, keepdims=True)
    e = jnp.exp(x - top)
    sm = jnp.sum(e, axis=1, keepdims=True)
    soft = valid * (0.1 * (top + jnp.log(sm)))
    lane = lax.broadcasted_iota(i32, (1, 128), 1)
    score = jnp.zeros((1, 128), f32)
    for p in range(nump):
        score = score + jnp.where(
            lane == p, jnp.sum(soft[p * QLEN : (p + 1) * QLEN], axis=0, keepdims=True), 0.0
        )
    w = e * (valid / sm)
    wh = w.astype(bf16)
    wl = (w - wh.astype(f32)).astype(bf16)
    msg[0, 0:total, :] = (nn(wh, ul[...]) + nn(wl, ul[...])).astype(bf16)
    hi = score.astype(bf16)
    rest = score - hi.astype(f32)
    mid = rest.astype(bf16)
    lo = (rest - mid.astype(f32)).astype(bf16)
    row = lax.broadcasted_iota(i32, (16, 128), 0)
    tail = jnp.where(row == 0, hi.astype(f32), 0.0)
    tail = tail + jnp.where(row == 1, mid.astype(f32), 0.0)
    tail = tail + jnp.where(row == 2, lo.astype(f32), 0.0)
    msg[0, total : total + 16, :] = tail.astype(bf16)
    dpb[...] = tn(wh, q) + tn(wl, q)


def loss_forward(me, lens, owner, gathered, ul):
    rows, out = ul.shape
    total = owner.shape[1] * QLEN
    smem = pl.BlockSpec(memory_space=pltpu.SMEM)
    vmem = pl.BlockSpec(memory_space=pltpu.VMEM)
    return pl.pallas_call(
        loss_kernel,
        in_specs=[smem] * 3 + [vmem] * 2,
        out_specs=[vmem] * 2,
        out_shape=[struct((1, total + 16, out), bf16), struct((rows, out), f32)],
        compiler_params=params(16),
        cost_estimate=cost(1e9, 2e6),
        name="loss_forward",
    )(me, lens, owner, gathered, ul)


def loss_back_kernel(
    me, lens, owner, place, messages, dpb, emb, nl, n2, i2, g2, wp,
    loss, dr2, dbr, gwp, sums, du, gwpt, inverse,
):
    n, nump = owner.shape
    groups = nump + 1
    rows, width = nl.shape
    total = nump * QLEN
    mine = me[0]

    def note(i, carry):
        for p in range(nump):
            inverse[owner[i, p] * nump + place[i, p]] = i * nump + p
        return carry

    lax.fori_loop(0, n, note, 0)
    group = [mine] + [owner[mine, p] for p in range(nump)]
    plc = [place[mine, p] for p in range(nump)]
    src, col = {}, {}
    for g in range(groups):
        for r in range(nump):
            entry = inverse[group[g] * nump + r]
            src[g, r] = relative(lax.div(entry, nump) ^ mine, n)
            col[g, r] = lax.rem(entry, nump)
    lane = lax.broadcasted_iota(i32, (8, 128), 1)
    sub = lax.broadcasted_iota(i32, (8, 128), 0)
    vals = []
    for r in range(nump):
        a = jnp.zeros((8, 128), f32)
        for g in range(groups):
            t = messages[src[g, r], total : total + 16, :].astype(f32)
            t = t[0:1, :] + t[1:2, :] + t[2:3, :]
            a = jnp.where((sub == g) & (lane == col[g, r]), t, a)
        vals.append(jnp.sum(a, axis=1, keepdims=True))
    top = vals[0]
    for v in vals[1:]:
        top = jnp.maximum(top, v)
    es = [jnp.exp(v - top) for v in vals]
    sm = es[0]
    for e in es[1:]:
        sm = sm + e
    loss[...] = jnp.broadcast_to((top + jnp.log(sm) - vals[0])[0:1], (8, 128))
    dt = [e / sm - (1.0 if r == 0 else 0.0) for r, e in enumerate(es)]
    sub1 = lax.broadcasted_iota(i32, (8, 1), 0)
    place = jnp.zeros((8, 1), i32)
    for p in range(nump):
        place = jnp.where(sub1 == p + 1, plc[p], place)
    dscore = jnp.zeros((8, 1), f32)
    for r in range(nump):
        dscore = jnp.where(place == r, dt[r], dscore)
    dmq = jnp.zeros((QLEN, 128), f32)
    for r in range(nump):
        at = pl.multiple_of(col[0, r] * QLEN, QLEN)
        dmq = dmq + dt[r][0:1] * messages[src[0, r], pl.ds(at, QLEN), :].astype(f32)
    sk = segment_of(segment_ends(lens), lax.broadcasted_iota(i32, (rows, 128), 0))
    scale = jnp.zeros(sk.shape, f32)
    for p in range(nump):
        scale = jnp.where(sk == p + 1, dscore[p + 1 : p + 2], scale)
    du[...] = scale * dpb[...]
    du[0:QLEN, :] = jnp.where(sk[0:QLEN] == 0, dmq, du[0:QLEN, :])

    gwpt[...] = jnp.zeros_like(gwpt)
    sums[...] = jnp.zeros_like(sums)
    tile = 256
    for r0 in range(0, rows, tile):
        r = slice(r0, r0 + tile)
        e = emb[r, :]
        inv = lax.rsqrt(jnp.sum(e * e, axis=-1, keepdims=True) + NORM_EPS)
        unit = e * inv
        d = du[r, :].astype(bf16).astype(f32)
        de = (inv * (d - unit * jnp.sum(unit * d, axis=-1, keepdims=True))).astype(bf16)
        gwpt[...] += tn(de, nl[r, :])
        dn = nt(de, wp[...])
        normal = n2[r, :].astype(f32)
        sums[0:1, :] += jnp.sum(dn * normal, axis=0, keepdims=True)
        sums[1:2, :] += jnp.sum(dn, axis=0, keepdims=True)
        dr = norm_back(dn, row(g2), normal, i2[r, :])
        dr2[r, :] = dr
        db = dr.astype(bf16)
        dbr[r, :] = db
        sums[2:3, :] += jnp.sum(db.astype(f32), axis=0, keepdims=True)
    gwp[...] = gwpt[...].T


def loss_back(me, lens, owner, place, messages, dpb, emb, nl, n2, i2, g2, wp):
    rows, width = nl.shape
    out = wp.shape[1]
    smem = pl.BlockSpec(memory_space=pltpu.SMEM)
    vmem = pl.BlockSpec(memory_space=pltpu.VMEM)
    return pl.pallas_call(
        loss_back_kernel,
        in_specs=[smem] * 4 + [vmem] * 8,
        out_specs=[vmem] * 5,
        out_shape=[
            struct((8, 128), f32),
            struct((rows, width), f32),
            struct((rows, width), bf16),
            struct((width, out), f32),
            struct((8, width), f32),
        ],
        scratch_shapes=[
            pltpu.VMEM((rows, out), f32),
            pltpu.VMEM((out, width), f32),
            pltpu.SMEM((owner.size,), i32),
        ],
        compiler_params=params(32),
        cost_estimate=cost(6e9, 10e6),
        name="loss_backward",
    )(me, lens, owner, place, messages, dpb, emb, nl, n2, i2, g2, wp)


def flip_of(device, dims):
    m = jnp.zeros((), i32)
    for i, d in enumerate(dims[:4]):
        m = m | jnp.where((device & d) != 0, 8 >> i, 0)
    return m


def sides(me, dims, keep, send):
    m = flip_of(me[0], dims)
    half = PIECES // 2
    top, low = lax.div(m, half), lax.rem(m, half)
    return [(keep, top, low), (send, 1 - top, low)]


def down_grad_kernel(dims, me, act, dbr, gwp, keep, send):
    pr, width = keep.shape[1], dbr.shape[1]
    parts = act.shape[1] // width
    half = PIECES // 2
    for dst, side, low in sides(me, dims, keep, send):
        for t in range(0, half, 2):
            at = pl.multiple_of((side * half + t) * (pr * parts), 128)
            g = tn(act[:, pl.ds(at, 2 * pr * parts)], dbr[...])
            for u in range(2):
                for i in range(parts):
                    r = (u * parts + i) * pr
                    dst[(t + u) ^ low, :, i * width : (i + 1) * width] = g[r : r + pr]
                first = pl.multiple_of((side * half + t + u) * pr, 16)
                dst[(t + u) ^ low, :, parts * width :] = gwp[pl.ds(first, pr), :]


def down_grad(dims, me, act, dbr, gwp):
    rows, width = dbr.shape
    buf = struct((PIECES // 2, width // PIECES, act.shape[1] + gwp.shape[1]), f32)
    return pl.pallas_call(
        functools.partial(down_grad_kernel, dims),
        in_specs=[SMEM] + [VMEM] * 3,
        out_specs=[VMEM] * 2,
        out_shape=[buf, buf],
        compiler_params=params(32),
        cost_estimate=cost(5e9, 17e6),
        name="down_gradient",
    )(me, act, dbr, gwp)


def up_grad_kernel(dims, me, dbr, slp, wd, ht, keep, send, din, dsum):
    pr = keep.shape[1]
    half = PIECES // 2
    rows = dbr.shape[0]
    tile = 256
    dsum[...] = jnp.zeros_like(dsum)
    for r0 in range(0, rows, tile):
        r = slice(r0, r0 + tile)
        d_inner = (nt(dbr[r, :], wd[...]) * slp[r, :].astype(f32)).astype(bf16)
        din[r, :] = d_inner
        dsum[...] += jnp.sum(d_inner.astype(f32), axis=0, keepdims=True)
    for dst, side, low in sides(me, dims, keep, send):
        at = pl.multiple_of(side * (half * pr), half * pr)
        g = nn(ht[pl.ds(at, half * pr), :], din[...])
        for t in range(half):
            dst[t ^ low] = g[t * pr : (t + 1) * pr]


def up_grad(dims, me, dbr, slp, wd, ht):
    rows, width = dbr.shape
    ff = slp.shape[1]
    half, pr = PIECES // 2, width // PIECES
    buf = struct((half, pr, ff), f32)
    part = pl.BlockSpec((half, pr, FF_CHUNK), lambda c: (0, 0, c))
    wide = pl.BlockSpec((rows, FF_CHUNK), lambda c: (0, c))
    return pl.pallas_call(
        functools.partial(up_grad_kernel, dims),
        grid=(ff // FF_CHUNK,),
        in_specs=[
            SMEM,
            held(dbr.shape),
            wide,
            pl.BlockSpec((FF_CHUNK, width), lambda c: (c, 0)),
            held(ht.shape),
        ],
        out_specs=[part, part, wide, pl.BlockSpec((1, FF_CHUNK), lambda c: (0, c))],
        out_shape=[buf, buf, struct((rows, ff), bf16), struct((1, ff), f32)],
        compiler_params=params(36),
        cost_estimate=cost(10e9, 30e6),
        name="up_gradient",
    )(me, dbr, slp, wd, ht)


def mid_back_kernel(me, din, wu, dr2, n1, i1, g1, wo, dr1, dpr, dat, sums, acc):
    c = pl.program_id(0)
    rows, width = dr1.shape
    span = dr2.shape[1]

    @pl.when(c == 0)
    def _():
        acc[...] = nt(din[...], wu[...])

    @pl.when(c > 0)
    def _():
        acc[...] += nt(din[...], wu[...])

    at = pl.ds(pl.multiple_of(c * span, span), span)
    acc[:, at] += dr2[...]

    @pl.when(c == pl.num_programs(0) - 1)
    def _():
        sums[...] = jnp.zeros_like(sums)
        tile = 256
        for r0 in range(0, rows, tile):
            r = slice(r0, r0 + tile)
            d = acc[r, :]
            normal = n1[r, :].astype(f32)
            sums[0:1, :] += jnp.sum(d * normal, axis=0, keepdims=True)
            sums[1:2, :] += jnp.sum(d, axis=0, keepdims=True)
            dr = norm_back(d, row(g1), normal, i1[r, :])
            dr1[r, :] = dr
            low = dr.astype(bf16)
            dpr[r, :] = low
            sums[2:3, :] += jnp.sum(low.astype(f32), axis=0, keepdims=True)
            dat[r, :] = nt(low, wo[...]).astype(bf16)


def mid_back(me, din, wu, dr2, n1, i1, g1, wo):
    rows, width = dr2.shape
    ff = din.shape[1]
    steps = ff // FF_CHUNK
    ins = [me, din, wu, dr2, n1, i1, g1, wo]
    specs = [held(x.shape) for x in ins]
    specs[0] = SMEM
    specs[1] = pl.BlockSpec((rows, FF_CHUNK), lambda c: (0, c))
    specs[2] = pl.BlockSpec((width, FF_CHUNK), lambda c: (0, c))
    specs[3] = pl.BlockSpec((rows, width // steps), lambda c: (0, c))
    outs = [
        struct((rows, width), f32),
        struct((rows, width), bf16),
        struct((rows, width), bf16),
        struct((8, width), f32),
    ]
    return pl.pallas_call(
        mid_back_kernel,
        grid=(steps,),
        in_specs=specs,
        out_specs=[whole(x.shape) for x in outs],
        out_shape=outs,
        scratch_shapes=[pltpu.VMEM((rows, width), f32)],
        compiler_params=params(36),
        cost_estimate=cost(9e9, 15e6),
        name="middle_backward",
    )(*ins)


def qkv_grad_kernel(dims, has_out, me, tok, d0, d1, d2, *rest):
    keep, send = rest[-2:]
    pairs = [(tok, d0), (tok, d1), (tok, d2)]
    if has_out:
        pairs.append(rest[:2])
    half = PIECES // 2
    pr = keep.shape[1]
    for dst, side, low in sides(me, dims, keep, send):
        at = pl.ds(pl.multiple_of(side * (half * pr), half * pr), half * pr)
        col = 0
        for left, d in pairs:
            g = tn(left[:, at], d[...])
            cols = d.shape[1]
            for t in range(half):
                dst[t ^ low, :, col : col + cols] = g[t * pr : (t + 1) * pr]
            col += cols


def qkv_grad(dims, me, tok, ds, outer):
    rows, width = tok.shape
    ins = [me, tok, *ds, *outer]
    cols = sum(d.shape[1] for d in ds) + (width if outer else 0)
    buf = struct((PIECES // 2, width // PIECES, cols), f32)
    return pl.pallas_call(
        functools.partial(qkv_grad_kernel, dims, bool(outer)),
        in_specs=[SMEM] + [VMEM] * (len(ins) - 1),
        out_specs=[VMEM] * 2,
        out_shape=[buf, buf],
        compiler_params=params(24),
        cost_estimate=cost(4e9, 8e6),
        name="qkv_gradient",
    )(*ins)


def input_grad_kernel(count, me, *refs):
    ds = refs[:count]
    w, dr1, out = refs[count:]
    tile = 256
    for r0 in range(0, out.shape[0], tile):
        r = slice(r0, r0 + tile)
        acc = dr1[r, :]
        for j, d in enumerate(ds):
            acc = acc + nt(d[r, :], w[:, j * 256 : (j + 1) * 256])
        out[r, :] = acc


def input_grad(me, ds, w, dr1):
    return pl.pallas_call(
        functools.partial(input_grad_kernel, len(ds)),
        in_specs=[SMEM] + [VMEM] * (len(ds) + 2),
        out_specs=VMEM,
        out_shape=struct(dr1.shape, f32),
        compiler_params=params(32),
        cost_estimate=cost(5e9, 15e6),
        name="input_gradient",
    )(me, *ds, w, dr1)


def collect_kernel(s0, s1, s2, dsum, sm1, sm2, out):
    width = out.shape[1]
    for j, s in enumerate((s0, s1, s2)):
        out[0:2, j * 256 : (j + 1) * 256] = s[0:2, :]
    out[2:3, :] = sm1[2:3, :]
    out[3:5, :] = sm1[0:2, :]
    end = 5
    for j in range(dsum.shape[1] // width):
        out[end : end + 1, :] = dsum[:, j * width : (j + 1) * width]
        end += 1
    out[end : end + 1, :] = sm2[2:3, :]
    out[end + 1 : end + 3, :] = sm2[0:2, :]
    out[end + 3 :, :] = jnp.zeros((out.shape[0] - end - 3, width), f32)


def collect(s, dsum, sm1, sm2):
    ins = [*s, dsum, sm1, sm2]
    return pl.pallas_call(
        collect_kernel,
        in_specs=[VMEM] * len(ins),
        out_specs=VMEM,
        out_shape=struct((16, sm1.shape[1]), f32),
        compiler_params=params(16),
        cost_estimate=cost(1e4, 1e5),
        name="collect_vectors",
    )(*ins)


def swap(x, mask, n):
    return lax.ppermute(x, "dp", [(i, i ^ mask) for i in range(n)])


def after(x, *others):
    return lax.optimization_barrier((x,) + others)[0]


def join(x, y):
    which = lax.broadcasted_iota(i32, (2,) + x.shape, 0)
    both = jnp.where(which == 0, x[None], y[None])
    return both.reshape((2 * x.shape[0],) + x.shape[1:])


class Chain:
    def __init__(self, keep, send, dims, n):
        self.keep, self.ready, self.dims, self.n = keep, send, dims, n
        self.at = 0
        self.out = None
        self.recv = None

    def start(self):
        k, dims = self.at, self.dims
        d = dims[k] if k < len(dims) else dims[3 - (k - len(dims))]
        self.recv = swap(self.ready, d, self.n)

    def land(self, *others):
        if self.recv is None:
            self.start()
        k, dims = self.at, self.dims
        self.at += 1
        recv = after(self.recv, *others) if others else self.recv
        self.recv = None
        if k < 4:
            recv = recv.astype(f32)
            half = self.keep.shape[0] // 2
            if k < 3:
                self.ready = (self.keep[half:] + recv[half:]).astype(bf16)
                self.keep = self.keep[:half] + recv[:half]
            else:
                self.ready = (self.keep + recv).astype(bf16)
        elif k < len(dims):
            self.ready = (self.ready.astype(f32) + recv.astype(f32)).astype(bf16)
        elif k == len(dims) + 3:
            self.out = (self.ready, recv)
        else:
            self.ready = join(self.ready, recv)

    def finish(self):
        while self.out is None:
            self.land()
        return self.out


class Total:
    def __init__(self, x, n):
        self.ready, self.n, self.at, self.recv, self.out = x, n, 0, None, None

    def start(self):
        self.recv = swap(self.ready, 1 << self.at, self.n)

    def land(self, *others):
        if self.recv is None:
            self.start()
        self.ready = self.ready + (after(self.recv, *others) if others else self.recv)
        self.recv = None
        self.at += 1
        if 1 << self.at == self.n:
            self.out = self.ready

    def finish(self):
        while self.out is None:
            self.land()
        return self.out


def gather_all(x, n):
    for b in reversed(range(n.bit_length() - 1)):
        x = join(x, swap(x, 1 << b, n))
    return x


BATCH = 4


def place_kernel(chains, layout, me, *refs):
    bufs, outs = refs[: 2 * len(chains)], refs[2 * len(chains) :]
    a = pl.program_id(0)
    here = PIECES // 2 // BATCH
    for i, dims in enumerate(chains):
        flip = flip_of(me[0], dims)
        low = flip & (BATCH - 1)
        group = a ^ lax.div(flip, BATCH)
        pr = bufs[2 * i].shape[1]

        def put(src, i=i, low=low, pr=pr):
            for t in range(BATCH):
                for which, col, cols, row0, out, out_col, out_rows in layout:
                    if which == i:
                        at = t * out_rows + row0
                        outs[out][at : at + pr, out_col : out_col + cols] = src[
                            t ^ low, :, col : col + cols
                        ].astype(f32)

        pl.when(group < here)(functools.partial(put, bufs[2 * i]))
        pl.when(group >= here)(functools.partial(put, bufs[2 * i + 1]))


def put_in_place(chains, me, layout, shapes, name):
    half = PIECES // 2 // BATCH
    ins, specs = [me], []

    def block(dims, second):
        def index(a, f):
            group = a ^ lax.div(flip_of(f[0], dims), BATCH)
            return (jnp.maximum(group - half, 0) if second else jnp.minimum(group, half - 1), 0, 0)

        return index

    for c in chains:
        for second, x in enumerate(c.out):
            ins.append(x)
            specs.append(pl.BlockSpec((BATCH,) + x.shape[1:], block(c.dims, second)))
    return pl.pallas_call(
        functools.partial(place_kernel, [c.dims for c in chains], layout),
        grid_spec=pltpu.PrefetchScalarGridSpec(
            num_scalar_prefetch=1,
            grid=(PIECES // BATCH,),
            in_specs=specs,
            out_specs=[
                pl.BlockSpec((r * BATCH // PIECES, w), lambda a, f: (a, 0)) for r, w in shapes
            ],
        ),
        out_shape=[struct(x, f32) for x in shapes],
        compiler_params=params(24),
        cost_estimate=cost(1e6, 6 * sum(x.size for x in ins)),
        name=name,
    )(*ins)


SCHEDULE = (
    "+D up +U -D +D mid -U +U E0 q0 +Q0 -D +D E1 -U +U",
    "-Q0 +Q0 -D +D q1 +Q1 E2 -D +D -Q1 +Q1 q2 +Q2 -U +U",
    "-Q0 +Q0 -Q2 +Q2 vec +V -Q1 +Q1 -D +D -U +U -V +V in",
    "-Q0 +Q0 -Q2 +Q2 -Q1 +Q1 -V +V -Q0 +Q0 -D +D -U +U",
    "-V +V -Q1 +Q1 -Q2 +Q2 -Q0 +Q0 -U +U -Q2 +Q2 -Q1 +Q1",
    "-D +D -Q0 +Q0 -Q2 +Q2 -Q1 +Q1 -V +V -Q2 +Q2 -Q0 +Q0",
    "-U +U -Q1 +Q1 -V -Q2 +Q2 -Q1 +Q1 -Q0 +Q0 -Q2 +Q2",
    "-D +D -Q0 -Q1 -Q2 =Q -U +U -D =D -U =U",
)


def axis_orders(n):
    rest = [1 << i for i in range(1, n.bit_length() - 1)]
    if n == 32:
        x, y, z, far = rest
        return {
            "D": (1, x, y, z, far),
            "U": (1, z, y, x, far),
            "Q0": (1, y, z, x, far),
            "Q1": (1, x, y, z, far),
            "Q2": (1, y, z, x, far),
        }
    names = ("D", "U", "Q0", "Q1", "Q2")
    return {name: tuple([1] + rest[i:] + rest[:i]) for i, name in enumerate(names)}


def body(
    tokens, seg_lengths, owner, place, w_qkv, b_qv, w_out, b_out, ln1_gain, ln1_bias,
    w_up, b_up, w_down, b_down, ln2_gain, ln2_bias, w_proj,
):
    rows, width = tokens.shape
    ff = w_up.shape[1]
    n = lax.axis_size("dp")
    me = lax.axis_index("dp").astype(i32).reshape(1)
    orders = axis_orders(n)

    packed, attended, lse, hid, low, ht, n1, i1 = attention(
        seg_lengths, tokens, w_qkv, b_qv, w_out, b_out, ln1_gain, ln1_bias
    )
    act, slp, n2, i2, nl, emb, ul, query = ffn_fwd(
        seg_lengths, hid, low, w_up, b_up, w_down, b_down, ln2_gain, ln2_bias, w_proj
    )

    msg, dpb = loss_forward(me, seg_lengths, owner, gather_all(query, n), ul)
    loss, dr2, dbr, gwp, sums2 = loss_back(
        me, seg_lengths, owner, place, gather_all(msg, n), dpb, emb, nl, n2, i2, ln2_gain, w_proj
    )

    chains = {"D": Chain(*down_grad(orders["D"], me, act, dbr, gwp), orders["D"], n)}
    flying = {}
    parts = []
    placed = {}
    last = None

    def now(x):
        return after(x, *flying.values()) if flying else x

    def finish(name):
        for other in ("Q0", "Q1", "Q2") if name == "Q" else (name,):
            chains[other].finish()
        if name == "D":
            layout = [(0, i * width, width, i * width // PIECES, 0, 0, ff // PIECES) for i in range(ff // width)]
            layout.append((0, ff, w_proj.shape[1], 0, 1, 0, width // PIECES))
            shapes = [(ff, width), w_proj.shape]
            placed["D"] = put_in_place([chains["D"]], me, layout, shapes, "down_place")
        elif name == "U":
            layout = [(0, 0, ff, 0, 0, 0, width // PIECES)]
            placed["U"] = put_in_place([chains["U"]], me, layout, [(width, ff)], "up_place")
        else:
            span = width // PORTIONS
            layout = [
                (c, i * span, span, 0, 0, i * width + c * span, width // PIECES)
                for c in range(PORTIONS)
                for i in range(3)
            ]
            layout.append((0, width, width, 0, 1, 0, width // PIECES))
            shapes = [(width, 3 * width), (width, width)]
            own = [chains["Q%d" % j] for j in range(PORTIONS)]
            placed["Q"] = put_in_place(own, me, layout, shapes, "qkv_place")
        return placed[name][0]

    for event in " ".join(SCHEDULE).split():
        if event[0] == "+":
            name = event[1:]
            if chains[name].out is None:
                chains[name].start()
                flying[name] = chains[name].ready
        elif event[0] == "-":
            name = event[1:]
            if chains[name].out is None:
                chains[name].land(*([] if last is None else [last]))
                flying.pop(name, None)
                last = chains[name].ready
        elif event[0] == "=":
            last = finish(event[1:])
        elif event == "up":
            keep, send, din, dsum = up_grad(orders["U"], now(me), dbr, slp, w_down, ht)
            chains["U"] = Chain(keep, send, orders["U"], n)
            last = dsum
        elif event == "mid":
            dr1, dpr, dat, sums1 = mid_back(now(me), din, w_up, dr2, n1, i1, ln1_gain, w_out)
            last = sums1
        elif event[0] == "E":
            j = int(event[1])
            parts.append(attention_back(j, now(seg_lengths), packed, dat, attended, lse))
            last = parts[j][3]
        elif event[0] == "q":
            j = int(event[1])
            outer = [attended, dpr] if j == 0 else []
            name = "Q%d" % j
            keep, send = qkv_grad(orders[name], now(me), tokens, parts[j][:3], outer)
            chains[name] = Chain(keep, send, orders[name], n)
            last = send
        elif event == "vec":
            chains["V"] = Total(collect([x[3] for x in parts], dsum, sums1, sums2), n)
        elif event == "in":
            ds = [x[i] for i in range(3) for x in parts]
            d_tokens = input_grad(now(me), ds, w_qkv, dr1)
            last = d_tokens
    g_w_down, g_w_proj = placed["D"]
    g_w_up = placed["U"][0]
    g_w_qkv, g_w_out = placed["Q"]
    vector = chains["V"].finish()
    at = 5 + ff // width
    return (
        loss[0, 0:1], d_tokens, g_w_qkv, vector[0:2].reshape(-1), g_w_out, vector[2], vector[3],
        vector[4], g_w_up, vector[5:at].reshape(-1), g_w_down, vector[at], vector[at + 1],
        vector[at + 2], g_w_proj,
    )


def solution(mesh):
    whole_rows = P("dp", None)
    return jax.shard_map(
        body,
        mesh=mesh,
        in_specs=(whole_rows, whole_rows) + (P(),) * 15,
        out_specs=(P("dp"), whole_rows) + (P(),) * 13,
        check_vma=False,
    )
```

```python
import functools

import jax
import jax.numpy as jnp
from jax import lax
from jax.experimental import pallas as pl
from jax.experimental.pallas import tpu as pltpu
from jax.sharding import PartitionSpec as P

HEADS = 12
QLEN = 32
PLEN = 180
QB = 128
WIDTHS = (256, 384, 512, 768, 1024)
PIECES = 16
PORTIONS = 3
NEG = -1e30
LN_EPS = 1e-12
NORM_EPS = 1e-6
f32, bf16, i32 = jnp.float32, jnp.bfloat16, jnp.int32


def nn(a, b):
    return lax.dot_general(a, b, (((1,), (0,)), ((), ())), preferred_element_type=f32)


def nt(a, b):
    return lax.dot_general(a, b, (((1,), (1,)), ((), ())), preferred_element_type=f32)


def tn(a, b):
    return lax.dot_general(a, b, (((0,), (0,)), ((), ())), preferred_element_type=f32)


def params(mib=48):
    return pltpu.CompilerParams(vmem_limit_bytes=mib << 20)


def cost(flops, nbytes):
    return pl.CostEstimate(flops=0, bytes_accessed=0, transcendentals=0)


SMEM = pl.BlockSpec(memory_space=pltpu.SMEM)
VMEM = pl.BlockSpec(memory_space=pltpu.VMEM)


def whole(shape):
    return pl.BlockSpec(shape, lambda *g: (0,) * len(shape))


def held(shape):
    return pl.BlockSpec(shape, lambda *g: (0,) * len(shape), pipeline_mode=pl.Buffered(1))


def in_hbm(x):
    return pltpu.with_memory_space_constraint(x, pltpu.HBM)


def struct(shape, dtype):
    return jax.ShapeDtypeStruct(shape, dtype)


def row(v):
    return v[...].reshape(1, -1)


def normalize(resid):
    center = resid - jnp.mean(resid, axis=-1, keepdims=True)
    inv = lax.rsqrt(jnp.mean(center * center, axis=-1, keepdims=True) + LN_EPS)
    return center * inv, inv


def segment_ends(lens):
    ends = [lens[0, 0]]
    for s in range(1, lens.shape[1]):
        ends.append(ends[-1] + lens[0, s])
    return ends


def segment_of(ends, position):
    seg = jnp.zeros(position.shape, i32)
    for e in ends:
        seg = seg + (position >= e).astype(i32)
    return seg


def key_window(ends, rows, first):
    lo = jnp.zeros((), i32)
    hi = jnp.asarray(rows, i32)
    for e in ends:
        lo = jnp.where(e <= first, e, lo)
    for e in reversed(ends):
        hi = jnp.where(e >= first + QB, e, hi)
    lo = lax.div(lo, QB) * QB
    need = hi - lo
    cls = jnp.zeros((), i32)
    wide = jnp.asarray(WIDTHS[0], i32)
    for c, w in enumerate(WIDTHS[:-1]):
        if WIDTHS[c + 1] <= rows:
            cls = jnp.where(need > w, c + 1, cls)
            wide = jnp.where(need > w, WIDTHS[c + 1], wide)
    return pl.multiple_of(jnp.minimum(lo, rows - wide), QB), cls


def fill_segments(ends, segq, segk):
    segk[...] = segment_of(ends, lax.broadcasted_iota(i32, segk.shape, 0))
    at = lax.broadcasted_iota(i32, segq.shape, 0) * QB + lax.broadcasted_iota(i32, segq.shape, 1)
    segq[...] = segment_of(ends, at)


def two_heads(x, scale=None):
    lane = lax.broadcasted_iota(i32, x.shape, 1)
    zero = jnp.zeros_like(x)
    if scale is not None:
        x = x * scale
    return jnp.concatenate([jnp.where(lane < 64, x, zero), jnp.where(lane < 64, zero, x)], axis=0)


def pick_heads(t):
    return jnp.concatenate([t[:64, :QB], t[64:, QB:]], axis=0)


def attn_fwd_kernel(lens, *refs):
    count = 7
    given, (packed_out, out, lse, hid, low, ht, n1, i1) = refs[:count], refs[count : count + 8]
    vt, segq, segk, packed = refs[count + 8 : count + 12]
    tok, wqkv, bqv, wo, bo, g1, b1 = refs[count + 12 : count + 12 + count]
    sems, wsems, psems = refs[count + 12 + count :]
    rows, width = tok.shape
    cols = 3
    fetch = [
        pltpu.make_async_copy(given[i], x, sems.at[i])
        for i, x in ((0, tok), (2, bqv), (3, wo), (4, bo), (5, g1), (6, b1))
    ]
    chunk = [
        pltpu.make_async_copy(
            given[1].at[:, j * width : (j + 1) * width],
            wqkv.at[:, j * width : (j + 1) * width],
            wsems.at[j],
        )
        for j in range(cols)
    ]
    keep = [
        pltpu.make_async_copy(
            packed.at[:, j * width : (j + 1) * width],
            packed_out.at[:, j * width : (j + 1) * width],
            psems.at[j],
        )
        for j in range(cols)
    ]
    for f in fetch[:2]:
        f.start()
    for c in chunk:
        c.start()
    for f in fetch[2:]:
        f.start()
    ends = segment_ends(lens)
    fill_segments(ends, segq, segk)
    pairs = width // 128
    for f in fetch[:2]:
        f.wait()
    for j in range(cols):
        at = slice(j * width, (j + 1) * width)
        chunk[j].wait()
        for r in (slice(0, rows // 2), slice(rows // 2, rows)):
            x = nn(tok[r, :], wqkv[:, at])
            if j != 1:
                b0 = width if j else 0
                x = x + bqv[b0 : b0 + width].reshape(1, width)
            packed[r, at] = x.astype(bf16)
        keep[j].start()
    q = packed.at[:, 0:width]
    k = packed.at[:, width : 2 * width]
    v = packed.at[:, 2 * width : 3 * width]
    for g in range(pairs):
        vt[g] = v[:, g * 128 : (g + 1) * 128].T

    def step(i, carry):
        base = pl.multiple_of(i * QB, QB)
        k0, cls = key_window(ends, rows, base)
        sq = segq[pl.ds(i, 1), :]

        def body(w):
            same = segk[pl.ds(k0, w), :] == sq
            sts = []
            for g in range(pairs):
                sl = slice(g * 128, (g + 1) * 128)
                q2 = two_heads(q[pl.ds(base, QB), sl], jnp.asarray(0.125, bf16))
                sts.append(nt(k[pl.ds(k0, w), sl], q2))
            for g in range(pairs):
                sl = slice(g * 128, (g + 1) * 128)
                st = sts[g]
                ps, ms, ls = [], [], []
                for h in range(2):
                    s = jnp.where(same, st[:, h * QB : (h + 1) * QB], NEG)
                    m = jnp.max(s, axis=0, keepdims=True)
                    p = jnp.exp(s - m)
                    ls.append(jnp.sum(p, axis=0, keepdims=True))
                    ms.append(m)
                    ps.append(p.astype(bf16))
                total = jnp.concatenate(ls, 1)
                top = jnp.concatenate(ms, 1)
                ot = nn(vt[g, :, pl.ds(k0, w)], jnp.concatenate(ps, 1)) * (1.0 / total)
                out[pl.ds(base, QB), sl] = pick_heads(ot).T.astype(bf16)
                lse[g, pl.ds(i, 1), :] = top + jnp.log(total)

        for c, w in enumerate(WIDTHS):
            if w <= rows:
                pl.when(cls == c)(functools.partial(body, w))
        return carry

    lax.fori_loop(0, rows // QB, step, 0)
    for f in fetch[2:]:
        f.wait()
    tile = 256
    for r0 in range(0, rows, tile):
        r = slice(r0, r0 + tile)
        resid = tok[r, :].astype(f32) + (nn(out[r, :], wo[...]) + row(bo))
        normal, inv = normalize(resid)
        hidden = normal * row(g1) + row(b1)
        hid[r, :] = hidden
        hl = hidden.astype(bf16)
        low[r, :] = hl
        ht[:, r] = hl.T
        n1[r, :] = normal.astype(bf16)
        i1[r, :] = inv
    for k in keep:
        k.wait()


def attn_bwd_kernel(
    lens, q, k, v, do, o, lse, dq, dk, dv, sums, kt, dka, dva, segq, segk
):
    rows, span = q.shape
    ends = segment_ends(lens)
    fill_segments(ends, segq, segk)
    pairs = span // 128
    for g in range(pairs):
        kt[g] = k[:, g * 128 : (g + 1) * 128].T
    dka[...] = jnp.zeros_like(dka)
    dva[...] = jnp.zeros_like(dva)
    head = (
        lax.broadcasted_iota(i32, (8, 128), 0) == lax.broadcasted_iota(i32, (8, 128), 1) // 64
    ).astype(f32)

    def step(i, carry):
        base = pl.multiple_of(i * QB, QB)
        k0, cls = key_window(ends, rows, base)
        sq = segq[pl.ds(i, 1), :]

        def body(w):
            at = pl.ds(k0, w)
            same = segk[at, :] == sq
            for g in range(pairs):
                gs = slice(g * 128, (g + 1) * 128)
                q2 = two_heads(q[pl.ds(base, QB), gs], jnp.asarray(0.125, bf16))
                do_ = do[pl.ds(base, QB), gs]
                do2 = two_heads(do_)
                d8 = lax.dot_general(
                    head,
                    do_.astype(f32) * o[pl.ds(base, QB), gs].astype(f32),
                    (((1,), (1,)), ((), ())),
                    precision=lax.Precision.HIGHEST,
                    preferred_element_type=f32,
                )
                lrow = lse[g, pl.ds(i, 1), :]
                st = nt(k[at, gs], q2)
                dpt = nt(v[at, gs], do2)
                ps, ds = [], []
                for h in range(2):
                    sl = slice(h * QB, (h + 1) * QB)
                    p = jnp.exp(jnp.where(same, st[:, sl] - lrow[:, sl], NEG))
                    ps.append(p.astype(bf16))
                    ds.append((p * (dpt[:, sl] - d8[h : h + 1, :])).astype(bf16))
                p = jnp.concatenate(ps, 1)
                d = jnp.concatenate(ds, 1)
                dka[at, gs] += nn(d, q2)
                dva[at, gs] += nn(p, do2)
                dqt = nn(kt[g, :, pl.ds(k0, w)], d)
                dq[pl.ds(base, QB), gs] = (pick_heads(dqt).T * 0.125).astype(bf16)

        for c, w in enumerate(WIDTHS):
            if w <= rows:
                pl.when(cls == c)(functools.partial(body, w))
        return carry

    lax.fori_loop(0, rows // QB, step, 0)
    dk[...] = dka[...].astype(bf16)
    dvl = dva[...].astype(bf16)
    dv[...] = dvl
    sums[0:1, :] = jnp.sum(dq[...].astype(f32), axis=0, keepdims=True)
    sums[1:2, :] = jnp.sum(dvl.astype(f32), axis=0, keepdims=True)


def segment_scratch(rows):
    return [pltpu.VMEM((rows // QB, QB), i32), pltpu.VMEM((rows, 128), i32)]


def attention(lens, tok, wqkv, bqv, wo, bo, g1, b1):
    rows, width = tok.shape
    pairs = width // 128
    ins = [tok, wqkv, bqv, wo, bo, g1, b1]
    anywhere = pl.BlockSpec(memory_space=pl.ANY)
    return pl.pallas_call(
        attn_fwd_kernel,
        in_specs=[SMEM] + [anywhere] * len(ins),
        out_specs=[anywhere] + [VMEM] * 7,
        out_shape=[
            pltpu.HBM((rows, 3 * width), bf16),
            struct((rows, width), bf16),
            struct((pairs, rows // QB, 2 * QB), f32),
            struct((rows, width), f32),
            struct((rows, width), bf16),
            pltpu.HBM((width, rows), bf16),
            pltpu.HBM((rows, width), bf16),
            pltpu.HBM((rows, 1), f32),
        ],
        scratch_shapes=[pltpu.VMEM((pairs, 128, rows), bf16)]
        + segment_scratch(rows)
        + [pltpu.VMEM((rows, 3 * width), bf16)]
        + [pltpu.VMEM(x.shape, x.dtype) for x in ins]
        + [
            pltpu.SemaphoreType.DMA((len(ins),)),
            pltpu.SemaphoreType.DMA((3,)),
            pltpu.SemaphoreType.DMA((3,)),
        ],
        compiler_params=params(32),
        cost_estimate=cost(18e9, 8 * rows * width),
        name="attention_forward",
    )(lens, *[in_hbm(x) for x in ins])


def attention_back(part, lens, packed, do, o, lse):
    rows, width = packed.shape[0], packed.shape[1] // 3
    span = width // PORTIONS
    pairs = span // 128
    shp = struct((rows, span), bf16)
    col = lambda off: pl.BlockSpec((rows, span), lambda g, off=off: (0, off * PORTIONS + part))
    own = pl.BlockSpec((rows, span), lambda g: (0, 0))
    return pl.pallas_call(
        attn_bwd_kernel,
        grid=(1,),
        in_specs=[SMEM, col(0), col(1), col(2), col(0), col(0)]
        + [pl.BlockSpec((pairs,) + lse.shape[1:], lambda g: (part, 0, 0))],
        out_specs=[own, own, own, whole((8, span))],
        out_shape=[shp, shp, shp, struct((8, span), f32)],
        scratch_shapes=[
            pltpu.VMEM((pairs, 128, rows), bf16),
            pltpu.VMEM((rows, span), f32),
            pltpu.VMEM((rows, span), f32),
        ]
        + segment_scratch(rows),
        compiler_params=params(16),
        cost_estimate=cost(10e9, 16 * rows * span),
        name="attention_backward",
    )(lens, packed, packed, packed, do, o, lse)


def norm_back(grad, gain, normal, inv):
    dn = grad * gain
    return inv * (
        dn
        - jnp.mean(dn, axis=-1, keepdims=True)
        - normal * jnp.mean(dn * normal, axis=-1, keepdims=True)
    )


FF_CHUNK = 1024


def ffn_fwd_kernel(
    lens, hid, low, wu, bu, wd, bd, g2, b2, wp, act, slp, n2, i2, nl, emb, ul, msg, acc
):
    c = pl.program_id(0)
    rows = low.shape[0]
    span = hid.shape[1]
    tile = 256
    tiles = [slice(r, r + tile) for r in range(0, rows, tile)]

    @pl.when(c == 0)
    def _():
        for r in tiles:
            acc[r, :] = jnp.broadcast_to(row(bd), acc[r, :].shape)

    for r in tiles:
        inner = nn(low[r, :], wu[...]) + row(bu)
        cdf = 0.5 + 0.5 * lax.erf(inner * 0.7071067811865476)
        a = (inner * cdf).astype(bf16)
        act[r, :] = a
        slp[r, :] = (cdf + inner * (jnp.exp(inner * inner * -0.5) * 0.3989422804014327)).astype(bf16)
        acc[r, :] += nn(a, wd[...])
    at = pl.ds(pl.multiple_of(c * span, span), span)
    acc[:, at] += hid[...]

    @pl.when(c == pl.num_programs(0) - 1)
    def _():
        for r in tiles:
            normal, inv = normalize(acc[r, :])
            normed = (normal * row(g2) + row(b2)).astype(bf16)
            n2[r, :] = normal.astype(bf16)
            i2[r, :] = inv
            nl[r, :] = normed
            e = nn(normed, wp[...])
            emb[r, :] = e
            ul[r, :] = (
                e * lax.rsqrt(jnp.sum(e * e, axis=-1, keepdims=True) + NORM_EPS)
            ).astype(bf16)
        count = lens[0, 0]
        slot = lax.broadcasted_iota(i32, (QLEN, ul.shape[1]), 0)
        msg[0, 0:QLEN, :] = jnp.where(slot < count, ul[0:QLEN, :].astype(f32), 0.0).astype(bf16)
        msg[0, QLEN : QLEN + 16, :] = (
            jnp.full((16, ul.shape[1]), count, i32).astype(f32).astype(bf16)
        )


def ffn_fwd(lens, hid, low, wu, bu, wd, bd, g2, b2, wp):
    rows, width = hid.shape
    ff, out = wu.shape[1], wp.shape[1]
    steps = ff // FF_CHUNK
    ins = [lens, hid, low, in_hbm(wu), bu, in_hbm(wd), bd, g2, b2, wp]
    specs = [held(x.shape) for x in ins]
    specs[0] = SMEM
    specs[1] = pl.BlockSpec((rows, width // steps), lambda c: (0, c))
    specs[3] = pl.BlockSpec((width, FF_CHUNK), lambda c: (0, c))
    specs[4] = pl.BlockSpec((FF_CHUNK,), lambda c: (c,))
    specs[5] = pl.BlockSpec((FF_CHUNK, width), lambda c: (c, 0))
    outs = [
        pltpu.HBM((rows, ff), bf16),
        pltpu.HBM((rows, ff), bf16),
        pltpu.HBM((rows, width), bf16),
        struct((rows, 1), f32),
        pltpu.HBM((rows, width), bf16),
        struct((rows, out), f32),
        struct((rows, out), bf16),
        struct((1, QLEN + 16, out), bf16),
    ]
    ospecs = [whole(x.shape) for x in outs]
    ospecs[0] = ospecs[1] = pl.BlockSpec((rows, FF_CHUNK), lambda c: (0, c))
    return pl.pallas_call(
        ffn_fwd_kernel,
        grid=(steps,),
        in_specs=specs,
        out_specs=ospecs,
        out_shape=outs,
        scratch_shapes=[pltpu.VMEM((rows, width), f32)],
        compiler_params=params(32),
        cost_estimate=cost(18e9, 40e6),
        name="ffn_forward",
    )(*ins)


def relative(device, n):
    bits = n.bit_length() - 1
    at = jnp.zeros((), i32)
    for b in range(bits):
        at = at | (((device >> b) & 1) << (bits - 1 - b))
    return at


def loss_kernel(me, lens, owner, gathered, ul, msg, dpb):
    n, nump = owner.shape
    rows = ul.shape[0]
    total = nump * QLEN
    seg = segment_of(segment_ends(lens), lax.broadcasted_iota(i32, (1, rows), 1))
    rel = [relative(owner[me[0], p] ^ me[0], n) for p in range(nump)]
    qs = [gathered[rel[p], 0:QLEN, :] for p in range(nump)]
    q = jnp.concatenate(qs, axis=0)
    slot = lax.broadcasted_iota(i32, (QLEN, 1), 0).astype(f32)
    valid = jnp.concatenate(
        [
            (slot < gathered[rel[p], QLEN : QLEN + 16, :][0:1, 0:1].astype(f32)).astype(f32)
            for p in range(nump)
        ],
        axis=0,
    )
    group = lax.broadcasted_iota(i32, (total, rows), 0) // QLEN + 1
    x = jnp.where(group == seg, nt(q, ul[...]) * 10.0, NEG)
    top = jnp.max(x, axis=1, keepdims=True)
    e = jnp.exp(x - top)
    sm = jnp.sum(e, axis=1, keepdims=True)
    soft = valid * (0.1 * (top + jnp.log(sm)))
    lane = lax.broadcasted_iota(i32, (1, 128), 1)
    score = jnp.zeros((1, 128), f32)
    for p in range(nump):
        score = score + jnp.where(
            lane == p, jnp.sum(soft[p * QLEN : (p + 1) * QLEN], axis=0, keepdims=True), 0.0
        )
    w = e * (valid / sm)
    wh = w.astype(bf16)
    wl = (w - wh.astype(f32)).astype(bf16)
    msg[0, 0:total, :] = (nn(wh, ul[...]) + nn(wl, ul[...])).astype(bf16)
    hi = score.astype(bf16)
    rest = score - hi.astype(f32)
    mid = rest.astype(bf16)
    lo = (rest - mid.astype(f32)).astype(bf16)
    row = lax.broadcasted_iota(i32, (16, 128), 0)
    tail = jnp.where(row == 0, hi.astype(f32), 0.0)
    tail = tail + jnp.where(row == 1, mid.astype(f32), 0.0)
    tail = tail + jnp.where(row == 2, lo.astype(f32), 0.0)
    msg[0, total : total + 16, :] = tail.astype(bf16)
    dpb[...] = tn(wh, q) + tn(wl, q)


def loss_forward(me, lens, owner, gathered, ul):
    rows, out = ul.shape
    total = owner.shape[1] * QLEN
    smem = pl.BlockSpec(memory_space=pltpu.SMEM)
    vmem = pl.BlockSpec(memory_space=pltpu.VMEM)
    return pl.pallas_call(
        loss_kernel,
        in_specs=[smem] * 3 + [vmem] * 2,
        out_specs=[vmem] * 2,
        out_shape=[struct((1, total + 16, out), bf16), struct((rows, out), f32)],
        compiler_params=params(8),
        cost_estimate=cost(1e9, 2e6),
        name="loss_forward",
    )(me, lens, owner, gathered, ul)


def loss_back_kernel(
    me, lens, owner, place, messages, dpb, emb, nl, n2, i2, g2, wp,
    loss, dr2, dbr, gwp, sums, du, gwpt, inverse,
):
    n, nump = owner.shape
    groups = nump + 1
    rows, width = nl.shape
    total = nump * QLEN
    mine = me[0]

    def note(i, carry):
        for p in range(nump):
            inverse[owner[i, p] * nump + place[i, p]] = i * nump + p
        return carry

    lax.fori_loop(0, n, note, 0)
    group = [mine] + [owner[mine, p] for p in range(nump)]
    plc = [place[mine, p] for p in range(nump)]
    src, col = {}, {}
    for g in range(groups):
        for r in range(nump):
            entry = inverse[group[g] * nump + r]
            src[g, r] = relative(lax.div(entry, nump) ^ mine, n)
            col[g, r] = lax.rem(entry, nump)
    lane = lax.broadcasted_iota(i32, (8, 128), 1)
    sub = lax.broadcasted_iota(i32, (8, 128), 0)
    vals = []
    for r in range(nump):
        a = jnp.zeros((8, 128), f32)
        for g in range(groups):
            t = messages[src[g, r], total : total + 16, :].astype(f32)
            t = t[0:1, :] + t[1:2, :] + t[2:3, :]
            a = jnp.where((sub == g) & (lane == col[g, r]), t, a)
        vals.append(jnp.sum(a, axis=1, keepdims=True))
    top = vals[0]
    for v in vals[1:]:
        top = jnp.maximum(top, v)
    es = [jnp.exp(v - top) for v in vals]
    sm = es[0]
    for e in es[1:]:
        sm = sm + e
    loss[...] = jnp.broadcast_to((top + jnp.log(sm) - vals[0])[0:1], (8, 128))
    dt = [e / sm - (1.0 if r == 0 else 0.0) for r, e in enumerate(es)]
    sub1 = lax.broadcasted_iota(i32, (8, 1), 0)
    place = jnp.zeros((8, 1), i32)
    for p in range(nump):
        place = jnp.where(sub1 == p + 1, plc[p], place)
    dscore = jnp.zeros((8, 1), f32)
    for r in range(nump):
        dscore = jnp.where(place == r, dt[r], dscore)
    dmq = jnp.zeros((QLEN, 128), f32)
    for r in range(nump):
        at = pl.multiple_of(col[0, r] * QLEN, QLEN)
        dmq = dmq + dt[r][0:1] * messages[src[0, r], pl.ds(at, QLEN), :].astype(f32)
    sk = segment_of(segment_ends(lens), lax.broadcasted_iota(i32, (rows, 128), 0))
    scale = jnp.zeros(sk.shape, f32)
    for p in range(nump):
        scale = jnp.where(sk == p + 1, dscore[p + 1 : p + 2], scale)
    du[...] = scale * dpb[...]
    du[0:QLEN, :] = jnp.where(sk[0:QLEN] == 0, dmq, du[0:QLEN, :])

    gwpt[...] = jnp.zeros_like(gwpt)
    sums[...] = jnp.zeros_like(sums)
    tile = 256
    for r0 in range(0, rows, tile):
        r = slice(r0, r0 + tile)
        e = emb[r, :]
        inv = lax.rsqrt(jnp.sum(e * e, axis=-1, keepdims=True) + NORM_EPS)
        unit = e * inv
        d = du[r, :].astype(bf16).astype(f32)
        de = (inv * (d - unit * jnp.sum(unit * d, axis=-1, keepdims=True))).astype(bf16)
        gwpt[...] += tn(de, nl[r, :])
        dn = nt(de, wp[...])
        normal = n2[r, :].astype(f32)
        sums[0:1, :] += jnp.sum(dn * normal, axis=0, keepdims=True)
        sums[1:2, :] += jnp.sum(dn, axis=0, keepdims=True)
        dr = norm_back(dn, row(g2), normal, i2[r, :])
        dr2[r, :] = dr
        db = dr.astype(bf16)
        dbr[r, :] = db
        sums[2:3, :] += jnp.sum(db.astype(f32), axis=0, keepdims=True)
    gwp[...] = gwpt[...].T


def loss_back(me, lens, owner, place, messages, dpb, emb, nl, n2, i2, g2, wp):
    rows, width = nl.shape
    out = wp.shape[1]
    smem = pl.BlockSpec(memory_space=pltpu.SMEM)
    vmem = pl.BlockSpec(memory_space=pltpu.VMEM)
    return pl.pallas_call(
        loss_back_kernel,
        in_specs=[smem] * 4 + [vmem] * 8,
        out_specs=[vmem] * 5,
        out_shape=[
            struct((8, 128), f32),
            pltpu.HBM((rows, width), f32),
            struct((rows, width), bf16),
            struct((width, out), f32),
            struct((8, width), f32),
        ],
        scratch_shapes=[
            pltpu.VMEM((rows, out), f32),
            pltpu.VMEM((out, width), f32),
            pltpu.SMEM((owner.size,), i32),
        ],
        compiler_params=params(14),
        cost_estimate=cost(6e9, 10e6),
        name="loss_backward",
    )(me, lens, owner, place, messages, dpb, emb, nl, n2, i2, g2, wp)


def flip_of(device, dims):
    m = jnp.zeros((), i32)
    for i, d in enumerate(dims[:4]):
        m = m | jnp.where((device & d) != 0, 8 >> i, 0)
    return m


def sides(me, dims, keep, send):
    m = flip_of(me[0], dims)
    half = PIECES // 2
    top, low = lax.div(m, half), lax.rem(m, half)
    return [(keep, top, low), (send, 1 - top, low)]


DOWN_BATCH = 4


def down_grad_kernel(dims, me, act, dbr, gwp, keep, send):
    r = pl.program_id(0)
    pr, width = keep.shape[1], dbr.shape[1]
    parts = act.shape[1] // (DOWN_BATCH * pr)
    flip = flip_of(me[0], dims)
    low = flip & (DOWN_BATCH - 1)
    first = (r ^ lax.div(flip, DOWN_BATCH)) * DOWN_BATCH

    def put(dst):
        g = tn(act[...], dbr[...])
        for u in range(DOWN_BATCH):
            for i in range(parts):
                at = (u * parts + i) * pr
                dst[u ^ low, :, i * width : (i + 1) * width] = g[at : at + pr]
            at = pl.multiple_of((first + u) * pr, 16)
            dst[u ^ low, :, parts * width :] = gwp[pl.ds(at, pr), :]

    pl.when(r < PIECES // 2 // DOWN_BATCH)(lambda: put(keep))
    pl.when(r >= PIECES // 2 // DOWN_BATCH)(lambda: put(send))


def down_grad(dims, me, act, dbr, gwp):
    rows, width = dbr.shape
    ff = act.shape[1]
    cols = ff + gwp.shape[1]
    half = PIECES // 2 // DOWN_BATCH
    buf = struct((PIECES // 2, width // PIECES, cols), f32)
    block = (DOWN_BATCH, width // PIECES, cols)
    return pl.pallas_call(
        functools.partial(down_grad_kernel, dims),
        grid_spec=pltpu.PrefetchScalarGridSpec(
            num_scalar_prefetch=1,
            grid=(PIECES // DOWN_BATCH,),
            in_specs=[
                pl.BlockSpec(
                    (rows, DOWN_BATCH * ff // PIECES),
                    lambda r, f: (0, r ^ lax.div(flip_of(f[0], dims), DOWN_BATCH)),
                ),
                held(dbr.shape),
                held(gwp.shape),
            ],
            out_specs=[
                pl.BlockSpec(block, lambda r, f: (jnp.minimum(r, half - 1), 0, 0)),
                pl.BlockSpec(block, lambda r, f: (jnp.maximum(r - half, 0), 0, 0)),
            ],
        ),
        out_shape=[buf, buf],
        compiler_params=params(24),
        cost_estimate=cost(5e9, 17e6),
        name="down_gradient",
    )(me, in_hbm(act), dbr, gwp)


def up_grad_kernel(dims, me, dbr, slp, wd, ht, keep, send, din, dsum):
    pr = keep.shape[1]
    half = PIECES // 2
    rows = dbr.shape[0]
    tile = 256
    dsum[...] = jnp.zeros_like(dsum)
    for r0 in range(0, rows, tile):
        r = slice(r0, r0 + tile)
        d_inner = (nt(dbr[r, :], wd[...]) * slp[r, :].astype(f32)).astype(bf16)
        din[r, :] = d_inner
        dsum[...] += jnp.sum(d_inner.astype(f32), axis=0, keepdims=True)
    for dst, side, low in sides(me, dims, keep, send):
        at = pl.multiple_of(side * (half * pr), half * pr)
        g = nn(ht[pl.ds(at, half * pr), :], din[...])
        for t in range(half):
            dst[t ^ low] = g[t * pr : (t + 1) * pr]


def up_grad(dims, me, dbr, slp, wd, ht):
    rows, width = dbr.shape
    ff = slp.shape[1]
    half, pr = PIECES // 2, width // PIECES
    buf = struct((half, pr, ff), f32)
    part = pl.BlockSpec((half, pr, FF_CHUNK), lambda c: (0, 0, c))
    wide = pl.BlockSpec((rows, FF_CHUNK), lambda c: (0, c))
    return pl.pallas_call(
        functools.partial(up_grad_kernel, dims),
        grid=(ff // FF_CHUNK,),
        in_specs=[
            SMEM,
            held(dbr.shape),
            wide,
            pl.BlockSpec((FF_CHUNK, width), lambda c: (c, 0)),
            held(ht.shape),
        ],
        out_specs=[part, part, wide, pl.BlockSpec((1, FF_CHUNK), lambda c: (0, c))],
        out_shape=[buf, buf, pltpu.HBM((rows, ff), bf16), struct((1, ff), f32)],
        compiler_params=params(28),
        cost_estimate=cost(10e9, 30e6),
        name="up_gradient",
    )(me, dbr, in_hbm(slp), in_hbm(wd), ht)


def mid_back_kernel(me, din, wu, dr2, n1, i1, g1, wo, dr1, dpr, dat, sums, acc):
    c = pl.program_id(0)
    rows, width = dr1.shape
    span = dr2.shape[1]

    @pl.when(c == 0)
    def _():
        acc[...] = nt(din[...], wu[...])

    @pl.when(c > 0)
    def _():
        acc[...] += nt(din[...], wu[...])

    at = pl.ds(pl.multiple_of(c * span, span), span)
    acc[:, at] += dr2[...]

    @pl.when(c == pl.num_programs(0) - 1)
    def _():
        sums[...] = jnp.zeros_like(sums)
        tile = 256
        for r0 in range(0, rows, tile):
            r = slice(r0, r0 + tile)
            d = acc[r, :]
            normal = n1[r, :].astype(f32)
            sums[0:1, :] += jnp.sum(d * normal, axis=0, keepdims=True)
            sums[1:2, :] += jnp.sum(d, axis=0, keepdims=True)
            dr = norm_back(d, row(g1), normal, i1[r, :])
            dr1[r, :] = dr
            low = dr.astype(bf16)
            dpr[r, :] = low
            sums[2:3, :] += jnp.sum(low.astype(f32), axis=0, keepdims=True)
            dat[r, :] = nt(low, wo[...]).astype(bf16)


def mid_back(me, din, wu, dr2, n1, i1, g1, wo):
    rows, width = dr2.shape
    ff = din.shape[1]
    steps = ff // FF_CHUNK
    ins = [me, in_hbm(din), in_hbm(wu), dr2, n1, i1, g1, wo]
    specs = [held(x.shape) for x in ins]
    specs[0] = SMEM
    specs[1] = pl.BlockSpec((rows, FF_CHUNK), lambda c: (0, c))
    specs[2] = pl.BlockSpec((width, FF_CHUNK), lambda c: (0, c))
    specs[3] = pl.BlockSpec((rows, width // steps), lambda c: (0, c))
    outs = [
        struct((rows, width), f32),
        struct((rows, width), bf16),
        struct((rows, width), bf16),
        struct((8, width), f32),
    ]
    return pl.pallas_call(
        mid_back_kernel,
        grid=(steps,),
        in_specs=specs,
        out_specs=[whole(x.shape) for x in outs],
        out_shape=outs,
        scratch_shapes=[pltpu.VMEM((rows, width), f32)],
        compiler_params=params(32),
        cost_estimate=cost(9e9, 15e6),
        name="middle_backward",
    )(*ins)


def qkv_grad_kernel(dims, has_out, me, tok, d0, d1, d2, *rest):
    keep, send = rest[-2:]
    pairs = [(tok, d0), (tok, d1), (tok, d2)]
    if has_out:
        pairs.append(rest[:2])
    half = PIECES // 2
    pr = keep.shape[1]
    for dst, side, low in sides(me, dims, keep, send):
        at = pl.ds(pl.multiple_of(side * (half * pr), half * pr), half * pr)
        col = 0
        for left, d in pairs:
            g = tn(left[:, at], d[...])
            cols = d.shape[1]
            for t in range(half):
                dst[t ^ low, :, col : col + cols] = g[t * pr : (t + 1) * pr]
            col += cols


def qkv_grad(dims, me, tok, ds, outer):
    rows, width = tok.shape
    ins = [me, tok, *ds, *outer]
    cols = sum(d.shape[1] for d in ds) + (width if outer else 0)
    buf = struct((PIECES // 2, width // PIECES, cols), f32)
    return pl.pallas_call(
        functools.partial(qkv_grad_kernel, dims, bool(outer)),
        in_specs=[SMEM] + [VMEM] * (len(ins) - 1),
        out_specs=[VMEM] * 2,
        out_shape=[buf, buf],
        compiler_params=params(10),
        cost_estimate=cost(4e9, 8e6),
        name="qkv_gradient",
    )(*ins)


def input_grad_kernel(count, me, *refs):
    ds = refs[:count]
    w, dr1, out = refs[count:]
    tile = 256
    for r0 in range(0, out.shape[0], tile):
        r = slice(r0, r0 + tile)
        acc = dr1[r, :]
        for j, d in enumerate(ds):
            acc = acc + nt(d[r, :], w[:, j * 256 : (j + 1) * 256])
        out[r, :] = acc


def input_grad(me, ds, w, dr1):
    return pl.pallas_call(
        functools.partial(input_grad_kernel, len(ds)),
        in_specs=[SMEM] + [VMEM] * (len(ds) + 2),
        out_specs=VMEM,
        out_shape=struct(dr1.shape, f32),
        compiler_params=params(10),
        cost_estimate=cost(5e9, 15e6),
        name="input_gradient",
    )(me, *ds, w, dr1)


def collect_kernel(s0, s1, s2, dsum, sm1, sm2, out):
    width = out.shape[1]
    for j, s in enumerate((s0, s1, s2)):
        out[0:2, j * 256 : (j + 1) * 256] = s[0:2, :]
    out[2:3, :] = sm1[2:3, :]
    out[3:5, :] = sm1[0:2, :]
    end = 5
    for j in range(dsum.shape[1] // width):
        out[end : end + 1, :] = dsum[:, j * width : (j + 1) * width]
        end += 1
    out[end : end + 1, :] = sm2[2:3, :]
    out[end + 1 : end + 3, :] = sm2[0:2, :]
    out[end + 3 :, :] = jnp.zeros((out.shape[0] - end - 3, width), f32)


def collect(s, dsum, sm1, sm2):
    ins = [*s, dsum, sm1, sm2]
    return pl.pallas_call(
        collect_kernel,
        in_specs=[VMEM] * len(ins),
        out_specs=VMEM,
        out_shape=struct((16, sm1.shape[1]), f32),
        compiler_params=params(6),
        cost_estimate=cost(1e4, 1e5),
        name="collect_vectors",
    )(*ins)


def swap(x, mask, n):
    return lax.ppermute(x, "dp", [(i, i ^ mask) for i in range(n)])


def after(x, *others):
    return lax.optimization_barrier((x,) + others)[0]


def join(x, y):
    which = lax.broadcasted_iota(i32, (2,) + x.shape, 0)
    both = jnp.where(which == 0, x[None], y[None])
    return both.reshape((2 * x.shape[0],) + x.shape[1:])


class Chain:
    def __init__(self, keep, send, dims, n):
        self.keep, self.ready, self.dims, self.n = keep, send, dims, n
        self.at = 0
        self.out = None
        self.recv = None

    def start(self):
        k, dims = self.at, self.dims
        d = dims[k] if k < len(dims) else dims[3 - (k - len(dims))]
        self.recv = swap(self.ready, d, self.n)

    def land(self, *others):
        if self.recv is None:
            self.start()
        k, dims = self.at, self.dims
        self.at += 1
        recv = after(self.recv, *others) if others else self.recv
        self.recv = None
        if k < 4:
            recv = recv.astype(f32)
            half = self.keep.shape[0] // 2
            if k < 3:
                self.ready = (self.keep[half:] + recv[half:]).astype(bf16)
                self.keep = self.keep[:half] + recv[:half]
            else:
                self.ready = (self.keep + recv).astype(bf16)
        elif k < len(dims):
            self.ready = (self.ready.astype(f32) + recv.astype(f32)).astype(bf16)
        elif k == len(dims) + 3:
            self.out = (self.ready, recv)
        else:
            self.ready = join(self.ready, recv)

    def finish(self):
        while self.out is None:
            self.land()
        return self.out


class Total:
    def __init__(self, x, n):
        self.ready, self.n, self.at, self.recv, self.out = x, n, 0, None, None

    def start(self):
        self.recv = swap(self.ready, 1 << self.at, self.n)

    def land(self, *others):
        if self.recv is None:
            self.start()
        self.ready = self.ready + (after(self.recv, *others) if others else self.recv)
        self.recv = None
        self.at += 1
        if 1 << self.at == self.n:
            self.out = self.ready

    def finish(self):
        while self.out is None:
            self.land()
        return self.out


def gather_all(x, n):
    for b in reversed(range(n.bit_length() - 1)):
        x = join(x, swap(x, 1 << b, n))
    return x


BATCH = 8


def place_kernel(chains, layout, me, *refs):
    bufs, outs = refs[: 2 * len(chains)], refs[2 * len(chains) :]
    a = pl.program_id(0)
    here = PIECES // 2 // BATCH
    for i, dims in enumerate(chains):
        flip = flip_of(me[0], dims)
        low = flip & (BATCH - 1)
        group = a ^ lax.div(flip, BATCH)
        pr = bufs[2 * i].shape[1]

        def put(src, i=i, low=low, pr=pr):
            for t in range(BATCH):
                for which, col, cols, row0, out, out_col, out_rows in layout:
                    if which == i:
                        at = t * out_rows + row0
                        outs[out][at : at + pr, out_col : out_col + cols] = src[
                            t ^ low, :, col : col + cols
                        ].astype(f32)

        pl.when(group < here)(functools.partial(put, bufs[2 * i]))
        pl.when(group >= here)(functools.partial(put, bufs[2 * i + 1]))


def put_in_place(chains, me, layout, shapes, name):
    half = PIECES // 2 // BATCH
    ins, specs = [me], []

    def block(dims, second):
        def index(a, f):
            group = a ^ lax.div(flip_of(f[0], dims), BATCH)
            return (jnp.maximum(group - half, 0) if second else jnp.minimum(group, half - 1), 0, 0)

        return index

    for c in chains:
        for second, x in enumerate(c.out):
            ins.append(x)
            specs.append(pl.BlockSpec((BATCH,) + x.shape[1:], block(c.dims, second)))
    return pl.pallas_call(
        functools.partial(place_kernel, [c.dims for c in chains], layout),
        grid_spec=pltpu.PrefetchScalarGridSpec(
            num_scalar_prefetch=1,
            grid=(PIECES // BATCH,),
            in_specs=specs,
            out_specs=[
                pl.BlockSpec((r * BATCH // PIECES, w), lambda a, f: (a, 0)) for r, w in shapes
            ],
        ),
        out_shape=[struct(x, f32) for x in shapes],
        compiler_params=params(28),
        cost_estimate=cost(1e6, 6 * sum(x.size for x in ins)),
        name=name,
    )(*ins)


SCHEDULE = (
    "+D", "up", "+U", "-D", "+D", "mid", "-U", "+U", "E0", "-D", "+D", "q0", "+Q0", "E1", "-U",
    "+U", "-D", "+D", "-Q0", "+Q0", "q1", "+Q1", "E2", "-U", "+U", "-D", "+D", "-Q1", "+Q1", "q2",
    "+Q2", "-Q0", "+Q0", "vec", "+V", "-U", "+U", "-Q2", "+Q2", "-Q1", "+Q1", "-V", "+V", "in",
    "-D", "+D", "-Q0", "+Q0", "-Q2", "+Q2", "-Q1", "+Q1", "-V", "+V", "-Q0", "+Q0", "-U", "+U",
    "-Q2", "+Q2", "-V", "+V", "-D", "+D", "-Q1", "+Q1", "-U", "+U", "-Q0", "+Q0", "-Q2", "+Q2",
    "-V", "+V", "-Q1", "+Q1", "-D", "+D", "-Q2", "+Q2", "-U", "+U", "-Q0", "+Q0", "-Q1", "+Q1",
    "-Q2", "+Q2", "-V", "-Q1", "+Q1", "-Q2", "+Q2", "-D", "+D", "-U", "+U", "-D", "-Q0", "+Q0",
    "=D", "-Q1", "+Q1", "-U", "=U", "-Q2", "+Q2", "-Q1", "-Q0", "+Q0", "-Q2", "-Q0", "=Q",
)


def axis_orders(n):
    rest = [1 << i for i in range(1, n.bit_length() - 1)]
    if n == 32:
        x, y, z, far = rest
        return {
            "D": (1, x, y, z, far),
            "U": (1, z, x, y, far),
            "Q0": (1, z, x, y, far),
            "Q1": (1, x, y, z, far),
            "Q2": (1, x, y, z, far),
        }
    names = ("D", "U", "Q0", "Q1", "Q2")
    return {name: tuple([1] + rest[i:] + rest[:i]) for i, name in enumerate(names)}


def body(
    tokens, seg_lengths, owner, place, w_qkv, b_qv, w_out, b_out, ln1_gain, ln1_bias,
    w_up, b_up, w_down, b_down, ln2_gain, ln2_bias, w_proj,
):
    rows, width = tokens.shape
    ff = w_up.shape[1]
    n = lax.axis_size("dp")
    me = lax.axis_index("dp").astype(i32).reshape(1)
    orders = axis_orders(n)

    packed, attended, lse, hid, low, ht, n1, i1 = attention(
        seg_lengths, tokens, w_qkv, b_qv, w_out, b_out, ln1_gain, ln1_bias
    )
    act, slp, n2, i2, nl, emb, ul, query = ffn_fwd(
        seg_lengths, hid, low, w_up, b_up, w_down, b_down, ln2_gain, ln2_bias, w_proj
    )

    msg, dpb = loss_forward(me, seg_lengths, owner, gather_all(query, n), ul)
    loss, dr2, dbr, gwp, sums2 = loss_back(
        me, seg_lengths, owner, place, gather_all(msg, n), dpb, emb, nl, n2, i2, ln2_gain, w_proj
    )

    chains = {"D": Chain(*down_grad(orders["D"], me, act, dbr, gwp), orders["D"], n)}
    flying = {}
    parts = []
    placed = {}
    small = None
    last = None

    def vectors(v):
        end = 5 + ff // width
        return [v[0:2].reshape(-1), v[5:end].reshape(-1)] + [
            v[i] for i in (2, 3, 4, end, end + 1, end + 2)
        ]

    def now(x):
        return after(x, *flying.values()) if flying else x

    def finish(name):
        for other in ("Q0", "Q1", "Q2") if name == "Q" else (name,):
            chains[other].finish()
        if name == "D":
            layout = [(0, i * width, width, i * width // PIECES, 0, 0, ff // PIECES) for i in range(ff // width)]
            layout.append((0, ff, w_proj.shape[1], 0, 1, 0, width // PIECES))
            shapes = [(ff, width), w_proj.shape]
            placed["D"] = put_in_place([chains["D"]], me, layout, shapes, "down_place")
        elif name == "U":
            layout = [(0, 0, ff, 0, 0, 0, width // PIECES)]
            placed["U"] = put_in_place([chains["U"]], me, layout, [(width, ff)], "up_place")
        else:
            span = width // PORTIONS
            layout = [
                (c, i * span, span, 0, 0, i * width + c * span, width // PIECES)
                for c in range(PORTIONS)
                for i in range(3)
            ]
            layout.append((0, width, width, 0, 1, 0, width // PIECES))
            shapes = [(width, 3 * width), (width, width)]
            own = [chains["Q%d" % j] for j in range(PORTIONS)]
            placed["Q"] = put_in_place(own, me, layout, shapes, "qkv_place")
        return placed[name][0]

    for event in SCHEDULE:
        if event[0] == "+":
            name = event[1:]
            if chains[name].out is None:
                chains[name].start()
                flying[name] = chains[name].ready
        elif event[0] == "-":
            name = event[1:]
            if chains[name].out is None:
                chains[name].land(*([] if last is None else [last]))
                flying.pop(name, None)
                last = chains[name].ready
                if name == "V" and chains[name].out is not None:
                    small = vectors(chains[name].out)
                    last = small[1]
        elif event[0] == "=":
            last = finish(event[1:])
        elif event == "up":
            keep, send, din, dsum = up_grad(orders["U"], now(me), dbr, slp, w_down, ht)
            chains["U"] = Chain(keep, send, orders["U"], n)
            last = dsum
        elif event == "mid":
            dr1, dpr, dat, sums1 = mid_back(now(me), din, w_up, dr2, n1, i1, ln1_gain, w_out)
            last = sums1
        elif event[0] == "E":
            j = int(event[1])
            parts.append(attention_back(j, now(seg_lengths), packed, dat, attended, lse))
            last = parts[j][3]
        elif event[0] == "q":
            j = int(event[1])
            outer = [attended, dpr] if j == 0 else []
            name = "Q%d" % j
            keep, send = qkv_grad(orders[name], now(me), tokens, parts[j][:3], outer)
            chains[name] = Chain(keep, send, orders[name], n)
            last = send
        elif event == "vec":
            chains["V"] = Total(collect([x[3] for x in parts], dsum, sums1, sums2), n)
        elif event == "in":
            ds = [x[i] for i in range(3) for x in parts]
            d_tokens = input_grad(now(me), ds, w_qkv, dr1)
            last = d_tokens
    if small is None:
        small = vectors(chains["V"].finish())
    g_w_down, g_w_proj = placed["D"]
    g_w_up = placed["U"][0]
    g_w_qkv, g_w_out = placed["Q"]
    g_b_qv, g_b_up, g_b_out, g_ln1_gain, g_ln1_bias, g_b_down, g_ln2_gain, g_ln2_bias = small
    return (
        loss[0, 0:1], d_tokens, g_w_qkv, g_b_qv, g_w_out, g_b_out, g_ln1_gain, g_ln1_bias,
        g_w_up, g_b_up, g_w_down, g_b_down, g_ln2_gain, g_ln2_bias, g_w_proj,
    )


def solution(mesh):
    whole_rows = P("dp", None)
    return jax.shard_map(
        body,
        mesh=mesh,
        in_specs=(whole_rows, whole_rows) + (P(),) * 15,
        out_specs=(P("dp"), whole_rows) + (P(),) * 13,
        check_vma=False,
    )
```

```python
import functools

import jax
import jax.numpy as jnp
from jax import lax
from jax.experimental import pallas as pl
from jax.experimental.pallas import tpu as pltpu
from jax.sharding import PartitionSpec as P

HEADS = 12
QLEN = 32
PLEN = 180
QB = 128
WIDTHS = (256, 384, 512, 768, 1024)
PIECES = 16
PORTIONS = 3
NEG = -1e30
LN_EPS = 1e-12
NORM_EPS = 1e-6
f32, bf16, i32 = jnp.float32, jnp.bfloat16, jnp.int32


def nn(a, b):
    return lax.dot_general(a, b, (((1,), (0,)), ((), ())), preferred_element_type=f32)


def nt(a, b):
    return lax.dot_general(a, b, (((1,), (1,)), ((), ())), preferred_element_type=f32)


def tn(a, b):
    return lax.dot_general(a, b, (((0,), (0,)), ((), ())), preferred_element_type=f32)


def params(mib=48):
    return pltpu.CompilerParams(vmem_limit_bytes=mib << 20)


def cost(flops, nbytes):
    return pl.CostEstimate(flops=0, bytes_accessed=0, transcendentals=0)


SMEM = pl.BlockSpec(memory_space=pltpu.SMEM)
VMEM = pl.BlockSpec(memory_space=pltpu.VMEM)


def whole(shape):
    return pl.BlockSpec(shape, lambda *g: (0,) * len(shape))


def held(shape):
    return pl.BlockSpec(shape, lambda *g: (0,) * len(shape), pipeline_mode=pl.Buffered(1))


def in_hbm(x):
    return pltpu.with_memory_space_constraint(x, pltpu.HBM)


def struct(shape, dtype):
    return jax.ShapeDtypeStruct(shape, dtype)


def row(v):
    return v[...].reshape(1, -1)


def normalize(resid):
    center = resid - jnp.mean(resid, axis=-1, keepdims=True)
    inv = lax.rsqrt(jnp.mean(center * center, axis=-1, keepdims=True) + LN_EPS)
    return center * inv, inv


def segment_ends(lens):
    ends = [lens[0, 0]]
    for s in range(1, lens.shape[1]):
        ends.append(ends[-1] + lens[0, s])
    return ends


def segment_of(ends, position):
    seg = jnp.zeros(position.shape, i32)
    for e in ends:
        seg = seg + (position >= e).astype(i32)
    return seg


def key_window(ends, rows, first):
    lo = jnp.zeros((), i32)
    hi = jnp.asarray(rows, i32)
    for e in ends:
        lo = jnp.where(e <= first, e, lo)
    for e in reversed(ends):
        hi = jnp.where(e >= first + QB, e, hi)
    lo = lax.div(lo, QB) * QB
    need = hi - lo
    cls = jnp.zeros((), i32)
    wide = jnp.asarray(WIDTHS[0], i32)
    for c, w in enumerate(WIDTHS[:-1]):
        if WIDTHS[c + 1] <= rows:
            cls = jnp.where(need > w, c + 1, cls)
            wide = jnp.where(need > w, WIDTHS[c + 1], wide)
    return pl.multiple_of(jnp.minimum(lo, rows - wide), QB), cls


def fill_segments(ends, segq, segk):
    segk[...] = segment_of(ends, lax.broadcasted_iota(i32, segk.shape, 0))
    at = lax.broadcasted_iota(i32, segq.shape, 0) * QB + lax.broadcasted_iota(i32, segq.shape, 1)
    segq[...] = segment_of(ends, at)


def two_heads(x, scale=None):
    lane = lax.broadcasted_iota(i32, x.shape, 1)
    zero = jnp.zeros_like(x)
    if scale is not None:
        x = x * scale
    return jnp.concatenate([jnp.where(lane < 64, x, zero), jnp.where(lane < 64, zero, x)], axis=0)


def pick_heads(t):
    return jnp.concatenate([t[:64, :QB], t[64:, QB:]], axis=0)


def attn_fwd_kernel(lens, *refs):
    count = 7
    given, (packed_out, out, lse, hid, low, ht, n1, i1) = refs[:count], refs[count : count + 8]
    vt, segq, segk, packed = refs[count + 8 : count + 12]
    tok, wqkv, bqv, wo, bo, g1, b1 = refs[count + 12 : count + 12 + count]
    sems, wsems, psems = refs[count + 12 + count :]
    rows, width = tok.shape
    cols = 3
    fetch = [
        pltpu.make_async_copy(given[i], x, sems.at[i])
        for i, x in ((0, tok), (2, bqv), (3, wo), (4, bo), (5, g1), (6, b1))
    ]
    chunk = [
        pltpu.make_async_copy(
            given[1].at[:, j * width : (j + 1) * width],
            wqkv.at[:, j * width : (j + 1) * width],
            wsems.at[j],
        )
        for j in range(cols)
    ]
    keep = [
        pltpu.make_async_copy(
            packed.at[:, j * width : (j + 1) * width],
            packed_out.at[:, j * width : (j + 1) * width],
            psems.at[j],
        )
        for j in range(cols)
    ]
    for f in fetch[:2]:
        f.start()
    for c in chunk:
        c.start()
    for f in fetch[2:]:
        f.start()
    ends = segment_ends(lens)
    fill_segments(ends, segq, segk)
    pairs = width // 128
    for f in fetch[:2]:
        f.wait()
    for j in range(cols):
        at = slice(j * width, (j + 1) * width)
        chunk[j].wait()
        for r in (slice(0, rows // 2), slice(rows // 2, rows)):
            x = nn(tok[r, :], wqkv[:, at])
            if j != 1:
                b0 = width if j else 0
                x = x + bqv[b0 : b0 + width].reshape(1, width)
            packed[r, at] = x.astype(bf16)
        keep[j].start()
    q = packed.at[:, 0:width]
    k = packed.at[:, width : 2 * width]
    v = packed.at[:, 2 * width : 3 * width]
    for g in range(pairs):
        vt[g] = v[:, g * 128 : (g + 1) * 128].T

    def step(i, carry):
        base = pl.multiple_of(i * QB, QB)
        k0, cls = key_window(ends, rows, base)
        sq = segq[pl.ds(i, 1), :]

        def body(w):
            same = segk[pl.ds(k0, w), :] == sq
            sts = []
            for g in range(pairs):
                sl = slice(g * 128, (g + 1) * 128)
                q2 = two_heads(q[pl.ds(base, QB), sl], jnp.asarray(0.125, bf16))
                sts.append(nt(k[pl.ds(k0, w), sl], q2))
            for g in range(pairs):
                sl = slice(g * 128, (g + 1) * 128)
                st = sts[g]
                ps, ms, ls = [], [], []
                for h in range(2):
                    s = jnp.where(same, st[:, h * QB : (h + 1) * QB], NEG)
                    m = jnp.max(s, axis=0, keepdims=True)
                    p = jnp.exp(s - m)
                    ls.append(jnp.sum(p, axis=0, keepdims=True))
                    ms.append(m)
                    ps.append(p.astype(bf16))
                total = jnp.concatenate(ls, 1)
                top = jnp.concatenate(ms, 1)
                ot = nn(vt[g, :, pl.ds(k0, w)], jnp.concatenate(ps, 1)) * (1.0 / total)
                out[pl.ds(base, QB), sl] = pick_heads(ot).T.astype(bf16)
                lse[g, pl.ds(i, 1), :] = top + jnp.log(total)

        for c, w in enumerate(WIDTHS):
            if w <= rows:
                pl.when(cls == c)(functools.partial(body, w))
        return carry

    lax.fori_loop(0, rows // QB, step, 0)
    for f in fetch[2:]:
        f.wait()
    tile = 256
    for r0 in range(0, rows, tile):
        r = slice(r0, r0 + tile)
        resid = tok[r, :].astype(f32) + (nn(out[r, :], wo[...]) + row(bo))
        normal, inv = normalize(resid)
        hidden = normal * row(g1) + row(b1)
        hid[r, :] = hidden
        hl = hidden.astype(bf16)
        low[r, :] = hl
        ht[:, r] = hl.T
        n1[r, :] = normal.astype(bf16)
        i1[r, :] = inv
    for k in keep:
        k.wait()


def attn_bwd_kernel(
    lens, q, k, v, do, o, lse, dq, dk, dv, sums, kt, dka, dva, segq, segk
):
    rows, span = q.shape
    ends = segment_ends(lens)
    fill_segments(ends, segq, segk)
    pairs = span // 128
    for g in range(pairs):
        kt[g] = k[:, g * 128 : (g + 1) * 128].T
    dka[...] = jnp.zeros_like(dka)
    dva[...] = jnp.zeros_like(dva)
    head = (
        lax.broadcasted_iota(i32, (8, 128), 0) == lax.broadcasted_iota(i32, (8, 128), 1) // 64
    ).astype(f32)

    def step(i, carry):
        base = pl.multiple_of(i * QB, QB)
        k0, cls = key_window(ends, rows, base)
        sq = segq[pl.ds(i, 1), :]

        def body(w):
            at = pl.ds(k0, w)
            same = segk[at, :] == sq
            for g in range(pairs):
                gs = slice(g * 128, (g + 1) * 128)
                q2 = two_heads(q[pl.ds(base, QB), gs], jnp.asarray(0.125, bf16))
                do_ = do[pl.ds(base, QB), gs]
                do2 = two_heads(do_)
                d8 = lax.dot_general(
                    head,
                    do_.astype(f32) * o[pl.ds(base, QB), gs].astype(f32),
                    (((1,), (1,)), ((), ())),
                    precision=lax.Precision.HIGHEST,
                    preferred_element_type=f32,
                )
                lrow = lse[g, pl.ds(i, 1), :]
                st = nt(k[at, gs], q2)
                dpt = nt(v[at, gs], do2)
                ps, ds = [], []
                for h in range(2):
                    sl = slice(h * QB, (h + 1) * QB)
                    p = jnp.exp(jnp.where(same, st[:, sl] - lrow[:, sl], NEG))
                    ps.append(p.astype(bf16))
                    ds.append((p * (dpt[:, sl] - d8[h : h + 1, :])).astype(bf16))
                p = jnp.concatenate(ps, 1)
                d = jnp.concatenate(ds, 1)
                dka[at, gs] += nn(d, q2)
                dva[at, gs] += nn(p, do2)
                dqt = nn(kt[g, :, pl.ds(k0, w)], d)
                dq[pl.ds(base, QB), gs] = (pick_heads(dqt).T * 0.125).astype(bf16)

        for c, w in enumerate(WIDTHS):
            if w <= rows:
                pl.when(cls == c)(functools.partial(body, w))
        return carry

    lax.fori_loop(0, rows // QB, step, 0)
    dk[...] = dka[...].astype(bf16)
    dvl = dva[...].astype(bf16)
    dv[...] = dvl
    sums[0:1, :] = jnp.sum(dq[...].astype(f32), axis=0, keepdims=True)
    sums[1:2, :] = jnp.sum(dvl.astype(f32), axis=0, keepdims=True)


def segment_scratch(rows):
    return [pltpu.VMEM((rows // QB, QB), i32), pltpu.VMEM((rows, 128), i32)]


def attention(lens, tok, wqkv, bqv, wo, bo, g1, b1):
    rows, width = tok.shape
    pairs = width // 128
    ins = [tok, wqkv, bqv, wo, bo, g1, b1]
    anywhere = pl.BlockSpec(memory_space=pl.ANY)
    return pl.pallas_call(
        attn_fwd_kernel,
        in_specs=[SMEM] + [anywhere] * len(ins),
        out_specs=[anywhere] + [VMEM] * 7,
        out_shape=[
            pltpu.HBM((rows, 3 * width), bf16),
            struct((rows, width), bf16),
            struct((pairs, rows // QB, 2 * QB), f32),
            struct((rows, width), f32),
            struct((rows, width), bf16),
            pltpu.HBM((width, rows), bf16),
            pltpu.HBM((rows, width), bf16),
            pltpu.HBM((rows, 1), f32),
        ],
        scratch_shapes=[pltpu.VMEM((pairs, 128, rows), bf16)]
        + segment_scratch(rows)
        + [pltpu.VMEM((rows, 3 * width), bf16)]
        + [pltpu.VMEM(x.shape, x.dtype) for x in ins]
        + [
            pltpu.SemaphoreType.DMA((len(ins),)),
            pltpu.SemaphoreType.DMA((3,)),
            pltpu.SemaphoreType.DMA((3,)),
        ],
        compiler_params=params(32),
        cost_estimate=cost(18e9, 8 * rows * width),
        name="attention_forward",
    )(lens, *[in_hbm(x) for x in ins])


def attention_back(part, lens, packed, do, o, lse):
    rows, width = packed.shape[0], packed.shape[1] // 3
    span = width // PORTIONS
    pairs = span // 128
    shp = struct((rows, span), bf16)
    col = lambda off: pl.BlockSpec((rows, span), lambda g, off=off: (0, off * PORTIONS + part))
    own = pl.BlockSpec((rows, span), lambda g: (0, 0))
    return pl.pallas_call(
        attn_bwd_kernel,
        grid=(1,),
        in_specs=[SMEM, col(0), col(1), col(2), col(0), col(0)]
        + [pl.BlockSpec((pairs,) + lse.shape[1:], lambda g: (part, 0, 0))],
        out_specs=[own, own, own, whole((8, span))],
        out_shape=[shp, shp, shp, struct((8, span), f32)],
        scratch_shapes=[
            pltpu.VMEM((pairs, 128, rows), bf16),
            pltpu.VMEM((rows, span), f32),
            pltpu.VMEM((rows, span), f32),
        ]
        + segment_scratch(rows),
        compiler_params=params(16),
        cost_estimate=cost(10e9, 16 * rows * span),
        name="attention_backward",
    )(lens, packed, packed, packed, do, o, lse)


def norm_back(grad, gain, normal, inv):
    dn = grad * gain
    return inv * (
        dn
        - jnp.mean(dn, axis=-1, keepdims=True)
        - normal * jnp.mean(dn * normal, axis=-1, keepdims=True)
    )


FF_CHUNK = 1024


def ffn_fwd_kernel(
    lens, hid, low, wu, bu, wd, bd, g2, b2, wp, act, slp, n2, i2, nl, emb, ul, msg, acc
):
    c = pl.program_id(0)
    rows = low.shape[0]
    span = hid.shape[1]
    tile = 256
    tiles = [slice(r, r + tile) for r in range(0, rows, tile)]

    @pl.when(c == 0)
    def _():
        for r in tiles:
            acc[r, :] = jnp.broadcast_to(row(bd), acc[r, :].shape)

    for r in tiles:
        inner = nn(low[r, :], wu[...]) + row(bu)
        cdf = 0.5 + 0.5 * lax.erf(inner * 0.7071067811865476)
        a = (inner * cdf).astype(bf16)
        act[r, :] = a
        slp[r, :] = (cdf + inner * (jnp.exp(inner * inner * -0.5) * 0.3989422804014327)).astype(bf16)
        acc[r, :] += nn(a, wd[...])
    at = pl.ds(pl.multiple_of(c * span, span), span)
    acc[:, at] += hid[...]

    @pl.when(c == pl.num_programs(0) - 1)
    def _():
        for r in tiles:
            normal, inv = normalize(acc[r, :])
            normed = (normal * row(g2) + row(b2)).astype(bf16)
            n2[r, :] = normal.astype(bf16)
            i2[r, :] = inv
            nl[r, :] = normed
            e = nn(normed, wp[...])
            emb[r, :] = e
            ul[r, :] = (
                e * lax.rsqrt(jnp.sum(e * e, axis=-1, keepdims=True) + NORM_EPS)
            ).astype(bf16)
        count = lens[0, 0]
        slot = lax.broadcasted_iota(i32, (QLEN, ul.shape[1]), 0)
        msg[0, 0:QLEN, :] = jnp.where(slot < count, ul[0:QLEN, :].astype(f32), 0.0).astype(bf16)
        msg[0, QLEN : QLEN + 16, :] = (
            jnp.full((16, ul.shape[1]), count, i32).astype(f32).astype(bf16)
        )


def ffn_fwd(lens, hid, low, wu, bu, wd, bd, g2, b2, wp):
    rows, width = hid.shape
    ff, out = wu.shape[1], wp.shape[1]
    steps = ff // FF_CHUNK
    ins = [lens, hid, low, in_hbm(wu), bu, in_hbm(wd), bd, g2, b2, wp]
    specs = [held(x.shape) for x in ins]
    specs[0] = SMEM
    specs[1] = pl.BlockSpec((rows, width // steps), lambda c: (0, c))
    specs[3] = pl.BlockSpec((width, FF_CHUNK), lambda c: (0, c))
    specs[4] = pl.BlockSpec((FF_CHUNK,), lambda c: (c,))
    specs[5] = pl.BlockSpec((FF_CHUNK, width), lambda c: (c, 0))
    outs = [
        pltpu.HBM((rows, ff), bf16),
        pltpu.HBM((rows, ff), bf16),
        pltpu.HBM((rows, width), bf16),
        struct((rows, 1), f32),
        pltpu.HBM((rows, width), bf16),
        struct((rows, out), f32),
        struct((rows, out), bf16),
        struct((1, QLEN + 16, out), bf16),
    ]
    ospecs = [whole(x.shape) for x in outs]
    ospecs[0] = ospecs[1] = pl.BlockSpec((rows, FF_CHUNK), lambda c: (0, c))
    return pl.pallas_call(
        ffn_fwd_kernel,
        grid=(steps,),
        in_specs=specs,
        out_specs=ospecs,
        out_shape=outs,
        scratch_shapes=[pltpu.VMEM((rows, width), f32)],
        compiler_params=params(32),
        cost_estimate=cost(18e9, 40e6),
        name="ffn_forward",
    )(*ins)


def relative(device, n):
    bits = n.bit_length() - 1
    at = jnp.zeros((), i32)
    for b in range(bits):
        at = at | (((device >> b) & 1) << (bits - 1 - b))
    return at


def loss_kernel(me, lens, owner, gathered, ul, msg, dpb):
    n, nump = owner.shape
    rows = ul.shape[0]
    total = nump * QLEN
    seg = segment_of(segment_ends(lens), lax.broadcasted_iota(i32, (1, rows), 1))
    rel = [relative(owner[me[0], p] ^ me[0], n) for p in range(nump)]
    qs = [gathered[rel[p], 0:QLEN, :] for p in range(nump)]
    q = jnp.concatenate(qs, axis=0)
    slot = lax.broadcasted_iota(i32, (QLEN, 1), 0).astype(f32)
    valid = jnp.concatenate(
        [
            (slot < gathered[rel[p], QLEN : QLEN + 16, :][0:1, 0:1].astype(f32)).astype(f32)
            for p in range(nump)
        ],
        axis=0,
    )
    group = lax.broadcasted_iota(i32, (total, rows), 0) // QLEN + 1
    x = jnp.where(group == seg, nt(q, ul[...]) * 10.0, NEG)
    top = jnp.max(x, axis=1, keepdims=True)
    e = jnp.exp(x - top)
    sm = jnp.sum(e, axis=1, keepdims=True)
    soft = valid * (0.1 * (top + jnp.log(sm)))
    lane = lax.broadcasted_iota(i32, (1, 128), 1)
    score = jnp.zeros((1, 128), f32)
    for p in range(nump):
        score = score + jnp.where(
            lane == p, jnp.sum(soft[p * QLEN : (p + 1) * QLEN], axis=0, keepdims=True), 0.0
        )
    w = e * (valid / sm)
    wh = w.astype(bf16)
    wl = (w - wh.astype(f32)).astype(bf16)
    msg[0, 0:total, :] = (nn(wh, ul[...]) + nn(wl, ul[...])).astype(bf16)
    hi = score.astype(bf16)
    rest = score - hi.astype(f32)
    mid = rest.astype(bf16)
    lo = (rest - mid.astype(f32)).astype(bf16)
    row = lax.broadcasted_iota(i32, (16, 128), 0)
    tail = jnp.where(row == 0, hi.astype(f32), 0.0)
    tail = tail + jnp.where(row == 1, mid.astype(f32), 0.0)
    tail = tail + jnp.where(row == 2, lo.astype(f32), 0.0)
    msg[0, total : total + 16, :] = tail.astype(bf16)
    dpb[...] = tn(wh, q) + tn(wl, q)


def loss_forward(me, lens, owner, gathered, ul):
    rows, out = ul.shape
    total = owner.shape[1] * QLEN
    smem = pl.BlockSpec(memory_space=pltpu.SMEM)
    vmem = pl.BlockSpec(memory_space=pltpu.VMEM)
    return pl.pallas_call(
        loss_kernel,
        in_specs=[smem] * 3 + [vmem] * 2,
        out_specs=[vmem] * 2,
        out_shape=[struct((1, total + 16, out), bf16), struct((rows, out), f32)],
        compiler_params=params(8),
        cost_estimate=cost(1e9, 2e6),
        name="loss_forward",
    )(me, lens, owner, gathered, ul)


def loss_back_kernel(
    me, lens, owner, place, messages, dpb, emb, nl, n2, i2, g2, wp,
    loss, dr2, dbr, gwp, sums, du, gwpt, inverse,
):
    n, nump = owner.shape
    groups = nump + 1
    rows, width = nl.shape
    total = nump * QLEN
    mine = me[0]

    def note(i, carry):
        for p in range(nump):
            inverse[owner[i, p] * nump + place[i, p]] = i * nump + p
        return carry

    lax.fori_loop(0, n, note, 0)
    group = [mine] + [owner[mine, p] for p in range(nump)]
    plc = [place[mine, p] for p in range(nump)]
    src, col = {}, {}
    for g in range(groups):
        for r in range(nump):
            entry = inverse[group[g] * nump + r]
            src[g, r] = relative(lax.div(entry, nump) ^ mine, n)
            col[g, r] = lax.rem(entry, nump)
    lane = lax.broadcasted_iota(i32, (8, 128), 1)
    sub = lax.broadcasted_iota(i32, (8, 128), 0)
    vals = []
    for r in range(nump):
        a = jnp.zeros((8, 128), f32)
        for g in range(groups):
            t = messages[src[g, r], total : total + 16, :].astype(f32)
            t = t[0:1, :] + t[1:2, :] + t[2:3, :]
            a = jnp.where((sub == g) & (lane == col[g, r]), t, a)
        vals.append(jnp.sum(a, axis=1, keepdims=True))
    top = vals[0]
    for v in vals[1:]:
        top = jnp.maximum(top, v)
    es = [jnp.exp(v - top) for v in vals]
    sm = es[0]
    for e in es[1:]:
        sm = sm + e
    loss[...] = jnp.broadcast_to((top + jnp.log(sm) - vals[0])[0:1], (8, 128))
    dt = [e / sm - (1.0 if r == 0 else 0.0) for r, e in enumerate(es)]
    sub1 = lax.broadcasted_iota(i32, (8, 1), 0)
    place = jnp.zeros((8, 1), i32)
    for p in range(nump):
        place = jnp.where(sub1 == p + 1, plc[p], place)
    dscore = jnp.zeros((8, 1), f32)
    for r in range(nump):
        dscore = jnp.where(place == r, dt[r], dscore)
    dmq = jnp.zeros((QLEN, 128), f32)
    for r in range(nump):
        at = pl.multiple_of(col[0, r] * QLEN, QLEN)
        dmq = dmq + dt[r][0:1] * messages[src[0, r], pl.ds(at, QLEN), :].astype(f32)
    sk = segment_of(segment_ends(lens), lax.broadcasted_iota(i32, (rows, 128), 0))
    scale = jnp.zeros(sk.shape, f32)
    for p in range(nump):
        scale = jnp.where(sk == p + 1, dscore[p + 1 : p + 2], scale)
    du[...] = scale * dpb[...]
    du[0:QLEN, :] = jnp.where(sk[0:QLEN] == 0, dmq, du[0:QLEN, :])

    gwpt[...] = jnp.zeros_like(gwpt)
    sums[...] = jnp.zeros_like(sums)
    tile = 256
    for r0 in range(0, rows, tile):
        r = slice(r0, r0 + tile)
        e = emb[r, :]
        inv = lax.rsqrt(jnp.sum(e * e, axis=-1, keepdims=True) + NORM_EPS)
        unit = e * inv
        d = du[r, :].astype(bf16).astype(f32)
        de = (inv * (d - unit * jnp.sum(unit * d, axis=-1, keepdims=True))).astype(bf16)
        gwpt[...] += tn(de, nl[r, :])
        dn = nt(de, wp[...])
        normal = n2[r, :].astype(f32)
        sums[0:1, :] += jnp.sum(dn * normal, axis=0, keepdims=True)
        sums[1:2, :] += jnp.sum(dn, axis=0, keepdims=True)
        dr = norm_back(dn, row(g2), normal, i2[r, :])
        dr2[r, :] = dr
        db = dr.astype(bf16)
        dbr[r, :] = db
        sums[2:3, :] += jnp.sum(db.astype(f32), axis=0, keepdims=True)
    gwp[...] = gwpt[...].T


def loss_back(me, lens, owner, place, messages, dpb, emb, nl, n2, i2, g2, wp):
    rows, width = nl.shape
    out = wp.shape[1]
    smem = pl.BlockSpec(memory_space=pltpu.SMEM)
    vmem = pl.BlockSpec(memory_space=pltpu.VMEM)
    return pl.pallas_call(
        loss_back_kernel,
        in_specs=[smem] * 4 + [vmem] * 8,
        out_specs=[vmem] * 5,
        out_shape=[
            struct((8, 128), f32),
            pltpu.HBM((rows, width), f32),
            struct((rows, width), bf16),
            struct((width, out), f32),
            struct((8, width), f32),
        ],
        scratch_shapes=[
            pltpu.VMEM((rows, out), f32),
            pltpu.VMEM((out, width), f32),
            pltpu.SMEM((owner.size,), i32),
        ],
        compiler_params=params(14),
        cost_estimate=cost(6e9, 10e6),
        name="loss_backward",
    )(me, lens, owner, place, messages, dpb, emb, nl, n2, i2, g2, wp)


def flip_of(device, dims):
    m = jnp.zeros((), i32)
    for i, d in enumerate(dims[:4]):
        m = m | jnp.where((device & d) != 0, 8 >> i, 0)
    return m


def sides(me, dims, keep, send):
    m = flip_of(me[0], dims)
    half = PIECES // 2
    top, low = lax.div(m, half), lax.rem(m, half)
    return [(keep, top, low), (send, 1 - top, low)]


DOWN_BATCH = 4


def down_grad_kernel(dims, me, act, dbr, gwp, keep, send):
    r = pl.program_id(0)
    pr, width = keep.shape[1], dbr.shape[1]
    parts = act.shape[1] // (DOWN_BATCH * pr)
    flip = flip_of(me[0], dims)
    low = flip & (DOWN_BATCH - 1)
    first = (r ^ lax.div(flip, DOWN_BATCH)) * DOWN_BATCH

    def put(dst):
        g = tn(act[...], dbr[...])
        for u in range(DOWN_BATCH):
            for i in range(parts):
                at = (u * parts + i) * pr
                dst[u ^ low, :, i * width : (i + 1) * width] = g[at : at + pr]
            at = pl.multiple_of((first + u) * pr, 16)
            dst[u ^ low, :, parts * width :] = gwp[pl.ds(at, pr), :]

    pl.when(r < PIECES // 2 // DOWN_BATCH)(lambda: put(keep))
    pl.when(r >= PIECES // 2 // DOWN_BATCH)(lambda: put(send))


def down_grad(dims, me, act, dbr, gwp):
    rows, width = dbr.shape
    ff = act.shape[1]
    cols = ff + gwp.shape[1]
    half = PIECES // 2 // DOWN_BATCH
    buf = struct((PIECES // 2, width // PIECES, cols), f32)
    block = (DOWN_BATCH, width // PIECES, cols)
    return pl.pallas_call(
        functools.partial(down_grad_kernel, dims),
        grid_spec=pltpu.PrefetchScalarGridSpec(
            num_scalar_prefetch=1,
            grid=(PIECES // DOWN_BATCH,),
            in_specs=[
                pl.BlockSpec(
                    (rows, DOWN_BATCH * ff // PIECES),
                    lambda r, f: (0, r ^ lax.div(flip_of(f[0], dims), DOWN_BATCH)),
                ),
                held(dbr.shape),
                held(gwp.shape),
            ],
            out_specs=[
                pl.BlockSpec(block, lambda r, f: (jnp.minimum(r, half - 1), 0, 0)),
                pl.BlockSpec(block, lambda r, f: (jnp.maximum(r - half, 0), 0, 0)),
            ],
        ),
        out_shape=[buf, buf],
        compiler_params=params(24),
        cost_estimate=cost(5e9, 17e6),
        name="down_gradient",
    )(me, in_hbm(act), dbr, gwp)


def up_grad_kernel(dims, me, dbr, slp, wd, ht, keep, send, din, dsum):
    pr = keep.shape[1]
    half = PIECES // 2
    rows = dbr.shape[0]
    tile = 256
    dsum[...] = jnp.zeros_like(dsum)
    for r0 in range(0, rows, tile):
        r = slice(r0, r0 + tile)
        d_inner = (nt(dbr[r, :], wd[...]) * slp[r, :].astype(f32)).astype(bf16)
        din[r, :] = d_inner
        dsum[...] += jnp.sum(d_inner.astype(f32), axis=0, keepdims=True)
    for dst, side, low in sides(me, dims, keep, send):
        at = pl.multiple_of(side * (half * pr), half * pr)
        g = nn(ht[pl.ds(at, half * pr), :], din[...])
        for t in range(half):
            dst[t ^ low] = g[t * pr : (t + 1) * pr]


def up_grad(dims, me, dbr, slp, wd, ht):
    rows, width = dbr.shape
    ff = slp.shape[1]
    half, pr = PIECES // 2, width // PIECES
    buf = struct((half, pr, ff), f32)
    part = pl.BlockSpec((half, pr, FF_CHUNK), lambda c: (0, 0, c))
    wide = pl.BlockSpec((rows, FF_CHUNK), lambda c: (0, c))
    return pl.pallas_call(
        functools.partial(up_grad_kernel, dims),
        grid=(ff // FF_CHUNK,),
        in_specs=[
            SMEM,
            held(dbr.shape),
            wide,
            pl.BlockSpec((FF_CHUNK, width), lambda c: (c, 0)),
            held(ht.shape),
        ],
        out_specs=[part, part, wide, pl.BlockSpec((1, FF_CHUNK), lambda c: (0, c))],
        out_shape=[buf, buf, pltpu.HBM((rows, ff), bf16), struct((1, ff), f32)],
        compiler_params=params(28),
        cost_estimate=cost(10e9, 30e6),
        name="up_gradient",
    )(me, dbr, in_hbm(slp), in_hbm(wd), ht)


def mid_back_kernel(me, din, wu, dr2, n1, i1, g1, wo, dr1, dpr, dat, sums, acc):
    c = pl.program_id(0)
    rows, width = dr1.shape
    span = dr2.shape[1]

    @pl.when(c == 0)
    def _():
        acc[...] = nt(din[...], wu[...])

    @pl.when(c > 0)
    def _():
        acc[...] += nt(din[...], wu[...])

    at = pl.ds(pl.multiple_of(c * span, span), span)
    acc[:, at] += dr2[...]

    @pl.when(c == pl.num_programs(0) - 1)
    def _():
        sums[...] = jnp.zeros_like(sums)
        tile = 256
        for r0 in range(0, rows, tile):
            r = slice(r0, r0 + tile)
            d = acc[r, :]
            normal = n1[r, :].astype(f32)
            sums[0:1, :] += jnp.sum(d * normal, axis=0, keepdims=True)
            sums[1:2, :] += jnp.sum(d, axis=0, keepdims=True)
            dr = norm_back(d, row(g1), normal, i1[r, :])
            dr1[r, :] = dr
            low = dr.astype(bf16)
            dpr[r, :] = low
            sums[2:3, :] += jnp.sum(low.astype(f32), axis=0, keepdims=True)
            dat[r, :] = nt(low, wo[...]).astype(bf16)


def mid_back(me, din, wu, dr2, n1, i1, g1, wo):
    rows, width = dr2.shape
    ff = din.shape[1]
    steps = ff // FF_CHUNK
    ins = [me, in_hbm(din), in_hbm(wu), dr2, n1, i1, g1, wo]
    specs = [held(x.shape) for x in ins]
    specs[0] = SMEM
    specs[1] = pl.BlockSpec((rows, FF_CHUNK), lambda c: (0, c))
    specs[2] = pl.BlockSpec((width, FF_CHUNK), lambda c: (0, c))
    specs[3] = pl.BlockSpec((rows, width // steps), lambda c: (0, c))
    outs = [
        struct((rows, width), f32),
        struct((rows, width), bf16),
        struct((rows, width), bf16),
        struct((8, width), f32),
    ]
    return pl.pallas_call(
        mid_back_kernel,
        grid=(steps,),
        in_specs=specs,
        out_specs=[whole(x.shape) for x in outs],
        out_shape=outs,
        scratch_shapes=[pltpu.VMEM((rows, width), f32)],
        compiler_params=params(32),
        cost_estimate=cost(9e9, 15e6),
        name="middle_backward",
    )(*ins)


def qkv_grad_kernel(dims, has_out, me, tok, d0, d1, d2, *rest):
    keep, send = rest[-2:]
    pairs = [(tok, d0), (tok, d1), (tok, d2)]
    if has_out:
        pairs.append(rest[:2])
    half = PIECES // 2
    pr = keep.shape[1]
    for dst, side, low in sides(me, dims, keep, send):
        at = pl.ds(pl.multiple_of(side * (half * pr), half * pr), half * pr)
        col = 0
        for left, d in pairs:
            g = tn(left[:, at], d[...])
            cols = d.shape[1]
            for t in range(half):
                dst[t ^ low, :, col : col + cols] = g[t * pr : (t + 1) * pr]
            col += cols


def qkv_grad(dims, me, tok, ds, outer):
    rows, width = tok.shape
    ins = [me, tok, *ds, *outer]
    cols = sum(d.shape[1] for d in ds) + (width if outer else 0)
    buf = struct((PIECES // 2, width // PIECES, cols), f32)
    return pl.pallas_call(
        functools.partial(qkv_grad_kernel, dims, bool(outer)),
        in_specs=[SMEM] + [VMEM] * (len(ins) - 1),
        out_specs=[VMEM] * 2,
        out_shape=[buf, buf],
        compiler_params=params(10),
        cost_estimate=cost(4e9, 8e6),
        name="qkv_gradient",
    )(*ins)


def input_grad_kernel(count, me, *refs):
    ds = refs[:count]
    w, dr1, out = refs[count:]
    tile = 256
    for r0 in range(0, out.shape[0], tile):
        r = slice(r0, r0 + tile)
        acc = dr1[r, :]
        for j, d in enumerate(ds):
            acc = acc + nt(d[r, :], w[:, j * 256 : (j + 1) * 256])
        out[r, :] = acc


def input_grad(me, ds, w, dr1):
    return pl.pallas_call(
        functools.partial(input_grad_kernel, len(ds)),
        in_specs=[SMEM] + [VMEM] * (len(ds) + 2),
        out_specs=VMEM,
        out_shape=struct(dr1.shape, f32),
        compiler_params=params(10),
        cost_estimate=cost(5e9, 15e6),
        name="input_gradient",
    )(me, *ds, w, dr1)


def collect_kernel(s0, s1, s2, dsum, sm1, sm2, out):
    width = out.shape[1]
    for j, s in enumerate((s0, s1, s2)):
        out[0:2, j * 256 : (j + 1) * 256] = s[0:2, :]
    out[2:3, :] = sm1[2:3, :]
    out[3:5, :] = sm1[0:2, :]
    end = 5
    for j in range(dsum.shape[1] // width):
        out[end : end + 1, :] = dsum[:, j * width : (j + 1) * width]
        end += 1
    out[end : end + 1, :] = sm2[2:3, :]
    out[end + 1 : end + 3, :] = sm2[0:2, :]
    out[end + 3 :, :] = jnp.zeros((out.shape[0] - end - 3, width), f32)


def collect(s, dsum, sm1, sm2):
    ins = [*s, dsum, sm1, sm2]
    return pl.pallas_call(
        collect_kernel,
        in_specs=[VMEM] * len(ins),
        out_specs=VMEM,
        out_shape=struct((16, sm1.shape[1]), f32),
        compiler_params=params(6),
        cost_estimate=cost(1e4, 1e5),
        name="collect_vectors",
    )(*ins)


def swap(x, mask, n):
    return lax.ppermute(x, "dp", [(i, i ^ mask) for i in range(n)])


def after(x, *others):
    return lax.optimization_barrier((x,) + others)[0]


def join(x, y):
    which = lax.broadcasted_iota(i32, (2,) + x.shape, 0)
    both = jnp.where(which == 0, x[None], y[None])
    return both.reshape((2 * x.shape[0],) + x.shape[1:])


class Chain:
    def __init__(self, keep, send, dims, n):
        self.keep, self.ready, self.dims, self.n = keep, send, dims, n
        self.at = 0
        self.steps = len(dims) + 4
        self.out = None
        self.recv = None

    def start(self):
        k, dims = self.at, self.dims
        d = dims[k] if k < len(dims) else dims[3 - (k - len(dims))]
        self.recv = swap(self.ready, d, self.n)

    def land(self, *others):
        if self.recv is None:
            self.start()
        k, dims = self.at, self.dims
        self.at += 1
        recv = after(self.recv, *others) if others else self.recv
        self.recv = None
        if k < 4:
            recv = recv.astype(f32)
            half = self.keep.shape[0] // 2
            if k < 3:
                self.ready = (self.keep[half:] + recv[half:]).astype(bf16)
                self.keep = self.keep[:half] + recv[:half]
            else:
                self.ready = (self.keep + recv).astype(bf16)
        elif k < len(dims):
            self.ready = (self.ready.astype(f32) + recv.astype(f32)).astype(bf16)
        elif k == len(dims) + 3:
            self.out = (self.ready, recv)
        else:
            self.ready = join(self.ready, recv)

    def finish(self):
        while self.out is None:
            self.land()
        return self.out


class Total:
    def __init__(self, x, n):
        self.ready, self.n, self.at, self.recv, self.out = x, n, 0, None, None

    def start(self):
        self.recv = swap(self.ready, 1 << self.at, self.n)

    def land(self, *others):
        if self.recv is None:
            self.start()
        self.ready = self.ready + (after(self.recv, *others) if others else self.recv)
        self.recv = None
        self.at += 1
        if 1 << self.at == self.n:
            self.out = self.ready

    def finish(self):
        while self.out is None:
            self.land()
        return self.out


def gather_all(x, n):
    for b in reversed(range(n.bit_length() - 1)):
        x = join(x, swap(x, 1 << b, n))
    return x


def place_kernel(chains, layout, count, me, *refs):
    bufs, outs = refs[: len(chains)], refs[-count:]
    half = PIECES // 2
    for i, dims in enumerate(chains):
        low = flip_of(me[0], dims) & (half - 1)
        pr = bufs[i].shape[1]
        for t in range(half):
            for which, col, cols, row0, out, out_col, out_rows in layout:
                if which == i:
                    at = t * out_rows + row0
                    outs[out][at : at + pr, out_col : out_col + cols] = bufs[i][
                        t ^ low, :, col : col + cols
                    ].astype(f32)


def put_in_place(chains, me, layout, shapes, previous, name):
    bufs = [c.ready if previous is None else c.out[1] for c in chains]
    ins = [me, *bufs]
    specs = [pl.BlockSpec(x.shape, lambda a, f: (0, 0, 0)) for x in bufs]
    aliases = {}
    if previous is not None:
        for i, g in enumerate(previous):
            aliases[len(ins)] = i
            ins.append(g)
            specs.append(pl.BlockSpec(memory_space=pl.ANY))
    dims = chains[0].dims

    def spot(a, f):
        own = lax.div(flip_of(f[0], dims), PIECES // 2)
        return (own if previous is None else 1 - own, 0)

    return pl.pallas_call(
        functools.partial(place_kernel, [c.dims for c in chains], layout, len(shapes)),
        grid_spec=pltpu.PrefetchScalarGridSpec(
            num_scalar_prefetch=1,
            grid=(1,),
            in_specs=specs,
            out_specs=[pl.BlockSpec((r // 2, w), spot) for r, w in shapes],
        ),
        out_shape=[struct(x, f32) for x in shapes],
        input_output_aliases=aliases,
        compiler_params=params(28),
        cost_estimate=cost(0, 0),
        name=name,
    )(*ins)


SCHEDULE = (
    "+D", "up", "+U", "-D", "+D", "mid", "-U", "+U", "E0", "-D", "+D", "q0", "+Q0", "E1", "-U",
    "+U", "-D", "+D", "-Q0", "+Q0", "q1", "+Q1", "E2", "-U", "+U", "-D", "+D", "-Q1", "+Q1", "q2",
    "+Q2", "-Q0", "+Q0", "vec", "+V", "-U", "+U", "-Q2", "+Q2", "-Q1", "+Q1", "-V", "+V", "in",
    "-D", "+D", "-Q0", "+Q0", "-Q2", "+Q2", "-Q1", "+Q1", "-V", "+V", "-Q0", "+Q0", "-U", "+U",
    "-Q2", "+Q2", "-V", "+V", "-D", "+D", "-Q1", "+Q1", "-U", "+U", "-Q0", "+Q0", "-Q2", "+Q2",
    "-V", "+V", "-Q1", "+Q1", "-D", "-Q2", "+Q2", "-Q0", "+Q0", "-V", "-U", "-Q1", "+Q1", "-Q2",
    "+Q2", "~U", "+U", "-Q0", "+Q0", "-Q1", "+Q1", "-Q2", "+Q2", "~D", "+D", "-Q0", "+Q0", "-Q1",
    "+Q1", "-U", "+U", "<U", "-Q2", "+Q2", "-D", "+D", "<D", "<Q", "-U", "=U", "-Q0", "-Q1", "-Q2",
    "=Q", "-D", "=D",
)


def axis_orders(n):
    rest = [1 << i for i in range(1, n.bit_length() - 1)]
    if n == 32:
        x, y, z, far = rest
        return {
            "D": (1, x, y, z, far),
            "U": (1, z, x, y, far),
            "Q0": (1, y, x, z, far),
            "Q1": (1, y, x, z, far),
            "Q2": (1, y, x, z, far),
        }
    names = ("D", "U", "Q0", "Q1", "Q2")
    return {name: tuple([1] + rest[i:] + rest[:i]) for i, name in enumerate(names)}


def body(
    tokens, seg_lengths, owner, place, w_qkv, b_qv, w_out, b_out, ln1_gain, ln1_bias,
    w_up, b_up, w_down, b_down, ln2_gain, ln2_bias, w_proj,
):
    rows, width = tokens.shape
    ff = w_up.shape[1]
    n = lax.axis_size("dp")
    me = lax.axis_index("dp").astype(i32).reshape(1)
    orders = axis_orders(n)

    packed, attended, lse, hid, low, ht, n1, i1 = attention(
        seg_lengths, tokens, w_qkv, b_qv, w_out, b_out, ln1_gain, ln1_bias
    )
    act, slp, n2, i2, nl, emb, ul, query = ffn_fwd(
        seg_lengths, hid, low, w_up, b_up, w_down, b_down, ln2_gain, ln2_bias, w_proj
    )

    msg, dpb = loss_forward(me, seg_lengths, owner, gather_all(query, n), ul)
    loss, dr2, dbr, gwp, sums2 = loss_back(
        me, seg_lengths, owner, place, gather_all(msg, n), dpb, emb, nl, n2, i2, ln2_gain, w_proj
    )

    chains = {"D": Chain(*down_grad(orders["D"], me, act, dbr, gwp), orders["D"], n)}
    flying = {}
    parts = []
    placed = {}
    small = None
    last = None

    def vectors(v):
        end = 5 + ff // width
        return [v[0:2].reshape(-1), v[5:end].reshape(-1)] + [
            v[i] for i in (2, 3, 4, end, end + 1, end + 2)
        ]

    def now(x):
        return after(x, *flying.values()) if flying else x

    members = {"Q": ["Q0", "Q1", "Q2"]}
    begun = {}

    def layout_of(name):
        if name == "D":
            layout = [(0, i * width, width, i * width // PIECES, 0, 0, ff // PIECES) for i in range(ff // width)]
            layout.append((0, ff, w_proj.shape[1], 0, 1, 0, width // PIECES))
            return layout, [(ff, width), w_proj.shape], "down_place"
        if name == "U":
            return [(0, 0, ff, 0, 0, 0, width // PIECES)], [(width, ff)], "up_place"
        span = width // PORTIONS
        layout = [
            (c, i * span, span, 0, 0, i * width + c * span, width // PIECES)
            for c in range(PORTIONS)
            for i in range(3)
        ]
        layout.append((0, width, width, 0, 1, 0, width // PIECES))
        return layout, [(width, 3 * width), (width, width)], "qkv_place"

    def begin(name):
        layout, shapes, title = layout_of(name)
        own = [chains[q] for q in members.get(name, [name])]
        for c in own:
            while c.at < c.steps - 1:
                c.land()
        begun[name] = put_in_place(own, me, layout, shapes, None, title)
        return begun[name][0]

    def finish(name):
        if name not in begun:
            begin(name)
        layout, shapes, title = layout_of(name)
        own = [chains[q] for q in members.get(name, [name])]
        for c in own:
            c.finish()
        placed[name] = put_in_place(own, me, layout, shapes, begun[name], title)
        return placed[name][0]

    for event in SCHEDULE:
        if event[0] == "+":
            name = event[1:]
            if chains[name].out is None:
                chains[name].start()
                flying[name] = chains[name].ready
        elif event[0] == "-":
            name = event[1:]
            if chains[name].out is None:
                chains[name].land(*(last if isinstance(last, list) else [last] if last is not None else []))
                flying.pop(name, None)
                last = chains[name].ready
                if name == "V" and chains[name].out is not None:
                    small = vectors(chains[name].out)
                    last = small
        elif event[0] == "~":
            c = chains[event[1:]]
            c.ready = after(c.ready, *(last if isinstance(last, list) else [last]))
        elif event[0] == "<":
            last = begin(event[1:])
        elif event[0] == "=":
            last = finish(event[1:])
        elif event == "up":
            keep, send, din, dsum = up_grad(orders["U"], now(me), dbr, slp, w_down, ht)
            chains["U"] = Chain(keep, send, orders["U"], n)
            last = dsum
        elif event == "mid":
            dr1, dpr, dat, sums1 = mid_back(now(me), din, w_up, dr2, n1, i1, ln1_gain, w_out)
            last = sums1
        elif event[0] == "E":
            j = int(event[1])
            parts.append(attention_back(j, now(seg_lengths), packed, dat, attended, lse))
            last = parts[j][3]
        elif event[0] == "q":
            j = int(event[1])
            outer = [attended, dpr] if j == 0 else []
            name = "Q%d" % j
            keep, send = qkv_grad(orders[name], now(me), tokens, parts[j][:3], outer)
            chains[name] = Chain(keep, send, orders[name], n)
            last = send
        elif event == "vec":
            chains["V"] = Total(collect([x[3] for x in parts], dsum, sums1, sums2), n)
        elif event == "in":
            ds = [x[i] for i in range(3) for x in parts]
            d_tokens = input_grad(now(me), ds, w_qkv, dr1)
            last = d_tokens
    if small is None:
        small = vectors(chains["V"].finish())
    g_w_down, g_w_proj = placed["D"]
    g_w_up = placed["U"][0]
    g_w_qkv, g_w_out = placed["Q"]
    g_b_qv, g_b_up, g_b_out, g_ln1_gain, g_ln1_bias, g_b_down, g_ln2_gain, g_ln2_bias = small
    return (
        loss[0, 0:1], d_tokens, g_w_qkv, g_b_qv, g_w_out, g_b_out, g_ln1_gain, g_ln1_bias,
        g_w_up, g_b_up, g_w_down, g_b_down, g_ln2_gain, g_ln2_bias, g_w_proj,
    )


def solution(mesh):
    whole_rows = P("dp", None)
    return jax.shard_map(
        body,
        mesh=mesh,
        in_specs=(whole_rows, whole_rows) + (P(),) * 15,
        out_specs=(P("dp"), whole_rows) + (P(),) * 13,
        check_vma=False,
    )
```

```python
import functools

import jax
import jax.numpy as jnp
from jax import lax
from jax.experimental import pallas as pl
from jax.experimental.pallas import tpu as pltpu
from jax.sharding import PartitionSpec as P

HEADS = 12
QLEN = 32
PLEN = 180
QB = 128
WIDTHS = (256, 384, 512, 768, 1024)
PIECES = 16
PORTIONS = 3
NEG = -1e30
LN_EPS = 1e-12
NORM_EPS = 1e-6
f32, bf16, i32 = jnp.float32, jnp.bfloat16, jnp.int32


def nn(a, b):
    return lax.dot_general(a, b, (((1,), (0,)), ((), ())), preferred_element_type=f32)


def nt(a, b):
    return lax.dot_general(a, b, (((1,), (1,)), ((), ())), preferred_element_type=f32)


def tn(a, b):
    return lax.dot_general(a, b, (((0,), (0,)), ((), ())), preferred_element_type=f32)


def params(mib=48):
    return pltpu.CompilerParams(vmem_limit_bytes=mib << 20)


def cost(flops, nbytes):
    return pl.CostEstimate(flops=0, bytes_accessed=0, transcendentals=0)


SMEM = pl.BlockSpec(memory_space=pltpu.SMEM)
VMEM = pl.BlockSpec(memory_space=pltpu.VMEM)


def whole(shape):
    return pl.BlockSpec(shape, lambda *g: (0,) * len(shape))


def held(shape):
    return pl.BlockSpec(shape, lambda *g: (0,) * len(shape), pipeline_mode=pl.Buffered(1))


def in_hbm(x):
    return pltpu.with_memory_space_constraint(x, pltpu.HBM)


def struct(shape, dtype):
    return jax.ShapeDtypeStruct(shape, dtype)


def row(v):
    return v[...].reshape(1, -1)


def normalize(resid):
    center = resid - jnp.mean(resid, axis=-1, keepdims=True)
    inv = lax.rsqrt(jnp.mean(center * center, axis=-1, keepdims=True) + LN_EPS)
    return center * inv, inv


def segment_ends(lens):
    ends = [lens[0, 0]]
    for s in range(1, lens.shape[1]):
        ends.append(ends[-1] + lens[0, s])
    return ends


def segment_of(ends, position):
    seg = jnp.zeros(position.shape, i32)
    for e in ends:
        seg = seg + (position >= e).astype(i32)
    return seg


def key_window(ends, rows, first):
    lo = jnp.zeros((), i32)
    hi = jnp.asarray(rows, i32)
    for e in ends:
        lo = jnp.where(e <= first, e, lo)
    for e in reversed(ends):
        hi = jnp.where(e >= first + QB, e, hi)
    lo = lax.div(lo, QB) * QB
    need = hi - lo
    cls = jnp.zeros((), i32)
    wide = jnp.asarray(WIDTHS[0], i32)
    for c, w in enumerate(WIDTHS[:-1]):
        if WIDTHS[c + 1] <= rows:
            cls = jnp.where(need > w, c + 1, cls)
            wide = jnp.where(need > w, WIDTHS[c + 1], wide)
    return pl.multiple_of(jnp.minimum(lo, rows - wide), QB), cls


def fill_segments(ends, segq, segk):
    segk[...] = segment_of(ends, lax.broadcasted_iota(i32, segk.shape, 0))
    at = lax.broadcasted_iota(i32, segq.shape, 0) * QB + lax.broadcasted_iota(i32, segq.shape, 1)
    segq[...] = segment_of(ends, at)


def two_heads(x, scale=None):
    lane = lax.broadcasted_iota(i32, x.shape, 1)
    zero = jnp.zeros_like(x)
    if scale is not None:
        x = x * scale
    return jnp.concatenate([jnp.where(lane < 64, x, zero), jnp.where(lane < 64, zero, x)], axis=0)


def pick_heads(t):
    return jnp.concatenate([t[:64, :QB], t[64:, QB:]], axis=0)


def attn_fwd_kernel(lens, *refs):
    count = 7
    given, (packed_out, out, lse, hid, low, ht, n1, i1) = refs[:count], refs[count : count + 8]
    vt, segq, segk, packed = refs[count + 8 : count + 12]
    tok, wqkv, bqv, wo, bo, g1, b1 = refs[count + 12 : count + 12 + count]
    sems, wsems, psems = refs[count + 12 + count :]
    rows, width = tok.shape
    cols = 3
    fetch = [
        pltpu.make_async_copy(given[i], x, sems.at[i])
        for i, x in ((0, tok), (2, bqv), (3, wo), (4, bo), (5, g1), (6, b1))
    ]
    chunk = [
        pltpu.make_async_copy(
            given[1].at[:, j * width : (j + 1) * width],
            wqkv.at[:, j * width : (j + 1) * width],
            wsems.at[j],
        )
        for j in range(cols)
    ]
    keep = [
        pltpu.make_async_copy(
            packed.at[:, j * width : (j + 1) * width],
            packed_out.at[:, j * width : (j + 1) * width],
            psems.at[j],
        )
        for j in range(cols)
    ]
    for f in fetch[:2]:
        f.start()
    for c in chunk:
        c.start()
    for f in fetch[2:]:
        f.start()
    ends = segment_ends(lens)
    fill_segments(ends, segq, segk)
    pairs = width // 128
    for f in fetch[:2]:
        f.wait()
    for j in range(cols):
        at = slice(j * width, (j + 1) * width)
        chunk[j].wait()
        for r in (slice(0, rows // 2), slice(rows // 2, rows)):
            x = nn(tok[r, :], wqkv[:, at])
            if j != 1:
                b0 = width if j else 0
                x = x + bqv[b0 : b0 + width].reshape(1, width)
            packed[r, at] = x.astype(bf16)
        keep[j].start()
    q = packed.at[:, 0:width]
    k = packed.at[:, width : 2 * width]
    v = packed.at[:, 2 * width : 3 * width]
    for g in range(pairs):
        vt[g] = v[:, g * 128 : (g + 1) * 128].T

    def step(i, carry):
        base = pl.multiple_of(i * QB, QB)
        k0, cls = key_window(ends, rows, base)
        sq = segq[pl.ds(i, 1), :]

        def body(w):
            same = segk[pl.ds(k0, w), :] == sq
            sts = []
            for g in range(pairs):
                sl = slice(g * 128, (g + 1) * 128)
                q2 = two_heads(q[pl.ds(base, QB), sl], jnp.asarray(0.125, bf16))
                sts.append(nt(k[pl.ds(k0, w), sl], q2))
            for g in range(pairs):
                sl = slice(g * 128, (g + 1) * 128)
                st = sts[g]
                ps, ms, ls = [], [], []
                for h in range(2):
                    s = jnp.where(same, st[:, h * QB : (h + 1) * QB], NEG)
                    m = jnp.max(s, axis=0, keepdims=True)
                    p = jnp.exp(s - m)
                    ls.append(jnp.sum(p, axis=0, keepdims=True))
                    ms.append(m)
                    ps.append(p.astype(bf16))
                total = jnp.concatenate(ls, 1)
                top = jnp.concatenate(ms, 1)
                ot = nn(vt[g, :, pl.ds(k0, w)], jnp.concatenate(ps, 1)) * (1.0 / total)
                out[pl.ds(base, QB), sl] = pick_heads(ot).T.astype(bf16)
                lse[g, pl.ds(i, 1), :] = top + jnp.log(total)

        for c, w in enumerate(WIDTHS):
            if w <= rows:
                pl.when(cls == c)(functools.partial(body, w))
        return carry

    lax.fori_loop(0, rows // QB, step, 0)
    for f in fetch[2:]:
        f.wait()
    tile = 256
    for r0 in range(0, rows, tile):
        r = slice(r0, r0 + tile)
        resid = tok[r, :].astype(f32) + (nn(out[r, :], wo[...]) + row(bo))
        normal, inv = normalize(resid)
        hidden = normal * row(g1) + row(b1)
        hid[r, :] = hidden
        hl = hidden.astype(bf16)
        low[r, :] = hl
        ht[:, r] = hl.T
        n1[r, :] = normal.astype(bf16)
        i1[r, :] = inv
    for k in keep:
        k.wait()


def attn_bwd_kernel(
    lens, q, k, v, do, o, lse, dq, dk, dv, sums, kt, dka, dva, segq, segk
):
    rows, span = q.shape
    ends = segment_ends(lens)
    fill_segments(ends, segq, segk)
    pairs = span // 128
    for g in range(pairs):
        kt[g] = k[:, g * 128 : (g + 1) * 128].T
    dka[...] = jnp.zeros_like(dka)
    dva[...] = jnp.zeros_like(dva)
    head = (
        lax.broadcasted_iota(i32, (8, 128), 0) == lax.broadcasted_iota(i32, (8, 128), 1) // 64
    ).astype(f32)

    def step(i, carry):
        base = pl.multiple_of(i * QB, QB)
        k0, cls = key_window(ends, rows, base)
        sq = segq[pl.ds(i, 1), :]

        def body(w):
            at = pl.ds(k0, w)
            same = segk[at, :] == sq
            for g in range(pairs):
                gs = slice(g * 128, (g + 1) * 128)
                q2 = two_heads(q[pl.ds(base, QB), gs], jnp.asarray(0.125, bf16))
                do_ = do[pl.ds(base, QB), gs]
                do2 = two_heads(do_)
                d8 = lax.dot_general(
                    head,
                    do_.astype(f32) * o[pl.ds(base, QB), gs].astype(f32),
                    (((1,), (1,)), ((), ())),
                    precision=lax.Precision.HIGHEST,
                    preferred_element_type=f32,
                )
                lrow = lse[g, pl.ds(i, 1), :]
                st = nt(k[at, gs], q2)
                dpt = nt(v[at, gs], do2)
                ps, ds = [], []
                for h in range(2):
                    sl = slice(h * QB, (h + 1) * QB)
                    p = jnp.exp(jnp.where(same, st[:, sl] - lrow[:, sl], NEG))
                    ps.append(p.astype(bf16))
                    ds.append((p * (dpt[:, sl] - d8[h : h + 1, :])).astype(bf16))
                p = jnp.concatenate(ps, 1)
                d = jnp.concatenate(ds, 1)
                dka[at, gs] += nn(d, q2)
                dva[at, gs] += nn(p, do2)
                dqt = nn(kt[g, :, pl.ds(k0, w)], d)
                dq[pl.ds(base, QB), gs] = (pick_heads(dqt).T * 0.125).astype(bf16)

        for c, w in enumerate(WIDTHS):
            if w <= rows:
                pl.when(cls == c)(functools.partial(body, w))
        return carry

    lax.fori_loop(0, rows // QB, step, 0)
    dk[...] = dka[...].astype(bf16)
    dvl = dva[...].astype(bf16)
    dv[...] = dvl
    sums[0:1, :] = jnp.sum(dq[...].astype(f32), axis=0, keepdims=True)
    sums[1:2, :] = jnp.sum(dvl.astype(f32), axis=0, keepdims=True)


def segment_scratch(rows):
    return [pltpu.VMEM((rows // QB, QB), i32), pltpu.VMEM((rows, 128), i32)]


def attention(lens, tok, wqkv, bqv, wo, bo, g1, b1):
    rows, width = tok.shape
    pairs = width // 128
    ins = [tok, wqkv, bqv, wo, bo, g1, b1]
    anywhere = pl.BlockSpec(memory_space=pl.ANY)
    return pl.pallas_call(
        attn_fwd_kernel,
        in_specs=[SMEM] + [anywhere] * len(ins),
        out_specs=[anywhere] + [VMEM] * 7,
        out_shape=[
            pltpu.HBM((rows, 3 * width), bf16),
            struct((rows, width), bf16),
            struct((pairs, rows // QB, 2 * QB), f32),
            struct((rows, width), f32),
            struct((rows, width), bf16),
            pltpu.HBM((width, rows), bf16),
            pltpu.HBM((rows, width), bf16),
            pltpu.HBM((rows, 1), f32),
        ],
        scratch_shapes=[pltpu.VMEM((pairs, 128, rows), bf16)]
        + segment_scratch(rows)
        + [pltpu.VMEM((rows, 3 * width), bf16)]
        + [pltpu.VMEM(x.shape, x.dtype) for x in ins]
        + [
            pltpu.SemaphoreType.DMA((len(ins),)),
            pltpu.SemaphoreType.DMA((3,)),
            pltpu.SemaphoreType.DMA((3,)),
        ],
        compiler_params=params(32),
        cost_estimate=cost(18e9, 8 * rows * width),
        name="attention_forward",
    )(lens, *[in_hbm(x) for x in ins])


def attention_back(part, lens, packed, do, o, lse):
    rows, width = packed.shape[0], packed.shape[1] // 3
    span = width // PORTIONS
    pairs = span // 128
    shp = struct((rows, span), bf16)
    col = lambda off: pl.BlockSpec((rows, span), lambda g, off=off: (0, off * PORTIONS + part))
    own = pl.BlockSpec((rows, span), lambda g: (0, 0))
    return pl.pallas_call(
        attn_bwd_kernel,
        grid=(1,),
        in_specs=[SMEM, col(0), col(1), col(2), col(0), col(0)]
        + [pl.BlockSpec((pairs,) + lse.shape[1:], lambda g: (part, 0, 0))],
        out_specs=[own, own, own, whole((8, span))],
        out_shape=[shp, shp, shp, struct((8, span), f32)],
        scratch_shapes=[
            pltpu.VMEM((pairs, 128, rows), bf16),
            pltpu.VMEM((rows, span), f32),
            pltpu.VMEM((rows, span), f32),
        ]
        + segment_scratch(rows),
        compiler_params=params(16),
        cost_estimate=cost(10e9, 16 * rows * span),
        name="attention_backward",
    )(lens, packed, packed, packed, do, o, lse)


def norm_back(grad, gain, normal, inv):
    dn = grad * gain
    return inv * (
        dn
        - jnp.mean(dn, axis=-1, keepdims=True)
        - normal * jnp.mean(dn * normal, axis=-1, keepdims=True)
    )


FF_CHUNK = 1024


def ffn_fwd_kernel(
    lens, hid, low, wu, bu, wd, bd, g2, b2, wp, act, slp, n2, i2, nl, emb, ul, msg, acc
):
    c = pl.program_id(0)
    rows = low.shape[0]
    span = hid.shape[1]
    tile = 256
    tiles = [slice(r, r + tile) for r in range(0, rows, tile)]

    @pl.when(c == 0)
    def _():
        for r in tiles:
            acc[r, :] = jnp.broadcast_to(row(bd), acc[r, :].shape)

    for r in tiles:
        inner = nn(low[r, :], wu[...]) + row(bu)
        cdf = 0.5 + 0.5 * lax.erf(inner * 0.7071067811865476)
        a = (inner * cdf).astype(bf16)
        act[r, :] = a
        slp[r, :] = (cdf + inner * (jnp.exp(inner * inner * -0.5) * 0.3989422804014327)).astype(bf16)
        acc[r, :] += nn(a, wd[...])
    at = pl.ds(pl.multiple_of(c * span, span), span)
    acc[:, at] += hid[...]

    @pl.when(c == pl.num_programs(0) - 1)
    def _():
        for r in tiles:
            normal, inv = normalize(acc[r, :])
            normed = (normal * row(g2) + row(b2)).astype(bf16)
            n2[r, :] = normal.astype(bf16)
            i2[r, :] = inv
            nl[r, :] = normed
            e = nn(normed, wp[...])
            emb[r, :] = e
            ul[r, :] = (
                e * lax.rsqrt(jnp.sum(e * e, axis=-1, keepdims=True) + NORM_EPS)
            ).astype(bf16)
        count = lens[0, 0]
        slot = lax.broadcasted_iota(i32, (QLEN, ul.shape[1]), 0)
        msg[0, 0:QLEN, :] = jnp.where(slot < count, ul[0:QLEN, :].astype(f32), 0.0).astype(bf16)
        msg[0, QLEN : QLEN + 16, :] = (
            jnp.full((16, ul.shape[1]), count, i32).astype(f32).astype(bf16)
        )


def ffn_fwd(lens, hid, low, wu, bu, wd, bd, g2, b2, wp):
    rows, width = hid.shape
    ff, out = wu.shape[1], wp.shape[1]
    steps = ff // FF_CHUNK
    ins = [lens, hid, low, in_hbm(wu), bu, in_hbm(wd), bd, g2, b2, wp]
    specs = [held(x.shape) for x in ins]
    specs[0] = SMEM
    specs[1] = pl.BlockSpec((rows, width // steps), lambda c: (0, c))
    specs[3] = pl.BlockSpec((width, FF_CHUNK), lambda c: (0, c))
    specs[4] = pl.BlockSpec((FF_CHUNK,), lambda c: (c,))
    specs[5] = pl.BlockSpec((FF_CHUNK, width), lambda c: (c, 0))
    outs = [
        pltpu.HBM((rows, ff), bf16),
        pltpu.HBM((rows, ff), bf16),
        pltpu.HBM((rows, width), bf16),
        struct((rows, 1), f32),
        pltpu.HBM((rows, width), bf16),
        struct((rows, out), f32),
        struct((rows, out), bf16),
        struct((1, QLEN + 16, out), bf16),
    ]
    ospecs = [whole(x.shape) for x in outs]
    ospecs[0] = ospecs[1] = pl.BlockSpec((rows, FF_CHUNK), lambda c: (0, c))
    return pl.pallas_call(
        ffn_fwd_kernel,
        grid=(steps,),
        in_specs=specs,
        out_specs=ospecs,
        out_shape=outs,
        scratch_shapes=[pltpu.VMEM((rows, width), f32)],
        compiler_params=params(32),
        cost_estimate=cost(18e9, 40e6),
        name="ffn_forward",
    )(*ins)


def relative(device, n):
    bits = n.bit_length() - 1
    at = jnp.zeros((), i32)
    for b in range(bits):
        at = at | (((device >> b) & 1) << (bits - 1 - b))
    return at


def loss_kernel(me, lens, owner, gathered, ul, msg, dpb):
    n, nump = owner.shape
    rows = ul.shape[0]
    total = nump * QLEN
    seg = segment_of(segment_ends(lens), lax.broadcasted_iota(i32, (1, rows), 1))
    rel = [relative(owner[me[0], p] ^ me[0], n) for p in range(nump)]
    qs = [gathered[rel[p], 0:QLEN, :] for p in range(nump)]
    q = jnp.concatenate(qs, axis=0)
    slot = lax.broadcasted_iota(i32, (QLEN, 1), 0).astype(f32)
    valid = jnp.concatenate(
        [
            (slot < gathered[rel[p], QLEN : QLEN + 16, :][0:1, 0:1].astype(f32)).astype(f32)
            for p in range(nump)
        ],
        axis=0,
    )
    group = lax.broadcasted_iota(i32, (total, rows), 0) // QLEN + 1
    x = jnp.where(group == seg, nt(q, ul[...]) * 10.0, NEG)
    top = jnp.max(x, axis=1, keepdims=True)
    e = jnp.exp(x - top)
    sm = jnp.sum(e, axis=1, keepdims=True)
    soft = valid * (0.1 * (top + jnp.log(sm)))
    lane = lax.broadcasted_iota(i32, (1, 128), 1)
    score = jnp.zeros((1, 128), f32)
    for p in range(nump):
        score = score + jnp.where(
            lane == p, jnp.sum(soft[p * QLEN : (p + 1) * QLEN], axis=0, keepdims=True), 0.0
        )
    w = e * (valid / sm)
    wh = w.astype(bf16)
    wl = (w - wh.astype(f32)).astype(bf16)
    msg[0, 0:total, :] = (nn(wh, ul[...]) + nn(wl, ul[...])).astype(bf16)
    hi = score.astype(bf16)
    rest = score - hi.astype(f32)
    mid = rest.astype(bf16)
    lo = (rest - mid.astype(f32)).astype(bf16)
    row = lax.broadcasted_iota(i32, (16, 128), 0)
    tail = jnp.where(row == 0, hi.astype(f32), 0.0)
    tail = tail + jnp.where(row == 1, mid.astype(f32), 0.0)
    tail = tail + jnp.where(row == 2, lo.astype(f32), 0.0)
    msg[0, total : total + 16, :] = tail.astype(bf16)
    dpb[...] = tn(wh, q) + tn(wl, q)


def loss_forward(me, lens, owner, gathered, ul):
    rows, out = ul.shape
    total = owner.shape[1] * QLEN
    smem = pl.BlockSpec(memory_space=pltpu.SMEM)
    vmem = pl.BlockSpec(memory_space=pltpu.VMEM)
    return pl.pallas_call(
        loss_kernel,
        in_specs=[smem] * 3 + [vmem] * 2,
        out_specs=[vmem] * 2,
        out_shape=[struct((1, total + 16, out), bf16), struct((rows, out), f32)],
        compiler_params=params(8),
        cost_estimate=cost(1e9, 2e6),
        name="loss_forward",
    )(me, lens, owner, gathered, ul)


def loss_back_kernel(
    me, lens, owner, place, messages, dpb, emb, nl, n2, i2, g2, wp,
    loss, dr2, dbr, gwp, sums, du, gwpt, inverse,
):
    n, nump = owner.shape
    groups = nump + 1
    rows, width = nl.shape
    total = nump * QLEN
    mine = me[0]

    def note(i, carry):
        for p in range(nump):
            inverse[owner[i, p] * nump + place[i, p]] = i * nump + p
        return carry

    lax.fori_loop(0, n, note, 0)
    group = [mine] + [owner[mine, p] for p in range(nump)]
    plc = [place[mine, p] for p in range(nump)]
    src, col = {}, {}
    for g in range(groups):
        for r in range(nump):
            entry = inverse[group[g] * nump + r]
            src[g, r] = relative(lax.div(entry, nump) ^ mine, n)
            col[g, r] = lax.rem(entry, nump)
    lane = lax.broadcasted_iota(i32, (8, 128), 1)
    sub = lax.broadcasted_iota(i32, (8, 128), 0)
    vals = []
    for r in range(nump):
        a = jnp.zeros((8, 128), f32)
        for g in range(groups):
            t = messages[src[g, r], total : total + 16, :].astype(f32)
            t = t[0:1, :] + t[1:2, :] + t[2:3, :]
            a = jnp.where((sub == g) & (lane == col[g, r]), t, a)
        vals.append(jnp.sum(a, axis=1, keepdims=True))
    top = vals[0]
    for v in vals[1:]:
        top = jnp.maximum(top, v)
    es = [jnp.exp(v - top) for v in vals]
    sm = es[0]
    for e in es[1:]:
        sm = sm + e
    loss[...] = jnp.broadcast_to((top + jnp.log(sm) - vals[0])[0:1], (8, 128))
    dt = [e / sm - (1.0 if r == 0 else 0.0) for r, e in enumerate(es)]
    sub1 = lax.broadcasted_iota(i32, (8, 1), 0)
    place = jnp.zeros((8, 1), i32)
    for p in range(nump):
        place = jnp.where(sub1 == p + 1, plc[p], place)
    dscore = jnp.zeros((8, 1), f32)
    for r in range(nump):
        dscore = jnp.where(place == r, dt[r], dscore)
    dmq = jnp.zeros((QLEN, 128), f32)
    for r in range(nump):
        at = pl.multiple_of(col[0, r] * QLEN, QLEN)
        dmq = dmq + dt[r][0:1] * messages[src[0, r], pl.ds(at, QLEN), :].astype(f32)
    sk = segment_of(segment_ends(lens), lax.broadcasted_iota(i32, (rows, 128), 0))
    scale = jnp.zeros(sk.shape, f32)
    for p in range(nump):
        scale = jnp.where(sk == p + 1, dscore[p + 1 : p + 2], scale)
    du[...] = scale * dpb[...]
    du[0:QLEN, :] = jnp.where(sk[0:QLEN] == 0, dmq, du[0:QLEN, :])

    gwpt[...] = jnp.zeros_like(gwpt)
    sums[...] = jnp.zeros_like(sums)
    tile = 256
    for r0 in range(0, rows, tile):
        r = slice(r0, r0 + tile)
        e = emb[r, :]
        inv = lax.rsqrt(jnp.sum(e * e, axis=-1, keepdims=True) + NORM_EPS)
        unit = e * inv
        d = du[r, :].astype(bf16).astype(f32)
        de = (inv * (d - unit * jnp.sum(unit * d, axis=-1, keepdims=True))).astype(bf16)
        gwpt[...] += tn(de, nl[r, :])
        dn = nt(de, wp[...])
        normal = n2[r, :].astype(f32)
        sums[0:1, :] += jnp.sum(dn * normal, axis=0, keepdims=True)
        sums[1:2, :] += jnp.sum(dn, axis=0, keepdims=True)
        dr = norm_back(dn, row(g2), normal, i2[r, :])
        dr2[r, :] = dr
        db = dr.astype(bf16)
        dbr[r, :] = db
        sums[2:3, :] += jnp.sum(db.astype(f32), axis=0, keepdims=True)
    gwp[...] = gwpt[...].T


def loss_back(me, lens, owner, place, messages, dpb, emb, nl, n2, i2, g2, wp):
    rows, width = nl.shape
    out = wp.shape[1]
    smem = pl.BlockSpec(memory_space=pltpu.SMEM)
    vmem = pl.BlockSpec(memory_space=pltpu.VMEM)
    return pl.pallas_call(
        loss_back_kernel,
        in_specs=[smem] * 4 + [vmem] * 8,
        out_specs=[vmem] * 5,
        out_shape=[
            struct((8, 128), f32),
            pltpu.HBM((rows, width), f32),
            struct((rows, width), bf16),
            struct((width, out), f32),
            struct((8, width), f32),
        ],
        scratch_shapes=[
            pltpu.VMEM((rows, out), f32),
            pltpu.VMEM((out, width), f32),
            pltpu.SMEM((owner.size,), i32),
        ],
        compiler_params=params(14),
        cost_estimate=cost(6e9, 10e6),
        name="loss_backward",
    )(me, lens, owner, place, messages, dpb, emb, nl, n2, i2, g2, wp)


def flip_of(device, dims):
    m = jnp.zeros((), i32)
    for i, d in enumerate(dims[:4]):
        m = m | jnp.where((device & d) != 0, 8 >> i, 0)
    return m


def sides(me, dims, keep, send):
    m = flip_of(me[0], dims)
    half = PIECES // 2
    top, low = lax.div(m, half), lax.rem(m, half)
    return [(keep, top, low), (send, 1 - top, low)]


DOWN_BATCH = 4


def down_grad_kernel(dims, me, act, dbr, gwp, keep, send):
    r = pl.program_id(0)
    pr, width = keep.shape[1], dbr.shape[1]
    parts = act.shape[1] // (DOWN_BATCH * pr)
    flip = flip_of(me[0], dims)
    low = flip & (DOWN_BATCH - 1)
    first = (r ^ lax.div(flip, DOWN_BATCH)) * DOWN_BATCH

    def put(dst):
        g = tn(act[...], dbr[...])
        for u in range(DOWN_BATCH):
            for i in range(parts):
                at = (u * parts + i) * pr
                dst[u ^ low, :, i * width : (i + 1) * width] = g[at : at + pr]
            at = pl.multiple_of((first + u) * pr, 16)
            dst[u ^ low, :, parts * width :] = gwp[pl.ds(at, pr), :]

    pl.when(r < PIECES // 2 // DOWN_BATCH)(lambda: put(keep))
    pl.when(r >= PIECES // 2 // DOWN_BATCH)(lambda: put(send))


def down_grad(dims, me, act, dbr, gwp):
    rows, width = dbr.shape
    ff = act.shape[1]
    cols = ff + gwp.shape[1]
    half = PIECES // 2 // DOWN_BATCH
    buf = struct((PIECES // 2, width // PIECES, cols), f32)
    block = (DOWN_BATCH, width // PIECES, cols)
    return pl.pallas_call(
        functools.partial(down_grad_kernel, dims),
        grid_spec=pltpu.PrefetchScalarGridSpec(
            num_scalar_prefetch=1,
            grid=(PIECES // DOWN_BATCH,),
            in_specs=[
                pl.BlockSpec(
                    (rows, DOWN_BATCH * ff // PIECES),
                    lambda r, f: (0, r ^ lax.div(flip_of(f[0], dims), DOWN_BATCH)),
                ),
                held(dbr.shape),
                held(gwp.shape),
            ],
            out_specs=[
                pl.BlockSpec(block, lambda r, f: (jnp.minimum(r, half - 1), 0, 0)),
                pl.BlockSpec(block, lambda r, f: (jnp.maximum(r - half, 0), 0, 0)),
            ],
        ),
        out_shape=[buf, buf],
        compiler_params=params(24),
        cost_estimate=cost(5e9, 17e6),
        name="down_gradient",
    )(me, in_hbm(act), dbr, gwp)


UP_CHUNK = 512


def up_grad_kernel(dims, me, dbr, slp, wd, ht, keep, send, din, dsum):
    pr = keep.shape[1]
    half = PIECES // 2
    rows = dbr.shape[0]
    tile = 256
    dsum[...] = jnp.zeros_like(dsum)
    for r0 in range(0, rows, tile):
        r = slice(r0, r0 + tile)
        d_inner = (nt(dbr[r, :], wd[...]) * slp[r, :].astype(f32)).astype(bf16)
        din[r, :] = d_inner
        dsum[...] += jnp.sum(d_inner.astype(f32), axis=0, keepdims=True)
    for dst, side, low in sides(me, dims, keep, send):
        at = pl.multiple_of(side * (half * pr), half * pr)
        g = nn(ht[pl.ds(at, half * pr), :], din[...])
        for t in range(half):
            dst[t ^ low] = g[t * pr : (t + 1) * pr]


def up_grad(dims, me, dbr, slp, wd, ht):
    rows, width = dbr.shape
    ff = slp.shape[1]
    half, pr = PIECES // 2, width // PIECES
    buf = struct((half, pr, ff), f32)
    part = pl.BlockSpec((half, pr, UP_CHUNK), lambda c: (0, 0, c))
    wide = pl.BlockSpec((rows, UP_CHUNK), lambda c: (0, c))
    return pl.pallas_call(
        functools.partial(up_grad_kernel, dims),
        grid=(ff // UP_CHUNK,),
        in_specs=[
            SMEM,
            held(dbr.shape),
            wide,
            pl.BlockSpec((UP_CHUNK, width), lambda c: (c, 0)),
            held(ht.shape),
        ],
        out_specs=[part, part, wide, pl.BlockSpec((1, UP_CHUNK), lambda c: (0, c))],
        out_shape=[buf, buf, pltpu.HBM((rows, ff), bf16), struct((1, ff), f32)],
        compiler_params=params(28),
        cost_estimate=cost(10e9, 30e6),
        name="up_gradient",
    )(me, dbr, in_hbm(slp), in_hbm(wd), ht)


def mid_back_kernel(me, din, wu, dr2, n1, i1, g1, wo, dr1, dpr, dat, sums, acc):
    c = pl.program_id(0)
    rows, width = dr1.shape
    span = dr2.shape[1]

    @pl.when(c == 0)
    def _():
        acc[...] = nt(din[...], wu[...])

    @pl.when(c > 0)
    def _():
        acc[...] += nt(din[...], wu[...])

    at = pl.ds(pl.multiple_of(c * span, span), span)
    acc[:, at] += dr2[...]

    @pl.when(c == pl.num_programs(0) - 1)
    def _():
        sums[...] = jnp.zeros_like(sums)
        tile = 256
        for r0 in range(0, rows, tile):
            r = slice(r0, r0 + tile)
            d = acc[r, :]
            normal = n1[r, :].astype(f32)
            sums[0:1, :] += jnp.sum(d * normal, axis=0, keepdims=True)
            sums[1:2, :] += jnp.sum(d, axis=0, keepdims=True)
            dr = norm_back(d, row(g1), normal, i1[r, :])
            dr1[r, :] = dr
            low = dr.astype(bf16)
            dpr[r, :] = low
            sums[2:3, :] += jnp.sum(low.astype(f32), axis=0, keepdims=True)
            dat[r, :] = nt(low, wo[...]).astype(bf16)


def mid_back(me, din, wu, dr2, n1, i1, g1, wo):
    rows, width = dr2.shape
    ff = din.shape[1]
    steps = ff // FF_CHUNK
    ins = [me, in_hbm(din), in_hbm(wu), dr2, n1, i1, g1, wo]
    specs = [held(x.shape) for x in ins]
    specs[0] = SMEM
    specs[1] = pl.BlockSpec((rows, FF_CHUNK), lambda c: (0, c))
    specs[2] = pl.BlockSpec((width, FF_CHUNK), lambda c: (0, c))
    specs[3] = pl.BlockSpec((rows, width // steps), lambda c: (0, c))
    outs = [
        struct((rows, width), f32),
        struct((rows, width), bf16),
        struct((rows, width), bf16),
        struct((8, width), f32),
    ]
    return pl.pallas_call(
        mid_back_kernel,
        grid=(steps,),
        in_specs=specs,
        out_specs=[whole(x.shape) for x in outs],
        out_shape=outs,
        scratch_shapes=[pltpu.VMEM((rows, width), f32)],
        compiler_params=params(32),
        cost_estimate=cost(9e9, 15e6),
        name="middle_backward",
    )(*ins)


def qkv_grad_kernel(dims, has_out, me, tok, d0, d1, d2, *rest):
    keep, send = rest[-2:]
    pairs = [(tok, d0), (tok, d1), (tok, d2)]
    if has_out:
        pairs.append(rest[:2])
    half = PIECES // 2
    pr = keep.shape[1]
    for dst, side, low in sides(me, dims, keep, send):
        at = pl.ds(pl.multiple_of(side * (half * pr), half * pr), half * pr)
        col = 0
        for left, d in pairs:
            g = tn(left[:, at], d[...])
            cols = d.shape[1]
            for t in range(half):
                dst[t ^ low, :, col : col + cols] = g[t * pr : (t + 1) * pr]
            col += cols


def qkv_grad(dims, me, tok, ds, outer):
    rows, width = tok.shape
    ins = [me, tok, *ds, *outer]
    cols = sum(d.shape[1] for d in ds) + (width if outer else 0)
    buf = struct((PIECES // 2, width // PIECES, cols), f32)
    return pl.pallas_call(
        functools.partial(qkv_grad_kernel, dims, bool(outer)),
        in_specs=[SMEM] + [VMEM] * (len(ins) - 1),
        out_specs=[VMEM] * 2,
        out_shape=[buf, buf],
        compiler_params=params(10),
        cost_estimate=cost(4e9, 8e6),
        name="qkv_gradient",
    )(*ins)


def input_grad_kernel(count, me, *refs):
    ds = refs[:count]
    w, dr1, out = refs[count:]
    tile = 256
    for r0 in range(0, out.shape[0], tile):
        r = slice(r0, r0 + tile)
        acc = dr1[r, :]
        for j, d in enumerate(ds):
            acc = acc + nt(d[r, :], w[:, j * 256 : (j + 1) * 256])
        out[r, :] = acc


def input_grad(me, ds, w, dr1):
    return pl.pallas_call(
        functools.partial(input_grad_kernel, len(ds)),
        in_specs=[SMEM] + [VMEM] * (len(ds) + 2),
        out_specs=VMEM,
        out_shape=struct(dr1.shape, f32),
        compiler_params=params(10),
        cost_estimate=cost(5e9, 15e6),
        name="input_gradient",
    )(me, *ds, w, dr1)


def collect_kernel(s0, s1, s2, dsum, sm1, sm2, out):
    width = out.shape[1]
    for j, s in enumerate((s0, s1, s2)):
        out[0:2, j * 256 : (j + 1) * 256] = s[0:2, :]
    out[2:3, :] = sm1[2:3, :]
    out[3:5, :] = sm1[0:2, :]
    end = 5
    for j in range(dsum.shape[1] // width):
        out[end : end + 1, :] = dsum[:, j * width : (j + 1) * width]
        end += 1
    out[end : end + 1, :] = sm2[2:3, :]
    out[end + 1 : end + 3, :] = sm2[0:2, :]
    out[end + 3 :, :] = jnp.zeros((out.shape[0] - end - 3, width), f32)


def collect(s, dsum, sm1, sm2):
    ins = [*s, dsum, sm1, sm2]
    return pl.pallas_call(
        collect_kernel,
        in_specs=[VMEM] * len(ins),
        out_specs=VMEM,
        out_shape=struct((16, sm1.shape[1]), f32),
        compiler_params=params(6),
        cost_estimate=cost(1e4, 1e5),
        name="collect_vectors",
    )(*ins)


def swap(x, mask, n):
    return lax.ppermute(x, "dp", [(i, i ^ mask) for i in range(n)])


def after(x, *others):
    return lax.optimization_barrier((x,) + others)[0]


def join(x, y):
    which = lax.broadcasted_iota(i32, (2,) + x.shape, 0)
    both = jnp.where(which == 0, x[None], y[None])
    return both.reshape((2 * x.shape[0],) + x.shape[1:])


class Chain:
    def __init__(self, keep, send, dims, n):
        self.keep, self.ready, self.dims, self.n = keep, send, dims, n
        self.at = 0
        self.steps = len(dims) + 4
        self.out = None
        self.recv = None

    def start(self):
        k, dims = self.at, self.dims
        d = dims[k] if k < len(dims) else dims[3 - (k - len(dims))]
        self.recv = swap(self.ready, d, self.n)

    def land(self, *others):
        if self.recv is None:
            self.start()
        k, dims = self.at, self.dims
        self.at += 1
        recv = after(self.recv, *others) if others else self.recv
        self.recv = None
        if k < 4:
            recv = recv.astype(f32)
            half = self.keep.shape[0] // 2
            if k < 3:
                self.ready = (self.keep[half:] + recv[half:]).astype(bf16)
                self.keep = self.keep[:half] + recv[:half]
            else:
                self.ready = (self.keep + recv).astype(bf16)
        elif k < len(dims):
            self.ready = (self.ready.astype(f32) + recv.astype(f32)).astype(bf16)
        elif k == len(dims) + 3:
            self.out = (self.ready, recv)
        else:
            self.ready = join(self.ready, recv)

    def finish(self):
        while self.out is None:
            self.land()
        return self.out


class Total:
    def __init__(self, x, n):
        self.ready, self.n, self.at, self.recv, self.out = x, n, 0, None, None

    def start(self):
        self.recv = swap(self.ready, 1 << self.at, self.n)

    def land(self, *others):
        if self.recv is None:
            self.start()
        self.ready = self.ready + (after(self.recv, *others) if others else self.recv)
        self.recv = None
        self.at += 1
        if 1 << self.at == self.n:
            self.out = self.ready

    def finish(self):
        while self.out is None:
            self.land()
        return self.out


def gather_all(x, n):
    for b in reversed(range(n.bit_length() - 1)):
        x = join(x, swap(x, 1 << b, n))
    return x


def place_kernel(chains, layout, count, me, *refs):
    bufs, outs = refs[: len(chains)], refs[-count:]
    half = PIECES // 2
    for i, dims in enumerate(chains):
        low = flip_of(me[0], dims) & (half - 1)
        pr = bufs[i].shape[1]
        for t in range(half):
            for which, col, cols, row0, out, out_col, out_rows in layout:
                if which == i:
                    at = t * out_rows + row0
                    outs[out][at : at + pr, out_col : out_col + cols] = bufs[i][
                        t ^ low, :, col : col + cols
                    ].astype(f32)


def put_in_place(chains, me, layout, shapes, previous, name):
    bufs = [c.ready if previous is None else c.out[1] for c in chains]
    ins = [me, *bufs]
    specs = [pl.BlockSpec(x.shape, lambda a, f: (0, 0, 0)) for x in bufs]
    aliases = {}
    if previous is not None:
        for i, g in enumerate(previous):
            aliases[len(ins)] = i
            ins.append(g)
            specs.append(pl.BlockSpec(memory_space=pl.ANY))
    dims = chains[0].dims

    def spot(a, f):
        own = lax.div(flip_of(f[0], dims), PIECES // 2)
        return (own if previous is None else 1 - own, 0)

    return pl.pallas_call(
        functools.partial(place_kernel, [c.dims for c in chains], layout, len(shapes)),
        grid_spec=pltpu.PrefetchScalarGridSpec(
            num_scalar_prefetch=1,
            grid=(1,),
            in_specs=specs,
            out_specs=[pl.BlockSpec((r // 2, w), spot) for r, w in shapes],
        ),
        out_shape=[struct(x, f32) for x in shapes],
        input_output_aliases=aliases,
        compiler_params=params(28),
        cost_estimate=cost(0, 0),
        name=name,
    )(*ins)


SCHEDULE = (
    "+D", "up", "+U", "-D", "+D", "mid", "-U", "+U", "E0", "-D", "+D", "q0", "+Q0", "E1", "-U",
    "+U", "-D", "+D", "-Q0", "+Q0", "q1", "+Q1", "E2", "-U", "+U", "-D", "+D", "-Q1", "+Q1", "q2",
    "+Q2", "-Q0", "+Q0", "vec", "+V", "-U", "+U", "-Q2", "+Q2", "-Q1", "+Q1", "-V", "+V", "in",
    "-D", "+D", "-Q0", "+Q0", "-Q2", "+Q2", "-Q1", "+Q1", "-V", "+V", "-Q0", "+Q0", "-U", "+U",
    "-Q2", "+Q2", "-V", "+V", "-D", "+D", "-Q1", "+Q1", "-U", "+U", "-Q0", "+Q0", "-Q2", "+Q2",
    "-V", "+V", "-Q1", "+Q1", "-D", "-Q2", "+Q2", "-Q0", "+Q0", "-V", "-U", "-Q1", "+Q1", "-Q2",
    "+Q2", "~U", "+U", "-Q0", "+Q0", "-Q1", "+Q1", "-Q2", "+Q2", "~D", "+D", "-Q0", "+Q0", "-Q1",
    "+Q1", "-U", "+U", "<U", "-Q2", "+Q2", "-D", "+D", "<D", "<Q", "-U", "=U", "-Q0", "-Q1", "-Q2",
    "=Q", "-D", "=D",
)


def axis_orders(n):
    rest = [1 << i for i in range(1, n.bit_length() - 1)]
    if n == 32:
        x, y, z, far = rest
        return {
            "D": (1, x, y, z, far),
            "U": (1, z, x, y, far),
            "Q0": (1, y, x, z, far),
            "Q1": (1, y, x, z, far),
            "Q2": (1, y, x, z, far),
        }
    names = ("D", "U", "Q0", "Q1", "Q2")
    return {name: tuple([1] + rest[i:] + rest[:i]) for i, name in enumerate(names)}


def body(
    tokens, seg_lengths, owner, place, w_qkv, b_qv, w_out, b_out, ln1_gain, ln1_bias,
    w_up, b_up, w_down, b_down, ln2_gain, ln2_bias, w_proj,
):
    rows, width = tokens.shape
    ff = w_up.shape[1]
    n = lax.axis_size("dp")
    me = lax.axis_index("dp").astype(i32).reshape(1)
    orders = axis_orders(n)

    packed, attended, lse, hid, low, ht, n1, i1 = attention(
        seg_lengths, tokens, w_qkv, b_qv, w_out, b_out, ln1_gain, ln1_bias
    )
    act, slp, n2, i2, nl, emb, ul, query = ffn_fwd(
        seg_lengths, hid, low, w_up, b_up, w_down, b_down, ln2_gain, ln2_bias, w_proj
    )

    msg, dpb = loss_forward(me, seg_lengths, owner, gather_all(query, n), ul)
    loss, dr2, dbr, gwp, sums2 = loss_back(
        me, seg_lengths, owner, place, gather_all(msg, n), dpb, emb, nl, n2, i2, ln2_gain, w_proj
    )

    chains = {"D": Chain(*down_grad(orders["D"], me, act, dbr, gwp), orders["D"], n)}
    flying = {}
    parts = []
    placed = {}
    small = None
    last = None

    def vectors(v):
        end = 5 + ff // width
        return [v[0:2].reshape(-1), v[5:end].reshape(-1)] + [
            v[i] for i in (2, 3, 4, end, end + 1, end + 2)
        ]

    def now(x):
        return after(x, *flying.values()) if flying else x

    members = {"Q": ["Q0", "Q1", "Q2"]}
    begun = {}

    def layout_of(name):
        if name == "D":
            layout = [(0, i * width, width, i * width // PIECES, 0, 0, ff // PIECES) for i in range(ff // width)]
            layout.append((0, ff, w_proj.shape[1], 0, 1, 0, width // PIECES))
            return layout, [(ff, width), w_proj.shape], "down_place"
        if name == "U":
            return [(0, 0, ff, 0, 0, 0, width // PIECES)], [(width, ff)], "up_place"
        span = width // PORTIONS
        layout = [
            (c, i * span, span, 0, 0, i * width + c * span, width // PIECES)
            for c in range(PORTIONS)
            for i in range(3)
        ]
        layout.append((0, width, width, 0, 1, 0, width // PIECES))
        return layout, [(width, 3 * width), (width, width)], "qkv_place"

    def begin(name):
        layout, shapes, title = layout_of(name)
        own = [chains[q] for q in members.get(name, [name])]
        for c in own:
            while c.at < c.steps - 1:
                c.land()
        begun[name] = put_in_place(own, me, layout, shapes, None, title)
        return begun[name][0]

    def finish(name):
        if name not in begun:
            begin(name)
        layout, shapes, title = layout_of(name)
        own = [chains[q] for q in members.get(name, [name])]
        for c in own:
            c.finish()
        placed[name] = put_in_place(own, me, layout, shapes, begun[name], title)
        return placed[name][0]

    for event in SCHEDULE:
        if event[0] == "+":
            name = event[1:]
            if chains[name].out is None:
                chains[name].start()
                flying[name] = chains[name].ready
        elif event[0] == "-":
            name = event[1:]
            if chains[name].out is None:
                chains[name].land(*(last if isinstance(last, list) else [last] if last is not None else []))
                flying.pop(name, None)
                last = chains[name].ready
                if name == "V" and chains[name].out is not None:
                    small = vectors(chains[name].out)
                    last = small
        elif event[0] == "~":
            c = chains[event[1:]]
            c.ready = after(c.ready, *(last if isinstance(last, list) else [last]))
        elif event[0] == "<":
            last = begin(event[1:])
        elif event[0] == "=":
            last = finish(event[1:])
        elif event == "up":
            keep, send, din, dsum = up_grad(orders["U"], now(me), dbr, slp, w_down, ht)
            chains["U"] = Chain(keep, send, orders["U"], n)
            last = dsum
        elif event == "mid":
            dr1, dpr, dat, sums1 = mid_back(now(me), din, w_up, dr2, n1, i1, ln1_gain, w_out)
            last = sums1
        elif event[0] == "E":
            j = int(event[1])
            parts.append(attention_back(j, now(seg_lengths), packed, dat, attended, lse))
            last = parts[j][3]
        elif event[0] == "q":
            j = int(event[1])
            outer = [attended, dpr] if j == 0 else []
            name = "Q%d" % j
            keep, send = qkv_grad(orders[name], now(me), tokens, parts[j][:3], outer)
            chains[name] = Chain(keep, send, orders[name], n)
            last = send
        elif event == "vec":
            chains["V"] = Total(collect([x[3] for x in parts], dsum, sums1, sums2), n)
        elif event == "in":
            ds = [x[i] for i in range(3) for x in parts]
            d_tokens = input_grad(now(me), ds, w_qkv, dr1)
            last = d_tokens
    if small is None:
        small = vectors(chains["V"].finish())
    g_w_down, g_w_proj = placed["D"]
    g_w_up = placed["U"][0]
    g_w_qkv, g_w_out = placed["Q"]
    g_b_qv, g_b_up, g_b_out, g_ln1_gain, g_ln1_bias, g_b_down, g_ln2_gain, g_ln2_bias = small
    return (
        loss[0, 0:1], d_tokens, g_w_qkv, g_b_qv, g_w_out, g_b_out, g_ln1_gain, g_ln1_bias,
        g_w_up, g_b_up, g_w_down, g_b_down, g_ln2_gain, g_ln2_bias, g_w_proj,
    )


def solution(mesh):
    whole_rows = P("dp", None)
    return jax.shard_map(
        body,
        mesh=mesh,
        in_specs=(whole_rows, whole_rows) + (P(),) * 15,
        out_specs=(P("dp"), whole_rows) + (P(),) * 13,
        check_vma=False,
    )
```
